256 devices in a mesh: seq: 32 (over x, z), head: 8 (over y, core).
Axes of the slice: x: 4, y: 4, z: 8, core: 2. Of those that a mesh axis runs over, the one named last changes fastest.
Arguments:
- queries: bfloat16 [32, 768, 8192], P('seq', None, 'head'), may hold values from -20 to 20
- keys: bfloat16 [32, 768, 8192], P('seq', None, 'head'), may hold values from -2.5 to 2.5
- values: bfloat16 [32, 768, 8192], P('seq', None, 'head'), may hold values from -64 to 64
- log_decay: float32 [32, 768, 64], P('seq', None, 'head'), may hold values from -1 to 0
- gain: float32 [8192], P('head'), may hold values from 0.25 to 1.75
- parents: int32 [32], replicated, may hold values from 15 to 31, as said below
- d_out: bfloat16 [32, 768, 8192], P('seq', None, 'head'), may hold values from -6 to 6
Outputs:
- out: bfloat16 [32, 768, 8192], P('seq', None, 'head')
- d_queries: bfloat16 [32, 768, 8192], P('seq', None, 'head')
- d_keys: bfloat16 [32, 768, 8192], P('seq', None, 'head')
- d_values: bfloat16 [32, 768, 8192], P('seq', None, 'head')
The draws below stay inside these ranges and needn't reach their ends.
Inputs may be any that keep to these rules, and one draw needn't show every extreme that they name: `parents`: every entry is the last index of some prompt, k * 16 + 15.
All inputs are finite; a program needn't handle non-finite values.
Results may differ from the reference program's by a relative error of at most 0.024.
Values may be sent and summed in bfloat16 or wider, within the bound.
No kernel may reach another device: no remote copies, remote signals or barrier semaphores. Data moves between devices by JAX's collectives and lax.ppermute only.
A program may use at most 192 MiB of HBM per device.

```python
import math
import jax
import jax.numpy as jnp
from jax import lax

H = 64
HD = 128
BLK = 256
PROMPTS = 2
P_DEV = 512
RLEN = 256
ROWS = 768
PSPAN = 16
N_SEQ = 32


def draw_queries(key, part):
    key = jax.random.fold_in(key, 11)
    first_key, second_key = jax.random.split(key)
    shape = (N_SEQ, P_DEV + RLEN, H * HD)
    base = jnp.clip(jax.random.normal(first_key, shape, jnp.float32), -4.0, 4.0)
    scales = jnp.exp(jax.random.uniform(second_key, (N_SEQ, P_DEV + RLEN, 1), jnp.float32, 0.0, math.log(10.0)))
    return (0.3 * base * scales).astype(jnp.bfloat16)


def draw_values(key, part):
    key = jax.random.fold_in(key, 12)
    first_key, second_key = jax.random.split(key)
    shape = (N_SEQ, P_DEV + RLEN, H, HD)
    rising = jnp.exp(jnp.arange(H, dtype=jnp.float32) * (math.log(3.0) / max(H - 1, 1)))
    base = jnp.clip(jax.random.normal(first_key, shape, jnp.float32), -4.0, 4.0)
    spread = jnp.exp(jax.random.uniform(second_key, (H,), jnp.float32, 0.0, math.log(3.3)))
    heads_scale = (rising * spread)[None, None, :, None]
    return (base * heads_scale).reshape(N_SEQ, P_DEV + RLEN, H * HD).astype(jnp.bfloat16)


def draw_log_decay(key, part):
    key = jax.random.fold_in(key, 13)
    keys_list = jax.random.split(key, 7)
    chain = PSPAN * P_DEV
    slow_share = 0.5
    slow = jax.random.uniform(keys_list[0], (H,), jnp.float32) < slow_share
    slow_rate = jnp.exp(jax.random.uniform(keys_list[1], (H,), jnp.float32, math.log(0.05), math.log(0.2))) / chain
    fast_rate = jnp.exp(jax.random.uniform(keys_list[2], (H,), jnp.float32, math.log(1.0 / 50.0), math.log(1.0 / 30.0)))
    rates = jnp.where(slow, slow_rate, fast_rate)
    shard_factor = jnp.exp(jax.random.uniform(keys_list[3], (N_SEQ, 1, 1), jnp.float32, math.log(0.5), math.log(2.0)))
    rough = jax.random.uniform(keys_list[4], (N_SEQ, P_DEV + RLEN, H), jnp.float32, 0.5, 1.5)
    stable_fraction = -rates[None, None, :] * shard_factor * rough
    location_shifts = jax.random.randint(keys_list[5], (2,), 0, N_SEQ * P_DEV)
    retained_items = jax.random.uniform(keys_list[6], (2,), jnp.float32, 0.55, 0.8)
    partition_labels = jnp.arange(N_SEQ, dtype=jnp.int32)[:, None]
    row_ids = jnp.arange(P_DEV + RLEN, dtype=jnp.int32)[None, :]
    linear_lines = jnp.where(row_ids < P_DEV, partition_labels * P_DEV + row_ids, -1)
    tile_clusters = jnp.sum(jnp.where(linear_lines[:, :, None] == location_shifts[None, None, :], jnp.log(retained_items)[None, None, :], 0.0), axis=-1)
    return (stable_fraction + tile_clusters[:, :, None]).astype(jnp.float32)


def draw_parents(key, part):
    key = jax.random.fold_in(key, 14)
    picked = jax.random.randint(key, (N_SEQ,), 0, PROMPTS).astype(jnp.int32)
    picked = picked.at[0].set(0).at[N_SEQ - 1].set(PROMPTS - 1)
    return (picked * PSPAN + PSPAN - 1).astype(jnp.int32)


def block_levels(stream_key, dims, cuts, smallest, high):
    def one(dim, parts):
        steps = jax.random.uniform(jax.random.fold_in(jax.random.fold_in(stream_key, 6), dim), (parts,), jnp.float32, smallest / len(cuts), high / len(cuts))
        return jnp.repeat(jnp.exp(steps), dims[dim] // parts).reshape((-1,) + (1,) * (len(dims) - dim - 1))

    level = one(*cuts[0])
    for cut in cuts[1:]:
        level = level * one(*cut)
    return level


def scatter_about(key, shape, width, reach, cuts=(), kind=jnp.bfloat16):
    factor_of = block_levels(key, shape, cuts, -0.22, 0.18) if cuts else 1.0
    result = jax.random.normal(key, shape, jnp.float32) * width * factor_of
    return jnp.minimum(jnp.maximum(result, -reach), reach).astype(kind)


def setup_inputs(seed: int = 0) -> dict:
    arg_keys = jax.random.split(jax.random.key(seed), 8)
    queries = draw_queries(jax.random.fold_in(arg_keys[7], 71), 0)
    keys = scatter_about(arg_keys[1], (N_SEQ, ROWS, H * HD), 0.3, 2.5, ((0, 32), (2, 8)))
    values = draw_values(jax.random.fold_in(arg_keys[7], 71), 0)
    log_decay = draw_log_decay(jax.random.fold_in(arg_keys[7], 71), 0)
    gain = jnp.clip(1.0 + 0.15 * jax.random.normal(arg_keys[4], (H * HD,), jnp.float32), 0.25, 1.75)
    parents = draw_parents(jax.random.fold_in(arg_keys[7], 71), 0)
    d_out = scatter_about(arg_keys[6], (N_SEQ, ROWS, H * HD), 1.0, 6.0, ((0, 32), (2, 8)))
    return {"queries": queries, "keys": keys, "values": values, "log_decay": log_decay, "gain": gain, "parents": parents, "d_out": d_out}


epsilon = 1e-05

def rounded(value):
    return lax.optimization_barrier(value.astype(jnp.bfloat16)).astype(jnp.float32)

def block_masks(decay_block):
    cumulative = jnp.cumsum(decay_block, axis=0)
    block_end = cumulative[-1]
    transposed = cumulative.T
    log_gaps = transposed[:, :, None] - transposed[:, None, :]
    extent = decay_block.shape[0]
    row_ids = lax.broadcasted_iota(jnp.int32, (extent, extent), 0)
    col_ids = lax.broadcasted_iota(jnp.int32, (extent, extent), 1)
    causal = (row_ids >= col_ids)[None]
    decay_mask = jnp.where(causal, jnp.exp(jnp.where(causal, log_gaps, 0.0)), 0.0)
    return (cumulative, block_end, decay_mask)

def block_forward_pass(query_block, key_block, value_block, decay_block, running):
    query_f = query_block.astype(jnp.float32)
    key_f = key_block.astype(jnp.float32)
    value_f = value_block.astype(jnp.float32)
    cumulative, block_end, decay_mask = block_masks(decay_block)
    scores = jnp.einsum('thd,uhd->htu', query_f, key_f)
    weights = rounded(scores * decay_mask)
    within = jnp.einsum('htu,uhe->the', weights, value_f)
    query_scaled = rounded(query_f * jnp.exp(cumulative)[:, :, None])
    across = jnp.einsum('thd,hde->the', query_scaled, rounded(running))
    key_scaled = rounded(key_f * jnp.exp(block_end[None, :] - cumulative)[:, :, None])
    following = jnp.exp(block_end)[:, None, None] * running + jnp.einsum('uhd,uhe->hde', key_scaled, value_f)
    return (within + across, following)

def backward_block(query_block, key_block, value_block, decay_block, running, grad_out, end_grad):
    query_f = query_block.astype(jnp.float32)
    key_f = key_block.astype(jnp.float32)
    value_f = value_block.astype(jnp.float32)
    cumulative, block_end, decay_mask = block_masks(decay_block)
    scores = jnp.einsum('thd,uhd->htu', query_f, key_f)
    weights = rounded(scores * decay_mask)
    query_scaled = rounded(query_f * jnp.exp(cumulative)[:, :, None])
    decay_per_key = jnp.exp(block_end[None, :] - cumulative)[:, :, None]
    key_scaled = rounded(key_f * decay_per_key)
    start_round = rounded(running)
    end_round = rounded(end_grad)
    weight_grad = jnp.einsum('the,uhe->htu', grad_out, value_f)
    score_grad = rounded(weight_grad * decay_mask)
    grad_values = jnp.einsum('htu,the->uhe', weights, grad_out) + jnp.einsum('uhd,hde->uhe', key_scaled, end_round)
    grad_queries = jnp.einsum('htu,uhd->thd', score_grad, key_f) + jnp.exp(cumulative)[:, :, None] * jnp.einsum('the,hde->thd', grad_out, start_round)
    grad_keys = jnp.einsum('htu,thd->uhd', score_grad, query_f) + decay_per_key * jnp.einsum('uhe,hde->uhd', value_f, end_round)
    start_grad = jnp.exp(block_end)[:, None, None] * end_grad + jnp.einsum('thd,the->hde', query_scaled, grad_out)
    return (grad_queries, grad_keys, grad_values, start_grad)

def reference(queries, keys, values, log_decay, gain, parents, d_out):
    prompt_count = P_DEV // BLK
    reply_count = RLEN // BLK

    def prompt_view(array, last):
        return array[:, :P_DEV].reshape((N_SEQ * prompt_count, BLK, H) + last)

    def reply_view(array, last):
        return array[:, P_DEV:].reshape((N_SEQ, reply_count, BLK, H) + last)
    prompt_in = (prompt_view(queries, (HD,)), prompt_view(keys, (HD,)), prompt_view(values, (HD,)), prompt_view(log_decay, ()))
    reply_in = (reply_view(queries, (HD,)), reply_view(keys, (HD,)), reply_view(values, (HD,)), reply_view(log_decay, ()))
    zero_state = jnp.zeros((H, HD, HD), jnp.float32)
    block_ids = jnp.arange(N_SEQ * prompt_count, dtype=jnp.int32)

    def prompt_step(running, pieces):
        block_id = pieces[4]
        first = jnp.logical_and(block_id % prompt_count == 0, block_id // prompt_count % PSPAN == 0)
        running = jnp.where(first, 0.0, running)
        attended, following = block_forward_pass(pieces[0], pieces[1], pieces[2], pieces[3], running)
        return (following, (attended, running, following))
    _, (prompt_attended, prompt_starts, followings) = lax.scan(prompt_step, zero_state, prompt_in + (block_ids,))
    ends = followings[prompt_count - 1::prompt_count]
    reply_begin = rounded(ends)[parents]

    def reply_forward(pieces):

        def reply_step(running, inner):
            attended, following = block_forward_pass(inner[0], inner[1], inner[2], inner[3], running)
            return (following, (attended, running))
        _, (attended, starts) = lax.scan(reply_step, pieces[4], pieces[:4])
        return (attended, starts)
    reply_attended, reply_starts = lax.map(reply_forward, reply_in + (reply_begin,))
    attended = jnp.concatenate([prompt_attended.reshape(N_SEQ, P_DEV, H * HD), reply_attended.reshape(N_SEQ, RLEN, H * HD)], axis=1)
    inverse = lax.rsqrt(lax.optimization_barrier(jnp.sum(attended * attended, axis=-1, keepdims=True)) / (H * HD) + epsilon)
    out = (attended * inverse * gain).astype(jnp.bfloat16)
    weighted = gain * d_out.astype(jnp.float32)
    products = lax.optimization_barrier(jnp.sum(weighted * attended, axis=-1, keepdims=True))
    grad_attended = rounded(inverse * weighted - attended * inverse * inverse * inverse * products / (H * HD))
    prompt_grad = grad_attended[:, :P_DEV].reshape(N_SEQ * prompt_count, BLK, H, HD)
    reply_grad = grad_attended[:, P_DEV:].reshape(N_SEQ, reply_count, BLK, H, HD)

    def reply_backward(pieces):

        def reply_step(end_grad, inner):
            grad_q, grad_k, derivative_wrt_vals, start_grad = backward_block(inner[0], inner[1], inner[2], inner[3], inner[4], inner[5], end_grad)
            return (start_grad, (grad_q, grad_k, derivative_wrt_vals))
        first_grad, gradients = lax.scan(reply_step, zero_state, pieces, reverse=True)
        return (first_grad, gradients)
    reply_first, reply_grads = lax.map(reply_backward, reply_in + (reply_starts, reply_grad))
    subtree_limb = jax.ops.segment_sum(rounded(reply_first), parents, num_segments=N_SEQ)

    def prompt_back(end_grad, pieces):
        block_id = pieces[6]
        closing = block_id % prompt_count == prompt_count - 1
        cut = jnp.logical_and(closing, block_id // prompt_count % PSPAN == PSPAN - 1)
        added = lax.dynamic_index_in_dim(subtree_limb, block_id // prompt_count, 0, keepdims=False)
        end_grad = jnp.where(cut, 0.0, end_grad) + jnp.where(closing, added, 0.0)
        grad_q, grad_k, derivative_wrt_vals, start_grad = backward_block(pieces[0], pieces[1], pieces[2], pieces[3], pieces[4], pieces[5], end_grad)
        return (start_grad, (grad_q, grad_k, derivative_wrt_vals))
    _, prompt_grads = lax.scan(prompt_back, zero_state, prompt_in + (prompt_starts, prompt_grad, block_ids), reverse=True)
    results = [out]
    for number in range(3):
        joined = jnp.concatenate([prompt_grads[number].reshape(N_SEQ, P_DEV, H * HD), reply_grads[number].reshape(N_SEQ, RLEN, H * HD)], axis=1)
        results.append(joined.astype(jnp.bfloat16))
    return (results[0], results[1], results[2], results[3])
```

```python
import jax
import jax.numpy as jnp
from jax import lax
from jax.experimental import pallas as pl
from jax.experimental.pallas import tpu as pltpu
from jax.sharding import PartitionSpec as P

H = 64
HD = 128
BLK = 256
PROMPTS = 2
P_DEV = 512
ROWS = 768
HL = 8
N_SEQ = 32
SPAN = N_SEQ // PROMPTS
COLS = HL * HD
PIECE = HL * HD // N_SEQ
EPS = 1e-05

F32 = jnp.float32
BF16 = jnp.bfloat16


def params(mib=32):
    return pltpu.CompilerParams(
        dimension_semantics=("arbitrary",), vmem_limit_bytes=mib * 1024 * 1024
    )


def dot(a, b, dims):
    return lax.dot_general(a, b, (dims, ((), ())), preferred_element_type=F32)


def mm(a, b):
    return dot(a, b, ((1,), (0,)))


def mm_nt(a, b):
    return dot(a, b, ((1,), (1,)))


def mm_tn(a, b):
    return dot(a, b, ((0,), (0,)))


def rows(number):
    return slice(number * BLK, (number + 1) * BLK)


def column(cum_ref, number, head):
    block = pltpu.roll(cum_ref[rows(number), :], lax.rem(HD - head, HD), 1)
    return block[:, 0:1]


def rounded_product(block, factor):
    return (block.astype(F32) * factor).astype(BF16)


def summary_kernel(decay_ref, keys_ref, values_ref, send_ref, term_ref, cum_ref, cum_rows_ref):
    head = pl.program_id(0)

    @pl.when(head == 0)
    def _():
        cum_ref[...] = jnp.zeros_like(cum_ref)
        for number in range(ROWS // BLK):
            total = decay_ref[0, rows(number), :]
            row_ids = lax.broadcasted_iota(jnp.int32, total.shape, 0)
            shift = 1
            while shift < BLK:
                moved = pltpu.roll(total, shift, 0)
                total = total + jnp.where(row_ids >= shift, moved, 0.0)
                shift *= 2
            cum_ref[rows(number), 0:HL] = total
        for tile in range(ROWS // HD):
            part = slice(tile * HD, (tile + 1) * HD)
            turned = cum_ref[part, :].T
            for each in range(HL):
                cum_rows_ref[each, :, part] = turned[each : each + 1, :]

    terms = []
    ends = []
    for number in range(2):
        col = column(cum_ref, number, head)
        end = col[BLK - 1 : BLK, :]
        key_scaled = rounded_product(keys_ref[0, rows(number), :], jnp.exp(end - col))
        terms.append(mm_tn(key_scaled, values_ref[0, rows(number), :]))
        ends.append(end)
    term_ref[0] = terms[0]
    summary = jnp.exp(ends[1]) * terms[0] + terms[1]
    send_ref[:, 0:PIECE, :] = summary.astype(BF16).reshape(HD // PIECE, PIECE, HD)
    decay = jnp.broadcast_to(jnp.exp(ends[0] + ends[1]), (16, HD))
    coarse = decay.astype(BF16)
    fine = (decay - coarse.astype(F32)).astype(BF16)
    row_ids = lax.broadcasted_iota(jnp.int32, (16, HD), 0)
    packed = jnp.where(
        row_ids == 0, coarse.astype(F32), jnp.where(row_ids == 1, fine.astype(F32), 0.0)
    ).astype(BF16)
    for piece in range(HD // PIECE):
        send_ref[piece, PIECE : PIECE + 16, :] = packed


def within_kernel(cum_ref, cum_rows_ref, queries_ref, keys_ref, values_ref, within_ref):
    head = pl.program_id(0)
    row_ids = lax.broadcasted_iota(jnp.int32, (BLK, BLK), 0)
    col_ids = lax.broadcasted_iota(jnp.int32, (BLK, BLK), 1)
    for number in range(ROWS // BLK):
        col = column(cum_ref, number, head)
        gaps = col - cum_rows_ref[0, :, rows(number)]
        mask = jnp.where(row_ids >= col_ids, jnp.exp(gaps), 0.0)
        scores = mm_nt(queries_ref[0, rows(number), :], keys_ref[0, rows(number), :])
        weights = (scores * mask).astype(BF16)
        within_ref[rows(number), :] = mm(weights, values_ref[0, rows(number), :])


def forward_scan_kernel(parents_ref, got_ref, send_ref, decay_ref):
    totals = []
    for prompt in range(PROMPTS):
        carry = jnp.zeros((PIECE, HD), F32)
        for index in range(prompt * SPAN, (prompt + 1) * SPAN):
            packed = got_ref[index, PIECE : PIECE + 16, :].astype(F32)
            decay = packed[0:1, :] + packed[1:2, :]
            decay_ref[index : index + 1, :] = decay
            send_ref[index, 0:PIECE, :] = carry.astype(BF16)
            carry = decay * carry + got_ref[index, 0:PIECE, :].astype(F32)
        totals.append(carry)
    for index in range(N_SEQ):
        prompt = parents_ref[index] // SPAN
        chosen = jnp.where(prompt == 0, totals[0], totals[1])
        send_ref[index, PIECE : 2 * PIECE, :] = chosen.astype(BF16)


def attend_kernel(
    cum_ref, queries_ref, d_out_ref, gain_ref, within_ref, starts_ref, term_ref,
    attended_ref, second_ref, stats_ref, squares_ref, products_ref,
):
    head = pl.program_id(0)

    @pl.when(head == 0)
    def _():
        squares_ref[...] = jnp.zeros_like(squares_ref)
        products_ref[...] = jnp.zeros_like(products_ref)

    first = starts_ref[:, 0:PIECE, :].reshape(HD, HD)
    reply = starts_ref[:, PIECE : 2 * PIECE, :].reshape(HD, HD)
    end = column(cum_ref, 0, head)[BLK - 1 : BLK, :]
    second = (jnp.exp(end) * first.astype(F32) + term_ref[0]).astype(BF16)
    second_ref[0] = second
    for number, start in enumerate((first, second, reply)):
        col = column(cum_ref, number, head)
        query_scaled = rounded_product(queries_ref[0, rows(number), :], jnp.exp(col))
        attended = within_ref[rows(number), :] + mm(query_scaled, start)
        attended_ref[rows(number), :] = attended
        weighted = gain_ref[...] * d_out_ref[0, rows(number), :].astype(F32)
        squares_ref[rows(number), :] += attended * attended
        products_ref[rows(number), :] += weighted * attended

    @pl.when(head == HL - 1)
    def _():
        stats_ref[...] = jnp.zeros_like(stats_ref)
        for tile in range(ROWS // HD):
            part = slice(tile * HD, (tile + 1) * HD)
            for base, sums_ref in ((0, squares_ref), (8, products_ref)):
                row = jnp.sum(sums_ref[part, :].T, axis=0, keepdims=True)
                stats_ref[:, base + tile : base + tile + 1, :] = jnp.broadcast_to(
                    row[None], (HL, 1, HD)
                )


def row_factors(stats_ref, inverse_ref, slope_ref):
    total = stats_ref[0]
    for source in range(1, HL):
        total = total + stats_ref[source]
    turned = jnp.concatenate([total, jnp.zeros((HD - 16, HD), F32)], axis=0).T
    for tile in range(ROWS // HD):
        part = slice(tile * HD, (tile + 1) * HD)
        squares = jnp.broadcast_to(turned[:, tile : tile + 1], (HD, HD))
        products = jnp.broadcast_to(turned[:, 8 + tile : 9 + tile], (HD, HD))
        inverse = lax.rsqrt(squares / (H * HD) + EPS)
        inverse_ref[part, :] = inverse
        if slope_ref is not None:
            slope_ref[part, :] = inverse * inverse * inverse * products / (H * HD)


def grad_kernel(
    cum_ref, queries_ref, d_out_ref, gain_ref, attended_ref, stats_ref,
    grad_ref, send_ref, term_ref, inverse_out_ref, inverse_ref, slope_ref,
):
    head = pl.program_id(0)

    @pl.when(head == 0)
    def _():
        row_factors(stats_ref, inverse_ref, slope_ref)
        inverse_out_ref[...] = inverse_ref[...]

    terms = []
    for number in range(ROWS // BLK):
        weighted = gain_ref[...] * d_out_ref[0, rows(number), :].astype(F32)
        grad = (
            inverse_ref[rows(number), :] * weighted
            - attended_ref[rows(number), :] * slope_ref[rows(number), :]
        ).astype(BF16)
        grad_ref[rows(number), :] = grad
        col = column(cum_ref, number, head)
        query_scaled = rounded_product(queries_ref[0, rows(number), :], jnp.exp(col))
        terms.append(mm_tn(query_scaled, grad))
    end = column(cum_ref, 0, head)[BLK - 1 : BLK, :]
    local_sum = jnp.exp(end) * terms[1] + terms[0]
    term_ref[0] = terms[1]
    send_ref[:, 0:PIECE, :] = local_sum.astype(BF16).reshape(HD // PIECE, PIECE, HD)
    send_ref[:, PIECE : 2 * PIECE, :] = terms[2].astype(BF16).reshape(HD // PIECE, PIECE, HD)


def backward_scan_kernel(parents_ref, got_ref, decay_ref, send_ref):
    branches = [jnp.zeros((PIECE, HD), F32) for _ in range(PROMPTS)]
    for index in range(N_SEQ):
        prompt = parents_ref[index] // SPAN
        start_grad = got_ref[index, PIECE : 2 * PIECE, :].astype(F32)
        for each in range(PROMPTS):
            branches[each] = branches[each] + jnp.where(prompt == each, start_grad, 0.0)
    for prompt in range(PROMPTS):
        carry = branches[prompt]
        for index in reversed(range(prompt * SPAN, (prompt + 1) * SPAN)):
            send_ref[index] = carry.astype(BF16)
            carry = decay_ref[index : index + 1, :] * carry + got_ref[index, 0:PIECE, :].astype(F32)


def local_grads_kernel(
    cum_ref, cum_rows_ref, queries_ref, keys_ref, values_ref, grad_ref, attended_ref, gain_ref,
    inverse_ref, starts_ref, second_ref,
    out_ref, d_queries_ref, d_keys_ref, d_values_ref, part_keys_ref, part_values_ref,
):
    head = pl.program_id(0)
    row_ids = lax.broadcasted_iota(jnp.int32, (BLK, BLK), 0)
    col_ids = lax.broadcasted_iota(jnp.int32, (BLK, BLK), 1)
    first = starts_ref[:, 0:PIECE, :].reshape(HD, HD)
    reply = starts_ref[:, PIECE : 2 * PIECE, :].reshape(HD, HD)
    for number, start in enumerate((first, second_ref[0], reply)):
        part = rows(number)
        queries = queries_ref[0, part, :]
        keys = keys_ref[0, part, :]
        values = values_ref[0, part, :]
        grad = grad_ref[part, :]
        col = column(cum_ref, number, head)
        gaps = cum_rows_ref[0, :, part] - col
        mask = jnp.where(col_ids >= row_ids, jnp.exp(gaps), 0.0)
        weights = (mm_nt(keys, queries) * mask).astype(BF16)
        score_grad = (mm_nt(values, grad) * mask).astype(BF16)
        grad_values = mm(weights, grad)
        grad_keys = mm(score_grad, queries)
        grad_queries = mm_tn(score_grad, keys) + jnp.exp(col) * mm_nt(grad, start)
        d_queries_ref[0, part, :] = grad_queries.astype(BF16)
        out_ref[0, part, :] = (
            attended_ref[part, :] * inverse_ref[part, :] * gain_ref[...]
        ).astype(BF16)
        if number < 2:
            part_keys_ref[part, :] = grad_keys
            part_values_ref[part, :] = grad_values
        else:
            d_keys_ref[0] = grad_keys.astype(BF16)
            d_values_ref[0] = grad_values.astype(BF16)


def far_grads_kernel(
    cum_ref, keys_ref, values_ref, ends_ref, term_ref, part_keys_ref, part_values_ref, _k, _v,
    d_keys_ref, d_values_ref,
):
    head = pl.program_id(0)
    cols = [column(cum_ref, number, head) for number in range(2)]
    ends = [col[BLK - 1 : BLK, :] for col in cols]
    second = ends_ref[...].reshape(HD, HD)
    first = (jnp.exp(ends[1]) * second.astype(F32) + term_ref[0]).astype(BF16)
    for number, end_grad in enumerate((first, second)):
        part = rows(number)
        factor = jnp.exp(ends[number] - cols[number])
        key_scaled = rounded_product(keys_ref[0, part, :], factor)
        grad_values = part_values_ref[part, :] + mm(key_scaled, end_grad)
        grad_keys = part_keys_ref[part, :] + factor * mm_nt(values_ref[0, part, :], end_grad)
        d_values_ref[0, part, :] = grad_values.astype(BF16)
        d_keys_ref[0, part, :] = grad_keys.astype(BF16)


def shape(dims, kind):
    return jax.ShapeDtypeStruct(dims, kind)


def whole(dims):
    return pl.BlockSpec(dims, lambda h: (0,) * len(dims))


def lead(dims):
    return pl.BlockSpec(dims, lambda h: (h,) + (0,) * (len(dims) - 1))


def cost(flops, moved):
    return pl.CostEstimate(flops=int(flops), bytes_accessed=int(moved), transcendentals=0)


FULL = pl.BlockSpec((1, ROWS, HD), lambda h: (0, 0, h))
PROMPT = pl.BlockSpec((1, P_DEV, HD), lambda h: (0, 0, h))
REPLY = pl.BlockSpec((1, BLK, HD), lambda h: (0, 2, h))
FLAT = pl.BlockSpec((ROWS, HD), lambda h: (0, h))
FLAT_PROMPT = pl.BlockSpec((P_DEV, HD), lambda h: (0, h))
LANES = pl.BlockSpec((1, HD), lambda h: (0, h))
CUM = whole((ROWS, HD))
CUM_ROWS = lead((1, 1, ROWS))
STATE = lead((1, HD, HD))
PARTS = HD // PIECE
SMEM = pl.BlockSpec(memory_space=pltpu.SMEM)
VMEM = pl.BlockSpec(memory_space=pltpu.VMEM)


def local(queries, keys, values, log_decay, gain, parents, d_out):
    gain_row = gain.reshape(1, COLS)
    mega = 1 << 20

    send, first_term, cum, cum_rows = pl.pallas_call(
        summary_kernel,
        grid=(HL,),
        in_specs=[whole((1, ROWS, HL)), PROMPT, PROMPT],
        out_specs=[lead((PARTS, PIECE + 16, HD)), STATE, CUM, whole((HL, 1, ROWS))],
        out_shape=[
            shape((N_SEQ, PIECE + 16, HD), BF16),
            shape((HL, HD, HD), F32),
            shape((ROWS, HD), F32),
            shape((HL, 1, ROWS), F32),
        ],
        compiler_params=params(),
        cost_estimate=cost(3e8, 4 * mega),
        name="summary",
    )(log_decay, keys, values)
    got = lax.all_to_all(send, "seq", 0, 0, tiled=True)

    within = pl.pallas_call(
        within_kernel,
        grid=(HL,),
        in_specs=[CUM, CUM_ROWS, FULL, FULL, FULL],
        out_specs=FLAT,
        out_shape=shape((ROWS, COLS), F32),
        compiler_params=params(),
        cost_estimate=cost(4e9, 16 * mega),
        name="within",
    )(cum, cum_rows, queries, keys, values)

    send, decays = pl.pallas_call(
        forward_scan_kernel,
        in_specs=[SMEM, VMEM],
        out_specs=[VMEM, VMEM],
        out_shape=[shape((N_SEQ, 2 * PIECE, HD), BF16), shape((N_SEQ, HD), F32)],
        compiler_params=pltpu.CompilerParams(vmem_limit_bytes=32 * mega),
        cost_estimate=cost(1e6, mega),
        name="forward_scan",
    )(parents, got)
    starts = lax.all_to_all(send, "seq", 0, 0, tiled=True)

    attended, second_start, stats = pl.pallas_call(
        attend_kernel,
        grid=(HL,),
        in_specs=[CUM, FULL, FULL, LANES, FLAT, lead((PARTS, 2 * PIECE, HD)), STATE],
        out_specs=[FLAT, STATE, whole((HL, 16, HD))],
        out_shape=[
            shape((ROWS, COLS), F32),
            shape((HL, HD, HD), BF16),
            shape((HL, 16, HD), F32),
        ],
        scratch_shapes=[pltpu.VMEM((ROWS, HD), F32), pltpu.VMEM((ROWS, HD), F32)],
        compiler_params=params(),
        cost_estimate=cost(3e8, 10 * mega),
        name="attend",
    )(cum, queries, d_out, gain_row, within, starts, first_term)
    stats = lax.all_to_all(stats, "head", 0, 0, tiled=True)

    grad, send, last_term, inverse = pl.pallas_call(
        grad_kernel,
        grid=(HL,),
        in_specs=[CUM, FULL, FULL, LANES, FLAT, whole((HL, 16, HD))],
        out_specs=[FLAT, lead((PARTS, 2 * PIECE, HD)), STATE, CUM],
        out_shape=[
            shape((ROWS, COLS), BF16),
            shape((N_SEQ, 2 * PIECE, HD), BF16),
            shape((HL, HD, HD), F32),
            shape((ROWS, HD), F32),
        ],
        scratch_shapes=[pltpu.VMEM((ROWS, HD), F32), pltpu.VMEM((ROWS, HD), F32)],
        compiler_params=params(),
        cost_estimate=cost(3e8, 10 * mega),
        name="grad",
    )(cum, queries, d_out, gain_row, attended, stats)
    got = lax.all_to_all(send, "seq", 0, 0, tiled=True)

    out, d_queries, d_keys, d_values, part_keys, part_values = pl.pallas_call(
        local_grads_kernel,
        grid=(HL,),
        in_specs=[
            CUM, CUM_ROWS, FULL, FULL, FULL, FLAT, FLAT, LANES, CUM,
            lead((PARTS, 2 * PIECE, HD)), STATE,
        ],
        out_specs=[FULL, FULL, REPLY, REPLY, FLAT_PROMPT, FLAT_PROMPT],
        out_shape=[shape((1, ROWS, COLS), BF16)] * 4 + [shape((P_DEV, COLS), F32)] * 2,
        compiler_params=params(),
        cost_estimate=cost(6e9, 24 * mega),
        name="local_grads",
    )(
        cum, cum_rows, queries, keys, values, grad, attended, gain_row, inverse, starts,
        second_start,
    )

    send = pl.pallas_call(
        backward_scan_kernel,
        in_specs=[SMEM, VMEM, VMEM],
        out_specs=VMEM,
        out_shape=shape((N_SEQ, PIECE, HD), BF16),
        compiler_params=pltpu.CompilerParams(vmem_limit_bytes=32 * mega),
        cost_estimate=cost(1e6, mega),
        name="backward_scan",
    )(parents, got, decays)
    ends = lax.all_to_all(send, "seq", 0, 0, tiled=True)

    anywhere = pl.BlockSpec(memory_space=pl.ANY)
    d_keys, d_values = pl.pallas_call(
        far_grads_kernel,
        grid=(HL,),
        in_specs=[
            CUM, PROMPT, PROMPT, lead((PARTS, PIECE, HD)), STATE, FLAT_PROMPT, FLAT_PROMPT,
            anywhere, anywhere,
        ],
        out_specs=[PROMPT, PROMPT],
        out_shape=[shape((1, ROWS, COLS), BF16)] * 2,
        input_output_aliases={7: 0, 8: 1},
        compiler_params=params(),
        cost_estimate=cost(3e8, 10 * mega),
        name="far_grads",
    )(cum, keys, values, ends, last_term, part_keys, part_values, d_keys, d_values)
    return (out, d_queries, d_keys, d_values)


def solution(mesh):
    cut = P("seq", None, "head")
    return jax.shard_map(
        local,
        mesh=mesh,
        in_specs=(cut, cut, cut, cut, P("head"), P(), cut),
        out_specs=(cut, cut, cut, cut),
        check_vma=False,
    )
```

```python
import jax
import jax.numpy as jnp
from jax import lax
from jax.experimental import pallas as pl
from jax.experimental.pallas import tpu as pltpu
from jax.sharding import PartitionSpec as P

H = 64
HD = 128
BLK = 256
PROMPTS = 2
P_DEV = 512
ROWS = 768
HL = 8
N_SEQ = 32
SPAN = N_SEQ // PROMPTS
COLS = HL * HD
PIECE = HL * HD // N_SEQ
PARTS = HD // PIECE
BLOCKS = ROWS // BLK
TILES = ROWS // HD
EPS = 1e-05

F32 = jnp.float32
BF16 = jnp.bfloat16


def dot(a, b, dims):
    return lax.dot_general(a, b, (dims, ((), ())), preferred_element_type=F32)


def mm(a, b):
    return dot(a, b, ((1,), (0,)))


def mm_nt(a, b):
    return dot(a, b, ((1,), (1,)))


def mm_tn(a, b):
    return dot(a, b, ((0,), (0,)))


def rows(number):
    return slice(number * BLK, (number + 1) * BLK)


def tile_rows(tile):
    return slice(tile * HD, (tile + 1) * HD)


def column(cum_ref, number, head):
    block = pltpu.roll(cum_ref[rows(number), :], lax.rem(HD - head, HD), 1)
    return block[:, 0:1]


def rounded_product(block, factor):
    return (block.astype(F32) * factor).astype(BF16)


def lanes(head):
    return pl.ds(pl.multiple_of(head * HD, HD), HD)


def of_rows(ref, count=ROWS, first=0):
    if len(ref.shape) == 3:
        return lambda head: ref.at[0, pl.ds(first, count), lanes(head)]
    return lambda head: ref.at[pl.ds(first, count), lanes(head)]


def of_lead(ref, count=1):
    if count == 1:
        return lambda head: ref.at[head]
    return lambda head: ref.at[pl.ds(head * count, count)]


class Copies:
    def __init__(self, pairs, sems):
        self.pairs, self.sems = pairs, sems

    def each(self, head):
        return [
            pltpu.make_async_copy(src(head), dst(head), self.sems.at[number, head])
            for number, (src, dst) in enumerate(self.pairs)
        ]

    def start(self, head):
        for copy in self.each(head):
            copy.start()

    def wait(self, head):
        for copy in self.each(head):
            copy.wait()


def over_heads(fetch, body, leave=None):
    if fetch is not None:
        for head in range(HL):
            fetch.start(head)

    def step(head, carry):
        if fetch is not None:
            fetch.wait(head)
        body(head)
        if leave is not None:
            leave.start(head)
        return carry

    lax.fori_loop(0, HL, step, 0)
    if leave is not None:
        for head in range(HL):
            leave.wait(head)


def split(value):
    coarse = value.astype(BF16)
    rest = value - coarse.astype(F32)
    middle = rest.astype(BF16)
    return coarse, middle, (rest - middle.astype(F32)).astype(BF16)


def summary_kernel(
    decay_ref, keys_ref, values_ref,
    send_ref, term_ref, cum_rows_ref, ends_ref,
    keys_buf, values_buf, in_sems,
):
    fetch = Copies(
        [
            (of_rows(keys_ref, P_DEV), of_lead(keys_buf)),
            (of_rows(values_ref, P_DEV), of_lead(values_buf)),
        ],
        in_sems,
    )
    for head in range(HL):
        fetch.start(head)
    before = lax.broadcasted_iota(jnp.int32, (BLK, BLK), 0)
    after = lax.broadcasted_iota(jnp.int32, (BLK, BLK), 1)
    upper = jnp.where(before <= after, 1.0, 0.0).astype(BF16)
    stacked = jnp.concatenate(
        [decay_ref[0, :, rows(number)] for number in range(BLOCKS)], axis=0
    )
    coarse, middle, fine = (mm(part, upper) for part in split(stacked))
    cumulative = (fine + middle) + coarse
    for number in range(BLOCKS):
        total = cumulative[number * HL : (number + 1) * HL]
        cum_rows_ref[:, rows(number)] = total
        ends_ref[:, number, :] = jnp.broadcast_to(jnp.exp(total[:, BLK - 1 : BLK]), (HL, HD))
    row_ids = lax.broadcasted_iota(jnp.int32, (16, HD), 0)

    def body(head):
        terms = []
        for number in range(2):
            row = cum_rows_ref[pl.ds(head, 1), rows(number)]
            factor = jnp.exp(row[:, BLK - 1 : BLK] - row)
            turned = keys_buf[head, rows(number), :].T
            key_scaled = rounded_product(turned, factor)
            terms.append(mm(key_scaled, values_buf[head, rows(number), :]))
        term_ref[head] = terms[0]
        end_decays = ends_ref[head]
        summary = end_decays[1:2, :] * terms[0] + terms[1]
        decay = jnp.broadcast_to(end_decays[0:1, :] * end_decays[1:2, :], (16, HD))
        coarse, middle, _ = split(decay)
        packed = jnp.where(
            row_ids == 0, coarse.astype(F32), jnp.where(row_ids == 1, middle.astype(F32), 0.0)
        ).astype(BF16)
        for piece in range(PARTS):
            at = head * PARTS + piece
            send_ref[at, 0:PIECE, :] = summary[piece * PIECE : (piece + 1) * PIECE].astype(BF16)
            send_ref[at, PIECE : PIECE + 16, :] = packed

    def step(head, carry):
        fetch.wait(head)
        body(head)
        return carry

    lax.fori_loop(0, HL, step, 0)


def within_kernel(
    cum_rows_ref, queries_ref, keys_ref, values_ref, d_out_ref,
    cum_ref, within_ref, scaled_queries_ref, scaled_keys_ref, d_out_buf,
    queries_buf, keys_buf, values_buf, in_sems,
):
    fetch = Copies(
        [
            (of_rows(queries_ref), of_lead(queries_buf)),
            (of_rows(keys_ref), of_lead(keys_buf)),
            (of_rows(values_ref), of_lead(values_buf)),
            (of_rows(d_out_ref), of_lead(d_out_buf)),
        ],
        in_sems,
    )
    for head in range(HL):
        fetch.start(head)
    for tile in range(TILES):
        part = tile_rows(tile)
        padded = jnp.concatenate(
            [cum_rows_ref[:, part], jnp.zeros((HD - HL, HD), F32)], axis=0
        )
        cum_ref[part, :] = padded.T
    row_ids = lax.broadcasted_iota(jnp.int32, (BLK, BLK), 0)
    col_ids = lax.broadcasted_iota(jnp.int32, (BLK, BLK), 1)

    def body(head):
        for number in range(BLOCKS):
            part = rows(number)
            queries = queries_buf[head, part, :]
            keys = keys_buf[head, part, :]
            col = column(cum_ref, number, head)
            gaps = col - cum_rows_ref[pl.ds(head, 1), part]
            mask = jnp.where(row_ids >= col_ids, jnp.exp(gaps), 0.0)
            weights = (mm_nt(queries, keys) * mask).astype(BF16)
            within_ref[head, part, :] = mm(weights, values_buf[head, part, :])
            scaled_queries_ref[head, part, :] = rounded_product(queries, jnp.exp(col))
            if number < 2:
                factor = jnp.exp(col[BLK - 1 : BLK, :] - col)
                scaled_keys_ref[head, part, :] = rounded_product(keys, factor)

    def step(head, carry):
        fetch.wait(head)
        body(head)
        return carry

    lax.fori_loop(0, HL, step, 0)


def forward_scan_kernel(parents_ref, got_ref, send_ref, decay_ref):
    totals = []
    for prompt in range(PROMPTS):
        carry = jnp.zeros((PIECE, HD), F32)
        for index in range(prompt * SPAN, (prompt + 1) * SPAN):
            packed = got_ref[index, PIECE : PIECE + 16, :].astype(F32)
            decay = packed[0:1, :] + packed[1:2, :]
            decay_ref[index : index + 1, :] = decay
            send_ref[index, 0:PIECE, :] = carry.astype(BF16)
            carry = decay * carry + got_ref[index, 0:PIECE, :].astype(F32)
        totals.append(carry)
    for index in range(N_SEQ):
        prompt = parents_ref[index] // SPAN
        chosen = jnp.where(prompt == 0, totals[0], totals[1])
        send_ref[index, PIECE : 2 * PIECE, :] = chosen.astype(BF16)


def attend_kernel(
    ends_ref, gain_ref, queries_ref, d_out_ref, within_ref, starts_ref, term_ref,
    attended_ref, second_ref, stats_ref, squares_ref, products_ref,
):
    squares_ref[...] = jnp.zeros_like(squares_ref)
    products_ref[...] = jnp.zeros_like(products_ref)

    def body(head):
        got = starts_ref[pl.ds(head * PARTS, PARTS)]
        first = got[:, 0:PIECE, :].reshape(HD, HD)
        reply = got[:, PIECE : 2 * PIECE, :].reshape(HD, HD)
        end_decay = ends_ref[head][0:1, :]
        second = (end_decay * first.astype(F32) + term_ref[head]).astype(BF16)
        second_ref[head] = second
        gain = gain_ref[pl.ds(head, 1), :]
        for number, start in enumerate((first, second, reply)):
            part = rows(number)
            attended = within_ref[head, part, :] + mm(queries_ref[head, part, :], start)
            attended_ref[head, part, :] = attended
            weighted = gain * d_out_ref[head, part, :].astype(F32)
            squares_ref[part, :] += attended * attended
            products_ref[part, :] += weighted * attended

    over_heads(None, body)
    stats_ref[...] = jnp.zeros_like(stats_ref)
    for tile in range(TILES):
        for base, sums_ref in ((0, squares_ref), (8, products_ref)):
            row = jnp.sum(sums_ref[tile_rows(tile), :].T, axis=0, keepdims=True)
            stats_ref[:, base + tile : base + tile + 1, :] = jnp.broadcast_to(
                row[None], (HL, 1, HD)
            )


def grad_kernel(
    ends_ref, gain_ref, stats_ref, queries_ref, d_out_ref, attended_ref,
    grad_ref, send_ref, term_ref, inverse_ref, slope_ref,
):
    total = stats_ref[0]
    for source in range(1, HL):
        total = total + stats_ref[source]
    turned = jnp.concatenate([total, jnp.zeros((HD - 16, HD), F32)], axis=0).T
    for tile in range(TILES):
        squares = turned[:, tile : tile + 1]
        products = turned[:, 8 + tile : 9 + tile]
        inverse = lax.rsqrt(squares / (H * HD) + EPS)
        slope = inverse * inverse * inverse * products / (H * HD)
        inverse_ref[tile_rows(tile), :] = jnp.broadcast_to(inverse, (HD, HD))
        slope_ref[tile_rows(tile), :] = jnp.broadcast_to(slope, (HD, HD))

    def body(head):
        gain = gain_ref[pl.ds(head, 1), :]
        terms = []
        for number in range(BLOCKS):
            part = rows(number)
            weighted = gain * d_out_ref[head, part, :].astype(F32)
            grad = (
                inverse_ref[part, :] * weighted
                - attended_ref[head, part, :] * slope_ref[part, :]
            ).astype(BF16)
            grad_ref[head, part, :] = grad
            terms.append(mm_tn(queries_ref[head, part, :], grad))
        local_sum = ends_ref[head][0:1, :] * terms[1] + terms[0]
        term_ref[head] = terms[1]
        for piece in range(PARTS):
            at = head * PARTS + piece
            part = slice(piece * PIECE, (piece + 1) * PIECE)
            send_ref[at, 0:PIECE, :] = local_sum[part].astype(BF16)
            send_ref[at, PIECE : 2 * PIECE, :] = terms[2][part].astype(BF16)

    over_heads(None, body)


def backward_scan_kernel(parents_ref, got_ref, decay_ref, send_ref):
    branches = [jnp.zeros((PIECE, HD), F32) for _ in range(PROMPTS)]
    for index in range(N_SEQ):
        prompt = parents_ref[index] // SPAN
        start_grad = got_ref[index, PIECE : 2 * PIECE, :].astype(F32)
        for each in range(PROMPTS):
            branches[each] = branches[each] + jnp.where(prompt == each, start_grad, 0.0)
    for prompt in range(PROMPTS):
        carry = branches[prompt]
        for index in reversed(range(prompt * SPAN, (prompt + 1) * SPAN)):
            send_ref[index] = carry.astype(BF16)
            carry = decay_ref[index : index + 1, :] * carry + got_ref[index, 0:PIECE, :].astype(F32)


def local_grads_kernel(
    cum_ref, cum_rows_ref, inverse_ref, gain_ref,
    queries_ref, keys_ref, values_ref, grad_ref, attended_ref, starts_ref, second_ref,
    out_ref, d_queries_ref, part_keys_ref, part_values_ref, d_keys_ref, d_values_ref, values_buf,
    queries_buf, keys_buf, out_buf, d_queries_buf, d_keys_buf, d_values_buf, in_sems, out_sems,
):
    fetch = Copies(
        [
            (of_rows(queries_ref), of_lead(queries_buf)),
            (of_rows(keys_ref), of_lead(keys_buf)),
            (of_rows(values_ref), of_lead(values_buf)),
        ],
        in_sems,
    )
    leave = Copies(
        [
            (of_lead(out_buf), of_rows(out_ref)),
            (of_lead(d_queries_buf), of_rows(d_queries_ref)),
            (of_lead(d_keys_buf), of_rows(d_keys_ref, BLK, P_DEV)),
            (of_lead(d_values_buf), of_rows(d_values_ref, BLK, P_DEV)),
        ],
        out_sems,
    )
    row_ids = lax.broadcasted_iota(jnp.int32, (BLK, BLK), 0)
    col_ids = lax.broadcasted_iota(jnp.int32, (BLK, BLK), 1)

    def body(head):
        got = starts_ref[pl.ds(head * PARTS, PARTS)]
        first = got[:, 0:PIECE, :].reshape(HD, HD)
        reply = got[:, PIECE : 2 * PIECE, :].reshape(HD, HD)
        gain = gain_ref[pl.ds(head, 1), :]
        for number, start in enumerate((first, second_ref[head], reply)):
            part = rows(number)
            queries = queries_buf[head, part, :]
            keys = keys_buf[head, part, :]
            values = values_buf[head, part, :]
            grad = grad_ref[head, part, :]
            col = column(cum_ref, number, head)
            gaps = cum_rows_ref[pl.ds(head, 1), part] - col
            mask = jnp.where(col_ids >= row_ids, jnp.exp(gaps), 0.0)
            weights = (mm_nt(keys, queries) * mask).astype(BF16)
            score_grad = (mm_nt(values, grad) * mask).astype(BF16)
            grad_values = mm(weights, grad)
            grad_keys = mm(score_grad, queries)
            grad_queries = mm_tn(score_grad, keys) + jnp.exp(col) * mm_nt(grad, start)
            d_queries_buf[head, part, :] = grad_queries.astype(BF16)
            out_buf[head, part, :] = (
                attended_ref[head, part, :] * inverse_ref[part, :] * gain
            ).astype(BF16)
            if number < 2:
                part_keys_ref[head, part, :] = grad_keys
                part_values_ref[head, part, :] = grad_values
            else:
                d_keys_buf[head] = grad_keys.astype(BF16)
                d_values_buf[head] = grad_values.astype(BF16)

    over_heads(fetch, body, leave)


def far_grads_kernel(
    cum_ref, ends_ref, far_ref, term_ref, scaled_keys_ref, values_ref,
    part_keys_ref, part_values_ref, _k, _v,
    d_keys_ref, d_values_ref, d_keys_buf, d_values_buf, out_sems,
):
    leave = Copies(
        [
            (of_lead(d_keys_buf), of_rows(d_keys_ref, P_DEV)),
            (of_lead(d_values_buf), of_rows(d_values_ref, P_DEV)),
        ],
        out_sems,
    )

    def body(head):
        second = far_ref[pl.ds(head * PARTS, PARTS)].reshape(HD, HD)
        first = (ends_ref[head][1:2, :] * second.astype(F32) + term_ref[head]).astype(BF16)
        for number, end_grad in enumerate((first, second)):
            part = rows(number)
            col = column(cum_ref, number, head)
            factor = jnp.exp(col[BLK - 1 : BLK, :] - col)
            grad_values = part_values_ref[head, part, :] + mm(scaled_keys_ref[head, part, :], end_grad)
            grad_keys = part_keys_ref[head, part, :] + factor * mm_nt(
                values_ref[head, part, :], end_grad
            )
            d_values_buf[head, part, :] = grad_values.astype(BF16)
            d_keys_buf[head, part, :] = grad_keys.astype(BF16)

    over_heads(None, body, leave)


def shape(dims, kind):
    return jax.ShapeDtypeStruct(dims, kind)


HBM = pl.BlockSpec(memory_space=pltpu.HBM)
SMEM = pl.BlockSpec(memory_space=pltpu.SMEM)
VMEM = pl.BlockSpec(memory_space=pltpu.VMEM)
WIDE = shape((1, ROWS, COLS), BF16)
HEAD_ROWS = (HL, ROWS, HD)
HEAD_PROMPT = (HL, P_DEV, HD)
HEAD_REPLY = (HL, BLK, HD)
STATE = (HL, HD, HD)
PIECES = (N_SEQ, PIECE, HD)
TWO_PIECES = (N_SEQ, 2 * PIECE, HD)
SENT_PIECES = (N_SEQ, PIECE + 16, HD)
CUM = (ROWS, HD)


def call(kernel, name, in_specs, outs, scratch, semaphores, mib, flops, moved, aliases=None):
    return pl.pallas_call(
        kernel,
        in_specs=in_specs,
        out_specs=[spec for spec, _ in outs],
        out_shape=[made for _, made in outs],
        scratch_shapes=[pltpu.VMEM(dims, kind) for dims, kind in scratch]
        + [pltpu.SemaphoreType.DMA((count, HL)) for count in semaphores],
        input_output_aliases=aliases or {},
        compiler_params=pltpu.CompilerParams(vmem_limit_bytes=mib << 20),
        cost_estimate=pl.CostEstimate(
            flops=int(flops), bytes_accessed=int(moved) << 20, transcendentals=0
        ),
        name=name,
    )


def summarize(decay_rows, keys, values):
    return call(
        summary_kernel, "summary", [VMEM, HBM, HBM],
        [
            (VMEM, shape(SENT_PIECES, BF16)), (VMEM, shape(STATE, F32)),
            (VMEM, shape((HL, ROWS), F32)), (VMEM, shape((HL, 8, HD), F32)),
        ],
        [(HEAD_PROMPT, BF16), (HEAD_PROMPT, BF16)], [2], 52, 3e8, 4,
    )(decay_rows, keys, values)


def inside(cum_rows, queries, keys, values, d_out):
    return call(
        within_kernel, "within", [VMEM] + [HBM] * 4,
        [
            (VMEM, shape(CUM, F32)), (VMEM, shape(HEAD_ROWS, F32)), (VMEM, shape(HEAD_ROWS, BF16)),
            (VMEM, shape(HEAD_PROMPT, BF16)), (VMEM, shape(HEAD_ROWS, BF16)),
        ],
        [(HEAD_ROWS, BF16)] * 3, [4], 20, 4e9, 16,
    )(cum_rows, queries, keys, values, d_out)


def forward_scan(parents, got):
    return call(
        forward_scan_kernel, "forward_scan", [SMEM, VMEM],
        [(VMEM, shape(TWO_PIECES, BF16)), (VMEM, shape((N_SEQ, HD), F32))],
        [], [], 12, 1e6, 1,
    )(parents, got)


def attend(ends, gains, scaled_queries, d_out, within, starts, term):
    return call(
        attend_kernel, "attend", [VMEM] * 7,
        [
            (VMEM, shape(HEAD_ROWS, F32)), (VMEM, shape(STATE, BF16)),
            (VMEM, shape((HL, 16, HD), F32)),
        ],
        [(CUM, F32), (CUM, F32)], [], 20, 3e8, 10,
    )(ends, gains, scaled_queries, d_out, within, starts, term)


def grads(ends, gains, stats, scaled_queries, d_out, attended):
    return call(
        grad_kernel, "grad", [VMEM] * 6,
        [
            (VMEM, shape(HEAD_ROWS, BF16)), (VMEM, shape(TWO_PIECES, BF16)),
            (VMEM, shape(STATE, F32)), (VMEM, shape(CUM, F32)),
        ],
        [(CUM, F32)], [], 20, 3e8, 10,
    )(ends, gains, stats, scaled_queries, d_out, attended)


def local_grads(
    cum, cum_rows, inverse, gains, queries, keys, values, grad, attended, starts, second
):
    return call(
        local_grads_kernel, "local_grads", [VMEM] * 4 + [HBM] * 3 + [VMEM] * 4,
        [
            (HBM, WIDE), (HBM, WIDE), (VMEM, shape(HEAD_PROMPT, F32)),
            (VMEM, shape(HEAD_PROMPT, F32)), (HBM, WIDE), (HBM, WIDE),
            (VMEM, shape(HEAD_ROWS, BF16)),
        ],
        [(HEAD_ROWS, BF16)] * 4 + [(HEAD_REPLY, BF16)] * 2, [3, 4], 28, 6e9, 24,
    )(cum, cum_rows, inverse, gains, queries, keys, values, grad, attended, starts, second)


def far_grads(cum, ends, far, term, scaled_keys, values, part_keys, part_values, d_keys, d_values):
    return call(
        far_grads_kernel, "far_grads", [VMEM] * 8 + [HBM] * 2,
        [(HBM, WIDE), (HBM, WIDE)],
        [(HEAD_PROMPT, BF16), (HEAD_PROMPT, BF16)], [2], 20, 3e8, 10, {8: 0, 9: 1},
    )(cum, ends, far, term, scaled_keys, values, part_keys, part_values, d_keys, d_values)


def backward_scan(parents, got, decays):
    return call(
        backward_scan_kernel, "backward_scan", [SMEM, VMEM, VMEM],
        [(VMEM, shape(PIECES, BF16))], [], [], 12, 1e6, 1,
    )(parents, got, decays)[0]


def everyone(array, axis):
    return lax.all_to_all(array, axis, 0, 0, tiled=True)


def local(queries, keys, values, log_decay, gain, parents, d_out):
    gains = gain.reshape(HL, HD)
    decay_rows = jnp.swapaxes(log_decay, 1, 2)
    send, first_term, cum_rows, block_ends = summarize(decay_rows, keys, values)
    got = everyone(send, "seq")
    cum, within, scaled_queries, scaled_keys, d_out_heads = inside(
        cum_rows, queries, keys, values, d_out
    )
    send, decays = forward_scan(parents, got)
    starts = everyone(send, "seq")
    attended, second, stats = attend(
        block_ends, gains, scaled_queries, d_out_heads, within, starts, first_term
    )
    stats = everyone(stats, "head")
    grad, send, last_term, inverse = grads(
        block_ends, gains, stats, scaled_queries, d_out_heads, attended
    )
    got = everyone(send, "seq")
    out, d_queries, part_keys, part_values, d_keys, d_values, value_heads = local_grads(
        cum, cum_rows, inverse, gains, queries, keys, values, grad, attended, starts, second
    )
    far = everyone(backward_scan(parents, got, decays), "seq")
    d_keys, d_values = far_grads(
        cum, block_ends, far, last_term, scaled_keys, value_heads, part_keys, part_values,
        d_keys, d_values,
    )
    return (out, d_queries, d_keys, d_values)


def solution(mesh):
    cut = P("seq", None, "head")
    return jax.shard_map(
        local,
        mesh=mesh,
        in_specs=(cut, cut, cut, cut, P("head"), P(), cut),
        out_specs=(cut, cut, cut, cut),
        check_vma=False,
    )
```

```python
import jax
import jax.numpy as jnp
from jax import lax
from jax.experimental import pallas as pl
from jax.experimental.pallas import tpu as pltpu
from jax.sharding import PartitionSpec as P

H = 64
HD = 128
BLK = 256
PROMPTS = 2
P_DEV = 512
ROWS = 768
HL = 8
N_SEQ = 32
SPAN = N_SEQ // PROMPTS
COLS = HL * HD
PIECE = HL * HD // N_SEQ
PARTS = HD // PIECE
BLOCKS = ROWS // BLK
TILES = ROWS // HD
EPS = 1e-05

F32 = jnp.float32
BF16 = jnp.bfloat16


def dot(a, b, dims):
    return lax.dot_general(a, b, (dims, ((), ())), preferred_element_type=F32)


def mm(a, b):
    return dot(a, b, ((1,), (0,)))


def mm_nt(a, b):
    return dot(a, b, ((1,), (1,)))


def mm_tn(a, b):
    return dot(a, b, ((0,), (0,)))


def rows(number):
    return slice(number * BLK, (number + 1) * BLK)


def tile_rows(tile):
    return slice(tile * HD, (tile + 1) * HD)


def column(cum_ref, number, head):
    block = pltpu.roll(cum_ref[rows(number), :], lax.rem(HD - head, HD), 1)
    return block[:, 0:1]


def rounded_product(block, factor):
    return (block.astype(F32) * factor).astype(BF16)


def lanes(head):
    return pl.ds(pl.multiple_of(head * HD, HD), HD)


def of_rows(ref, count=ROWS, first=0):
    if len(ref.shape) == 3:
        return lambda head: ref.at[0, pl.ds(first, count), lanes(head)]
    return lambda head: ref.at[pl.ds(first, count), lanes(head)]


def of_lead(ref, count=1):
    if count == 1:
        return lambda head: ref.at[head]
    return lambda head: ref.at[pl.ds(head * count, count)]


class Copies:
    def __init__(self, pairs, sems):
        self.pairs, self.sems = pairs, sems

    def each(self, head):
        return [
            pltpu.make_async_copy(src(head), dst(head), self.sems.at[number, head])
            for number, (src, dst) in enumerate(self.pairs)
        ]

    def start(self, head):
        for copy in self.each(head):
            copy.start()

    def wait(self, head):
        for copy in self.each(head):
            copy.wait()


def over_heads(fetch, body, leave=None):
    if fetch is not None:
        for head in range(HL):
            fetch.start(head)

    def step(head, carry):
        if fetch is not None:
            fetch.wait(head)
        body(head)
        if leave is not None:
            leave.start(head)
        return carry

    lax.fori_loop(0, HL, step, 0)
    if leave is not None:
        for head in range(HL):
            leave.wait(head)


def split(value):
    coarse = value.astype(BF16)
    rest = value - coarse.astype(F32)
    middle = rest.astype(BF16)
    return coarse, middle, (rest - middle.astype(F32)).astype(BF16)


def summary_kernel(
    decay_ref, keys_ref, values_ref,
    send_ref, term_ref, cum_rows_ref, ends_ref,
    keys_buf, values_buf, in_sems,
):
    fetch = Copies(
        [
            (of_rows(keys_ref, P_DEV), of_lead(keys_buf)),
            (of_rows(values_ref, P_DEV), of_lead(values_buf)),
        ],
        in_sems,
    )
    for head in range(HL):
        fetch.start(head)
    before = lax.broadcasted_iota(jnp.int32, (BLK, BLK), 0)
    after = lax.broadcasted_iota(jnp.int32, (BLK, BLK), 1)
    upper = jnp.where(before <= after, 1.0, 0.0).astype(BF16)
    stacked = jnp.concatenate(
        [decay_ref[0, :, rows(number)] for number in range(BLOCKS)], axis=0
    )
    coarse, middle, fine = (mm(part, upper) for part in split(stacked))
    cumulative = (fine + middle) + coarse
    for number in range(BLOCKS):
        total = cumulative[number * HL : (number + 1) * HL]
        cum_rows_ref[:, rows(number)] = total
        ends_ref[:, number, :] = jnp.broadcast_to(jnp.exp(total[:, BLK - 1 : BLK]), (HL, HD))
    row_ids = lax.broadcasted_iota(jnp.int32, (16, HD), 0)

    def body(head):
        terms = []
        for number in range(2):
            row = cum_rows_ref[pl.ds(head, 1), rows(number)]
            factor = jnp.exp(row[:, BLK - 1 : BLK] - row)
            turned = keys_buf[head, rows(number), :].T
            key_scaled = rounded_product(turned, factor)
            terms.append(mm(key_scaled, values_buf[head, rows(number), :]))
        term_ref[head] = terms[0]
        end_decays = ends_ref[head]
        summary = end_decays[1:2, :] * terms[0] + terms[1]
        decay = jnp.broadcast_to(end_decays[0:1, :] * end_decays[1:2, :], (16, HD))
        coarse, middle, _ = split(decay)
        packed = jnp.where(
            row_ids == 0, coarse.astype(F32), jnp.where(row_ids == 1, middle.astype(F32), 0.0)
        ).astype(BF16)
        for piece in range(PARTS):
            at = head * PARTS + piece
            send_ref[at, 0:PIECE, :] = summary[piece * PIECE : (piece + 1) * PIECE].astype(BF16)
            send_ref[at, PIECE : PIECE + 16, :] = packed

    def step(head, carry):
        fetch.wait(head)
        body(head)
        return carry

    lax.fori_loop(0, HL, step, 0)


def within_kernel(
    cum_rows_ref, queries_ref, keys_ref, values_ref,
    cum_ref, within_ref, scaled_queries_ref, scaled_keys_ref, done_ref,
    queries_buf, keys_buf, values_buf, within_buf, scaled_queries_buf, scaled_keys_buf,
    in_sems, out_sems,
):
    fetch = Copies(
        [
            (of_rows(queries_ref), of_lead(queries_buf)),
            (of_rows(keys_ref), of_lead(keys_buf)),
            (of_rows(values_ref), of_lead(values_buf)),
        ],
        in_sems,
    )
    leave = Copies(
        [
            (of_lead(within_buf), of_lead(within_ref)),
            (of_lead(scaled_queries_buf), of_lead(scaled_queries_ref)),
            (of_lead(scaled_keys_buf), of_lead(scaled_keys_ref)),
        ],
        out_sems,
    )
    for head in range(HL):
        fetch.start(head)
    for tile in range(TILES):
        part = tile_rows(tile)
        padded = jnp.concatenate(
            [cum_rows_ref[:, part], jnp.zeros((HD - HL, HD), F32)], axis=0
        )
        cum_ref[part, :] = padded.T
    done_ref[...] = jnp.zeros_like(done_ref)
    row_ids = lax.broadcasted_iota(jnp.int32, (BLK, BLK), 0)
    col_ids = lax.broadcasted_iota(jnp.int32, (BLK, BLK), 1)

    def body(head):
        for number in range(BLOCKS):
            part = rows(number)
            queries = queries_buf[head, part, :]
            keys = keys_buf[head, part, :]
            col = column(cum_ref, number, head)
            gaps = col - cum_rows_ref[pl.ds(head, 1), part]
            mask = jnp.where(row_ids >= col_ids, jnp.exp(gaps), 0.0)
            weights = (mm_nt(queries, keys) * mask).astype(BF16)
            within_buf[head, part, :] = mm(weights, values_buf[head, part, :])
            scaled_queries_buf[head, part, :] = rounded_product(queries, jnp.exp(col))
            if number < 2:
                factor = jnp.exp(col[BLK - 1 : BLK, :] - col)
                scaled_keys_buf[head, part, :] = rounded_product(keys, factor)

    def step(head, carry):
        fetch.wait(head)
        body(head)
        leave.start(head)
        return carry

    lax.fori_loop(0, HL, step, 0)
    for head in range(HL):
        leave.wait(head)


def forward_scan_kernel(parents_ref, got_ref, _after, send_ref, decay_ref):
    totals = []
    for prompt in range(PROMPTS):
        carry = jnp.zeros((PIECE, HD), F32)
        for index in range(prompt * SPAN, (prompt + 1) * SPAN):
            packed = got_ref[index, PIECE : PIECE + 16, :].astype(F32)
            decay = packed[0:1, :] + packed[1:2, :]
            decay_ref[index : index + 1, :] = decay
            send_ref[index, 0:PIECE, :] = carry.astype(BF16)
            carry = decay * carry + got_ref[index, 0:PIECE, :].astype(F32)
        totals.append(carry)
    for index in range(N_SEQ):
        prompt = parents_ref[index] // SPAN
        chosen = jnp.where(prompt == 0, totals[0], totals[1])
        send_ref[index, PIECE : 2 * PIECE, :] = chosen.astype(BF16)


def attend_kernel(
    ends_ref, gain_ref, queries_ref, d_out_ref, within_ref, starts_ref, term_ref,
    attended_ref, second_ref, stats_ref, squares_ref, products_ref,
):
    squares_ref[...] = jnp.zeros_like(squares_ref)
    products_ref[...] = jnp.zeros_like(products_ref)

    def body(head):
        got = starts_ref[pl.ds(head * PARTS, PARTS)]
        first = got[:, 0:PIECE, :].reshape(HD, HD)
        reply = got[:, PIECE : 2 * PIECE, :].reshape(HD, HD)
        end_decay = ends_ref[head][0:1, :]
        second = (end_decay * first.astype(F32) + term_ref[head]).astype(BF16)
        second_ref[head] = second
        gain = gain_ref[pl.ds(head, 1), :]
        for number, start in enumerate((first, second, reply)):
            part = rows(number)
            attended = within_ref[head, part, :] + mm(queries_ref[head, part, :], start)
            attended_ref[head, part, :] = attended
            weighted = gain * d_out_ref[0, part, lanes(head)].astype(F32)
            squares_ref[part, :] += attended * attended
            products_ref[part, :] += weighted * attended

    over_heads(None, body)
    stats_ref[...] = jnp.zeros_like(stats_ref)
    for tile in range(TILES):
        for base, sums_ref in ((0, squares_ref), (8, products_ref)):
            row = jnp.sum(sums_ref[tile_rows(tile), :].T, axis=0, keepdims=True)
            stats_ref[:, base + tile : base + tile + 1, :] = jnp.broadcast_to(
                row[None], (HL, 1, HD)
            )


def row_factors(stats_ref, inverse_ref, slope_ref):
    total = stats_ref[0]
    for source in range(1, HL):
        total = total + stats_ref[source]
    turned = jnp.concatenate([total, jnp.zeros((HD - 16, HD), F32)], axis=0).T
    for tile in range(TILES):
        squares = turned[:, tile : tile + 1]
        products = turned[:, 8 + tile : 9 + tile]
        inverse = lax.rsqrt(squares / (H * HD) + EPS)
        slope = inverse * inverse * inverse * products / (H * HD)
        inverse_ref[tile_rows(tile), :] = jnp.broadcast_to(inverse, (HD, HD))
        slope_ref[tile_rows(tile), :] = jnp.broadcast_to(slope, (HD, HD))


def grad_kernel(
    ends_ref, gain_ref, stats_ref, queries_ref, d_out_ref, attended_ref,
    send_ref, inverse_ref, slope_ref,
):
    row_factors(stats_ref, inverse_ref, slope_ref)

    def body(head):
        gain = gain_ref[pl.ds(head, 1), :]
        terms = []
        for number in range(BLOCKS):
            part = rows(number)
            weighted = gain * d_out_ref[0, part, lanes(head)].astype(F32)
            grad = (
                inverse_ref[part, :] * weighted
                - attended_ref[head, part, :] * slope_ref[part, :]
            ).astype(BF16)
            terms.append(mm_tn(queries_ref[head, part, :], grad))
        local_sum = ends_ref[head][0:1, :] * terms[1] + terms[0]
        for piece in range(PARTS):
            at = head * PARTS + piece
            part = slice(piece * PIECE, (piece + 1) * PIECE)
            send_ref[at, 0:PIECE, :] = local_sum[part].astype(BF16)
            send_ref[at, PIECE : 2 * PIECE, :] = terms[2][part].astype(BF16)

    over_heads(None, body)


def backward_scan_kernel(parents_ref, got_ref, decay_ref, _after, send_ref):
    branches = [jnp.zeros((PIECE, HD), F32) for _ in range(PROMPTS)]
    for index in range(N_SEQ):
        prompt = parents_ref[index] // SPAN
        start_grad = got_ref[index, PIECE : 2 * PIECE, :].astype(F32)
        for each in range(PROMPTS):
            branches[each] = branches[each] + jnp.where(prompt == each, start_grad, 0.0)
    for prompt in range(PROMPTS):
        carry = branches[prompt]
        for index in reversed(range(prompt * SPAN, (prompt + 1) * SPAN)):
            send_ref[index] = carry.astype(BF16)
            carry = decay_ref[index : index + 1, :] * carry + got_ref[index, 0:PIECE, :].astype(F32)


def local_grads_kernel(
    cum_ref, cum_rows_ref, stats_ref, gain_ref,
    queries_ref, keys_ref, values_ref, d_out_ref, attended_ref, starts_ref, second_ref,
    out_ref, d_queries_ref, part_keys_ref, part_values_ref, d_keys_ref, d_values_ref, term_ref,
    done_ref, queries_buf, keys_buf, values_buf, d_out_buf, attended_buf, starts_buf, second_buf,
    out_buf, d_queries_buf, part_keys_buf, part_values_buf, d_keys_buf, d_values_buf, term_buf,
    inverse_ref, slope_ref, in_sems, out_sems,
):
    fetch = Copies(
        [
            (of_rows(d_out_ref), of_lead(d_out_buf)),
            (of_lead(attended_ref), of_lead(attended_buf)),
            (of_rows(queries_ref), of_lead(queries_buf)),
            (of_rows(keys_ref), of_lead(keys_buf)),
            (of_rows(values_ref), of_lead(values_buf)),
            (of_lead(starts_ref, PARTS), of_lead(starts_buf, PARTS)),
            (of_lead(second_ref), of_lead(second_buf)),
        ],
        in_sems,
    )
    leave = Copies(
        [
            (of_lead(out_buf), of_rows(out_ref)),
            (of_lead(d_queries_buf), of_rows(d_queries_ref)),
            (of_lead(part_keys_buf), of_lead(part_keys_ref)),
            (of_lead(part_values_buf), of_lead(part_values_ref)),
            (of_lead(d_keys_buf), of_rows(d_keys_ref, BLK, P_DEV)),
            (of_lead(d_values_buf), of_rows(d_values_ref, BLK, P_DEV)),
            (of_lead(term_buf), of_lead(term_ref)),
        ],
        out_sems,
    )
    for head in range(HL):
        fetch.start(head)
    done_ref[...] = jnp.zeros_like(done_ref)
    row_factors(stats_ref, inverse_ref, slope_ref)
    row_ids = lax.broadcasted_iota(jnp.int32, (BLK, BLK), 0)
    col_ids = lax.broadcasted_iota(jnp.int32, (BLK, BLK), 1)

    def body(head):
        got = starts_buf[pl.ds(head * PARTS, PARTS)]
        first = got[:, 0:PIECE, :].reshape(HD, HD)
        reply = got[:, PIECE : 2 * PIECE, :].reshape(HD, HD)
        gain = gain_ref[pl.ds(head, 1), :]
        for number, start in enumerate((first, second_buf[head], reply)):
            part = rows(number)
            queries = queries_buf[head, part, :]
            keys = keys_buf[head, part, :]
            values = values_buf[head, part, :]
            attended = attended_buf[head, part, :]
            inverse = inverse_ref[part, :]
            weighted = gain * d_out_buf[head, part, :].astype(F32)
            grad = (inverse * weighted - attended * slope_ref[part, :]).astype(BF16)
            out_buf[head, part, :] = (attended * inverse * gain).astype(BF16)
            col = column(cum_ref, number, head)
            gaps = cum_rows_ref[pl.ds(head, 1), part] - col
            mask = jnp.where(col_ids >= row_ids, jnp.exp(gaps), 0.0)
            weights = (mm_nt(keys, queries) * mask).astype(BF16)
            score_grad = (mm_nt(values, grad) * mask).astype(BF16)
            grad_values = mm(weights, grad)
            grad_keys = mm(score_grad, queries)
            growth = jnp.exp(col)
            grad_queries = mm_tn(score_grad, keys) + growth * mm_nt(grad, start)
            d_queries_buf[head, part, :] = grad_queries.astype(BF16)
            if number == 1:
                term_buf[head] = mm_tn(rounded_product(queries, growth), grad)
            if number < 2:
                part_keys_buf[head, part, :] = grad_keys
                part_values_buf[head, part, :] = grad_values
            else:
                d_keys_buf[head] = grad_keys.astype(BF16)
                d_values_buf[head] = grad_values.astype(BF16)

    def step(head, carry):
        fetch.wait(head)
        body(head)
        leave.start(head)
        return carry

    lax.fori_loop(0, HL, step, 0)
    for head in range(HL):
        leave.wait(head)


def far_grads_kernel(
    cum_ref, ends_ref, far_ref, term_ref, scaled_keys_ref, values_ref,
    part_keys_ref, part_values_ref, _k, _v,
    d_keys_ref, d_values_ref, d_keys_buf, d_values_buf, out_sems,
):
    leave = Copies(
        [
            (of_lead(d_keys_buf), of_rows(d_keys_ref, P_DEV)),
            (of_lead(d_values_buf), of_rows(d_values_ref, P_DEV)),
        ],
        out_sems,
    )

    def body(head):
        second = far_ref[pl.ds(head * PARTS, PARTS)].reshape(HD, HD)
        first = (ends_ref[head][1:2, :] * second.astype(F32) + term_ref[head]).astype(BF16)
        for number, end_grad in enumerate((first, second)):
            part = rows(number)
            col = column(cum_ref, number, head)
            factor = jnp.exp(col[BLK - 1 : BLK, :] - col)
            grad_values = part_values_ref[head, part, :] + mm(scaled_keys_ref[head, part, :], end_grad)
            grad_keys = part_keys_ref[head, part, :] + factor * mm_nt(
                values_ref[0, part, lanes(head)], end_grad
            )
            d_values_buf[head, part, :] = grad_values.astype(BF16)
            d_keys_buf[head, part, :] = grad_keys.astype(BF16)

    over_heads(None, body, leave)


def shape(dims, kind):
    return jax.ShapeDtypeStruct(dims, kind)


HBM = pl.BlockSpec(memory_space=pltpu.HBM)
SMEM = pl.BlockSpec(memory_space=pltpu.SMEM)
VMEM = pl.BlockSpec(memory_space=pltpu.VMEM)
WIDE = shape((1, ROWS, COLS), BF16)
HEAD_ROWS = (HL, ROWS, HD)
HEAD_PROMPT = (HL, P_DEV, HD)
HEAD_REPLY = (HL, BLK, HD)
STATE = (HL, HD, HD)
PIECES = (N_SEQ, PIECE, HD)
TWO_PIECES = (N_SEQ, 2 * PIECE, HD)
SENT_PIECES = (N_SEQ, PIECE + 16, HD)
CUM = (ROWS, HD)


def call(kernel, name, in_specs, outs, scratch, semaphores, mib, flops, moved, aliases=None):
    return pl.pallas_call(
        kernel,
        in_specs=in_specs,
        out_specs=[spec for spec, _ in outs],
        out_shape=[made for _, made in outs],
        scratch_shapes=[pltpu.VMEM(dims, kind) for dims, kind in scratch]
        + [pltpu.SemaphoreType.DMA((count, HL)) for count in semaphores],
        input_output_aliases=aliases or {},
        compiler_params=pltpu.CompilerParams(vmem_limit_bytes=mib << 20),
        cost_estimate=pl.CostEstimate(
            flops=int(flops), bytes_accessed=int(moved) << 20, transcendentals=0
        ),
        name=name,
    )


def summarize(decay_rows, keys, values):
    return call(
        summary_kernel, "summary", [VMEM, HBM, HBM],
        [
            (VMEM, shape(SENT_PIECES, BF16)), (VMEM, shape(STATE, F32)),
            (VMEM, shape((HL, ROWS), F32)), (VMEM, shape((HL, 8, HD), F32)),
        ],
        [(HEAD_PROMPT, BF16), (HEAD_PROMPT, BF16)], [2], 52, 3e8, 4,
    )(decay_rows, keys, values)


def inside(cum_rows, queries, keys, values):
    return call(
        within_kernel, "within", [VMEM] + [HBM] * 3,
        [
            (VMEM, shape(CUM, F32)), (HBM, shape(HEAD_ROWS, F32)), (HBM, shape(HEAD_ROWS, BF16)),
            (HBM, shape(HEAD_PROMPT, BF16)), (VMEM, shape((8, HD), F32)),
        ],
        [(HEAD_ROWS, BF16)] * 3 + [(HEAD_ROWS, F32), (HEAD_ROWS, BF16), (HEAD_PROMPT, BF16)],
        [3, 3], 56, 4e9, 16,
    )(cum_rows, queries, keys, values)


def forward_scan(parents, got, after):
    return call(
        forward_scan_kernel, "forward_scan", [SMEM, VMEM, HBM],
        [(VMEM, shape(TWO_PIECES, BF16)), (VMEM, shape((N_SEQ, HD), F32))],
        [], [], 12, 1e6, 1,
    )(parents, got, after)


def attend(ends, gains, scaled_queries, d_out, within, starts, term):
    return call(
        attend_kernel, "attend", [VMEM] * 7,
        [
            (VMEM, shape(HEAD_ROWS, F32)), (VMEM, shape(STATE, BF16)),
            (VMEM, shape((HL, 16, HD), F32)),
        ],
        [(CUM, F32), (CUM, F32)], [], 20, 3e8, 10,
    )(ends, gains, scaled_queries, d_out, within, starts, term)


def grads(ends, gains, stats, scaled_queries, d_out, attended):
    return call(
        grad_kernel, "grad", [VMEM] * 6, [(VMEM, shape(TWO_PIECES, BF16))],
        [(CUM, F32), (CUM, F32)], [], 20, 3e8, 10,
    )(ends, gains, stats, scaled_queries, d_out, attended)[0]


def local_grads(
    cum, cum_rows, stats, gains, queries, keys, values, d_out, attended, starts, second
):
    return call(
        local_grads_kernel, "local_grads", [VMEM] * 4 + [HBM] * 7,
        [
            (HBM, WIDE), (HBM, WIDE), (HBM, shape(HEAD_PROMPT, F32)),
            (HBM, shape(HEAD_PROMPT, F32)), (HBM, WIDE), (HBM, WIDE), (HBM, shape(STATE, F32)),
            (VMEM, shape((8, HD), F32)),
        ],
        [(HEAD_ROWS, BF16)] * 4 + [(HEAD_ROWS, F32), (TWO_PIECES, BF16), (STATE, BF16)]
        + [(HEAD_ROWS, BF16)] * 2 + [(HEAD_PROMPT, F32)] * 2 + [(HEAD_REPLY, BF16)] * 2
        + [(STATE, F32), (CUM, F32), (CUM, F32)],
        [7, 7], 56, 6e9, 24,
    )(cum, cum_rows, stats, gains, queries, keys, values, d_out, attended, starts, second)


def far_grads(cum, ends, far, term, scaled_keys, values, part_keys, part_values, d_keys, d_values):
    return call(
        far_grads_kernel, "far_grads", [VMEM] * 8 + [HBM] * 2,
        [(HBM, WIDE), (HBM, WIDE)],
        [(HEAD_PROMPT, BF16), (HEAD_PROMPT, BF16)], [2], 24, 3e8, 10, {8: 0, 9: 1},
    )(cum, ends, far, term, scaled_keys, values, part_keys, part_values, d_keys, d_values)


def backward_scan(parents, got, decays, after):
    return call(
        backward_scan_kernel, "backward_scan", [SMEM, VMEM, VMEM, HBM],
        [(VMEM, shape(PIECES, BF16))], [], [], 12, 1e6, 1,
    )(parents, got, decays, after)[0]


def everyone(array, axis):
    return lax.all_to_all(array, axis, 0, 0, tiled=True)


def local(queries, keys, values, log_decay, gain, parents, d_out):
    gains = gain.reshape(HL, HD)
    decay_rows = jnp.swapaxes(log_decay, 1, 2)
    send, first_term, cum_rows, block_ends = summarize(decay_rows, keys, values)
    got = everyone(send, "seq")
    cum, within, scaled_queries, scaled_keys, done = inside(cum_rows, queries, keys, values)
    send, decays = forward_scan(parents, got, done)
    starts = everyone(send, "seq")
    attended, second, stats = attend(
        block_ends, gains, scaled_queries, d_out, within, starts, first_term
    )
    stats = everyone(stats, "head")
    send = grads(block_ends, gains, stats, scaled_queries, d_out, attended)
    got = everyone(send, "seq")
    out, d_queries, part_keys, part_values, d_keys, d_values, last_term, done = local_grads(
        cum, cum_rows, stats, gains, queries, keys, values, d_out, attended, starts, second
    )
    far = everyone(backward_scan(parents, got, decays, done), "seq")
    d_keys, d_values = far_grads(
        cum, block_ends, far, last_term, scaled_keys, values, part_keys, part_values,
        d_keys, d_values,
    )
    return (out, d_queries, d_keys, d_values)


def solution(mesh):
    cut = P("seq", None, "head")
    return jax.shard_map(
        local,
        mesh=mesh,
        in_specs=(cut, cut, cut, cut, P("head"), P(), cut),
        out_specs=(cut, cut, cut, cut),
        check_vma=False,
    )
```

```python
import jax
import jax.numpy as jnp
from jax import lax
from jax.experimental import pallas as pl
from jax.experimental.pallas import tpu as pltpu
from jax.sharding import PartitionSpec as P

H = 64
HD = 128
BLK = 256
PROMPTS = 2
P_DEV = 512
ROWS = 768
HL = 8
N_SEQ = 32
SPAN = N_SEQ // PROMPTS
COLS = HL * HD
PIECE = HL * HD // N_SEQ
PARTS = HD // PIECE
BLOCKS = ROWS // BLK
TILES = ROWS // HD
EPS = 1e-05

F32 = jnp.float32
BF16 = jnp.bfloat16


def dot(a, b, dims):
    return lax.dot_general(a, b, (dims, ((), ())), preferred_element_type=F32)


def mm(a, b):
    return dot(a, b, ((1,), (0,)))


def mm_nt(a, b):
    return dot(a, b, ((1,), (1,)))


def mm_tn(a, b):
    return dot(a, b, ((0,), (0,)))


def rows(number):
    return slice(number * BLK, (number + 1) * BLK)


def tile_rows(tile):
    return slice(tile * HD, (tile + 1) * HD)


def down(row):
    return jnp.broadcast_to(row, (HD, BLK)).T


def twice(block):
    return jnp.concatenate([block, block], axis=1)


def rounded_product(block, factor):
    return (block.astype(F32) * factor).astype(BF16)


def lanes(head):
    return pl.ds(pl.multiple_of(head * HD, HD), HD)


def of_rows(ref, count=ROWS, first=0):
    if len(ref.shape) == 3:
        return lambda head: ref.at[0, pl.ds(first, count), lanes(head)]
    return lambda head: ref.at[pl.ds(first, count), lanes(head)]


def of_lead(ref, count=1, first=0):
    if count == 1:
        return lambda head: ref.at[head + first]
    return lambda head: ref.at[pl.ds(head * count, count)]


class Copies:
    def __init__(self, pairs, sems):
        self.pairs, self.sems = pairs, sems

    def each(self, head):
        return [
            pltpu.make_async_copy(src(head), dst(head), self.sems.at[number, head])
            for number, (src, dst) in enumerate(self.pairs)
        ]

    def start(self, head):
        for copy in self.each(head):
            copy.start()

    def wait(self, head):
        for copy in self.each(head):
            copy.wait()


def over_heads(fetch, body, leave=None, started=False):
    if fetch is not None and not started:
        for head in range(HL):
            fetch.start(head)

    def step(head, carry):
        if fetch is not None:
            fetch.wait(head)
        body(head)
        if leave is not None:
            leave.start(head)
        return carry

    lax.fori_loop(0, HL, step, 0)
    if leave is not None:
        for head in range(HL):
            leave.wait(head)


def split(value):
    coarse = value.astype(BF16)
    rest = value - coarse.astype(F32)
    middle = rest.astype(BF16)
    return coarse, middle, (rest - middle.astype(F32)).astype(BF16)


def summary_kernel(
    decay_ref, keys_ref, values_ref,
    send_ref, term_ref, cum_rows_ref, ends_ref,
    keys_buf, values_buf, in_sems,
):
    fetch = Copies(
        [
            (of_rows(keys_ref, P_DEV), of_lead(keys_buf)),
            (of_rows(values_ref, P_DEV), of_lead(values_buf)),
        ],
        in_sems,
    )
    for head in range(HL):
        fetch.start(head)
    before = lax.broadcasted_iota(jnp.int32, (BLK, BLK), 0)
    after = lax.broadcasted_iota(jnp.int32, (BLK, BLK), 1)
    upper = jnp.where(before <= after, 1.0, 0.0).astype(BF16)
    stacked = jnp.concatenate(
        [decay_ref[0, :, rows(number)] for number in range(BLOCKS)], axis=0
    )
    coarse, middle, fine = (mm(part, upper) for part in split(stacked))
    cumulative = (fine + middle) + coarse
    for number in range(BLOCKS):
        total = cumulative[number * HL : (number + 1) * HL]
        cum_rows_ref[:, rows(number)] = total
        ends_ref[:, number, :] = jnp.broadcast_to(jnp.exp(total[:, BLK - 1 : BLK]), (HL, HD))
    row_ids = lax.broadcasted_iota(jnp.int32, (16, HD), 0)

    def body(head):
        terms = []
        for number in range(2):
            row = cum_rows_ref[pl.ds(head, 1), rows(number)]
            factor = jnp.exp(row[:, BLK - 1 : BLK] - row)
            turned = keys_buf[head, rows(number), :].T
            key_scaled = rounded_product(turned, factor)
            terms.append(mm(key_scaled, values_buf[head, rows(number), :]))
        term_ref[head] = terms[0]
        end_decays = ends_ref[head]
        summary = end_decays[1:2, :] * terms[0] + terms[1]
        decay = jnp.broadcast_to(end_decays[0:1, :] * end_decays[1:2, :], (16, HD))
        coarse, middle, _ = split(decay)
        packed = jnp.where(
            row_ids == 0, coarse.astype(F32), jnp.where(row_ids == 1, middle.astype(F32), 0.0)
        ).astype(BF16)
        for piece in range(PARTS):
            at = head * PARTS + piece
            send_ref[at, 0:PIECE, :] = summary[piece * PIECE : (piece + 1) * PIECE].astype(BF16)
            send_ref[at, PIECE : PIECE + 16, :] = packed

    def step(head, carry):
        fetch.wait(head)
        body(head)
        return carry

    lax.fori_loop(0, HL, step, 0)


def within_kernel(
    cum_rows_ref, queries_ref, keys_ref, values_ref,
    within_ref, scaled_keys_ref, done_ref,
    queries_buf, keys_buf, values_buf, within_buf, scaled_queries_buf, scaled_keys_buf,
    in_sems, out_sems,
):
    fetch = Copies(
        [
            (of_rows(queries_ref), of_lead(queries_buf)),
            (of_rows(keys_ref), of_lead(keys_buf)),
            (of_rows(values_ref), of_lead(values_buf)),
        ],
        in_sems,
    )
    leave = Copies(
        [
            (of_lead(within_buf), of_lead(within_ref)),
            (of_lead(scaled_queries_buf), of_lead(within_ref, first=HL)),
            (of_lead(scaled_keys_buf), of_lead(scaled_keys_ref)),
        ],
        out_sems,
    )
    done_ref[...] = jnp.zeros_like(done_ref)
    row_ids = lax.broadcasted_iota(jnp.int32, (BLK, BLK), 0)
    col_ids = lax.broadcasted_iota(jnp.int32, (BLK, BLK), 1)

    def body(head):
        for number in range(BLOCKS):
            part = rows(number)
            queries = queries_buf[head, part, :]
            keys = keys_buf[head, part, :]
            row = cum_rows_ref[pl.ds(head, 1), part]
            gaps = twice(down(row)) - row
            mask = jnp.where(row_ids >= col_ids, jnp.exp(gaps), 0.0)
            weights = (mm_nt(queries, keys) * mask).astype(BF16)
            within_buf[head, part, :] = mm(weights, values_buf[head, part, :]).astype(BF16)
            scaled_queries_buf[head, part, :] = rounded_product(queries, down(jnp.exp(row)))
            if number < 2:
                factor = down(jnp.exp(row[:, BLK - 1 : BLK] - row))
                scaled_keys_buf[head, part, :] = rounded_product(keys, factor)

    over_heads(fetch, body, leave)


def forward_scan_kernel(parents_ref, got_ref, _after, send_ref, decay_ref):
    totals = []
    for prompt in range(PROMPTS):
        carry = jnp.zeros((PIECE, HD), F32)
        for index in range(prompt * SPAN, (prompt + 1) * SPAN):
            packed = got_ref[index, PIECE : PIECE + 16, :].astype(F32)
            decay = packed[0:1, :] + packed[1:2, :]
            decay_ref[index : index + 1, :] = decay
            send_ref[index, 0:PIECE, :] = carry.astype(BF16)
            carry = decay * carry + got_ref[index, 0:PIECE, :].astype(F32)
        totals.append(carry)
    for index in range(N_SEQ):
        prompt = parents_ref[index] // SPAN
        chosen = jnp.where(prompt == 0, totals[0], totals[1])
        decay_ref[N_SEQ + index : N_SEQ + index + 1, :] = jnp.full((1, HD), prompt, F32)
        send_ref[index, PIECE : 2 * PIECE, :] = chosen.astype(BF16)


def attend_kernel(
    ends_ref, gain_ref, d_out_ref, starts_ref, term_ref, within_ref,
    queries_ref, attended_ref, stats_ref, kept_ref, states_ref,
    within_buf, states_buf, squares_ref, products_ref, in_sems, out_sems,
):
    fetch = Copies(
        [
            (of_lead(within_ref, first=HL), of_lead(queries_ref)),
            (of_lead(within_ref), of_lead(within_buf)),
        ],
        in_sems,
    )
    leave = Copies(
        [
            (of_lead(attended_ref), of_lead(kept_ref)),
            (of_lead(states_buf, BLOCKS), of_lead(states_ref, BLOCKS)),
        ],
        out_sems,
    )
    for head in range(HL):
        fetch.start(head)
    squares_ref[...] = jnp.zeros_like(squares_ref)
    products_ref[...] = jnp.zeros_like(products_ref)

    def body(head):
        got = starts_ref[pl.ds(head * PARTS, PARTS)]
        first = got[:, 0:PIECE, :].reshape(HD, HD)
        reply = got[:, PIECE : 2 * PIECE, :].reshape(HD, HD)
        end_decay = ends_ref[head][0:1, :]
        second = (end_decay * first.astype(F32) + term_ref[head]).astype(BF16)
        gain = gain_ref[pl.ds(head, 1), :]
        for number, start in enumerate((first, second, reply)):
            part = rows(number)
            states_buf[head * BLOCKS + number] = start
            attended = within_buf[head, part, :].astype(F32) + mm(
                queries_ref[head, part, :], start
            )
            attended_ref[head, part, :] = attended.astype(BF16)
            weighted = gain * d_out_ref[0, part, lanes(head)].astype(F32)
            squares_ref[part, :] += attended * attended
            products_ref[part, :] += weighted * attended

    over_heads(fetch, body, leave, started=True)
    stats_ref[...] = jnp.zeros_like(stats_ref)
    for tile in range(TILES):
        for base, sums_ref in ((0, squares_ref), (8, products_ref)):
            row = jnp.sum(sums_ref[tile_rows(tile), :].T, axis=0, keepdims=True)
            stats_ref[:, base + tile : base + tile + 1, :] = jnp.broadcast_to(
                row[None], (HL, 1, HD)
            )


def row_factors(stats_ref, inverse_ref, slope_ref):
    total = stats_ref[0]
    for source in range(1, HL):
        total = total + stats_ref[source]
    turned = jnp.concatenate([total, jnp.zeros((HD - 16, HD), F32)], axis=0).T
    for tile in range(TILES):
        squares = turned[:, tile : tile + 1]
        products = turned[:, 8 + tile : 9 + tile]
        inverse = lax.rsqrt(squares / (H * HD) + EPS)
        slope = inverse * inverse * inverse * products / (H * HD)
        inverse_ref[tile_rows(tile), :] = jnp.broadcast_to(inverse, (HD, HD))
        slope_ref[tile_rows(tile), :] = jnp.broadcast_to(slope, (HD, HD))


def grad_kernel(
    ends_ref, gain_ref, stats_ref, queries_ref, d_out_ref, attended_ref,
    send_ref, inverse_ref, slope_ref,
):
    row_factors(stats_ref, inverse_ref, slope_ref)

    def body(head):
        gain = gain_ref[pl.ds(head, 1), :]
        terms = []
        for number in range(BLOCKS):
            part = rows(number)
            weighted = gain * d_out_ref[0, part, lanes(head)].astype(F32)
            grad = (
                inverse_ref[part, :] * weighted
                - attended_ref[head, part, :].astype(F32) * slope_ref[part, :]
            ).astype(BF16)
            terms.append(mm_tn(queries_ref[head, part, :], grad))
        local_sum = ends_ref[head][0:1, :] * terms[1] + terms[0]
        for piece in range(PARTS):
            at = head * PARTS + piece
            part = slice(piece * PIECE, (piece + 1) * PIECE)
            send_ref[at, 0:PIECE, :] = local_sum[part].astype(BF16)
            send_ref[at, PIECE : 2 * PIECE, :] = terms[2][part].astype(BF16)

    over_heads(None, body)


def backward_scan_kernel(got_ref, decay_ref, _after, send_ref):
    branches = [jnp.zeros((PIECE, HD), F32) for _ in range(PROMPTS)]
    for index in range(N_SEQ):
        prompt = decay_ref[N_SEQ + index : N_SEQ + index + 1, :]
        start_grad = got_ref[index, PIECE : 2 * PIECE, :].astype(F32)
        for each in range(PROMPTS):
            branches[each] = branches[each] + jnp.where(prompt == each, start_grad, 0.0)
    for prompt in range(PROMPTS):
        carry = branches[prompt]
        for index in reversed(range(prompt * SPAN, (prompt + 1) * SPAN)):
            send_ref[index] = carry.astype(BF16)
            carry = decay_ref[index : index + 1, :] * carry + got_ref[index, 0:PIECE, :].astype(F32)


def local_grads_kernel(
    cum_rows_ref, stats_ref, gain_ref,
    queries_ref, keys_ref, values_ref, d_out_ref, attended_ref, states_ref,
    out_ref, d_queries_ref, d_keys_ref, d_values_ref, term_ref, done_ref,
    queries_buf, keys_buf, values_buf, d_out_buf, attended_buf, states_buf,
    out_buf, d_queries_buf, d_keys_buf, d_values_buf, term_buf,
    inverse_ref, slope_ref, in_sems, out_sems,
):
    fetch = Copies(
        [
            (of_rows(d_out_ref), of_lead(d_out_buf)),
            (of_lead(attended_ref), of_lead(attended_buf)),
            (of_rows(queries_ref), of_lead(queries_buf)),
            (of_rows(keys_ref), of_lead(keys_buf)),
            (of_rows(values_ref), of_lead(values_buf)),
            (of_lead(states_ref, BLOCKS), of_lead(states_buf, BLOCKS)),
        ],
        in_sems,
    )
    leave = Copies(
        [
            (of_lead(out_buf), of_rows(out_ref)),
            (of_lead(d_queries_buf), of_rows(d_queries_ref)),
            (of_lead(d_keys_buf), of_rows(d_keys_ref)),
            (of_lead(d_values_buf), of_rows(d_values_ref)),
            (of_lead(term_buf), of_lead(term_ref)),
        ],
        out_sems,
    )
    for head in range(HL):
        fetch.start(head)
    done_ref[...] = jnp.zeros_like(done_ref)
    row_factors(stats_ref, inverse_ref, slope_ref)
    row_ids = lax.broadcasted_iota(jnp.int32, (BLK, BLK), 0)
    col_ids = lax.broadcasted_iota(jnp.int32, (BLK, BLK), 1)

    def body(head):
        gain = gain_ref[pl.ds(head, 1), :]
        for number in range(BLOCKS):
            part = rows(number)
            queries = queries_buf[head, part, :]
            keys = keys_buf[head, part, :]
            values = values_buf[head, part, :]
            attended = attended_buf[head, part, :].astype(F32)
            inverse = inverse_ref[part, :]
            weighted = gain * d_out_buf[head, part, :].astype(F32)
            grad = (inverse * weighted - attended * slope_ref[part, :]).astype(BF16)
            out_buf[head, part, :] = (attended * inverse * gain).astype(BF16)
            row = cum_rows_ref[pl.ds(head, 1), part]
            gaps = row - twice(down(row))
            mask = jnp.where(col_ids >= row_ids, jnp.exp(gaps), 0.0)
            weights = (mm_nt(keys, queries) * mask).astype(BF16)
            score_grad = (mm_nt(values, grad) * mask).astype(BF16)
            growth = down(jnp.exp(row))
            start = states_buf[head * BLOCKS + number]
            grad_queries = mm_tn(score_grad, keys) + growth * mm_nt(grad, start)
            d_queries_buf[head, part, :] = grad_queries.astype(BF16)
            if number == 1:
                term_buf[head] = mm_tn(rounded_product(queries, growth), grad)
            d_keys_buf[head, part, :] = mm(score_grad, queries).astype(BF16)
            d_values_buf[head, part, :] = mm(weights, grad).astype(BF16)

    over_heads(fetch, body, leave, started=True)


def far_grads_kernel(
    cum_rows_ref, ends_ref, far_ref, scaled_keys_ref, values_ref, term_ref,
    near_keys_ref, near_values_ref, d_keys_ref, d_values_ref,
    term_buf, near_keys_buf, near_values_buf, d_keys_buf, d_values_buf, in_sems, out_sems,
):
    fetch = Copies(
        [
            (of_lead(term_ref), of_lead(term_buf)),
            (of_rows(near_keys_ref, P_DEV), of_lead(near_keys_buf)),
            (of_rows(near_values_ref, P_DEV), of_lead(near_values_buf)),
        ],
        in_sems,
    )
    leave = Copies(
        [
            (of_lead(d_keys_buf), of_rows(d_keys_ref, P_DEV)),
            (of_lead(d_values_buf), of_rows(d_values_ref, P_DEV)),
        ],
        out_sems,
    )

    def body(head):
        second = far_ref[pl.ds(head * PARTS, PARTS)].reshape(HD, HD)
        first = (ends_ref[head][1:2, :] * second.astype(F32) + term_buf[head]).astype(BF16)
        for number, end_grad in enumerate((first, second)):
            part = rows(number)
            row = cum_rows_ref[pl.ds(head, 1), part]
            factor = down(jnp.exp(row[:, BLK - 1 : BLK] - row))
            grad_values = near_values_buf[head, part, :].astype(F32) + mm(
                scaled_keys_ref[head, part, :], end_grad
            )
            grad_keys = near_keys_buf[head, part, :].astype(F32) + factor * mm_nt(
                values_ref[0, part, lanes(head)], end_grad
            )
            d_values_buf[head, part, :] = grad_values.astype(BF16)
            d_keys_buf[head, part, :] = grad_keys.astype(BF16)

    over_heads(fetch, body, leave)


def shape(dims, kind):
    return jax.ShapeDtypeStruct(dims, kind)


HBM = pl.BlockSpec(memory_space=pltpu.HBM)
SMEM = pl.BlockSpec(memory_space=pltpu.SMEM)
VMEM = pl.BlockSpec(memory_space=pltpu.VMEM)
WIDE = shape((1, ROWS, COLS), BF16)
HEAD_ROWS = (HL, ROWS, HD)
HEAD_PROMPT = (HL, P_DEV, HD)
HEAD_REPLY = (HL, BLK, HD)
STATE = (HL, HD, HD)
PIECES = (N_SEQ, PIECE, HD)
TWO_PIECES = (N_SEQ, 2 * PIECE, HD)
SENT_PIECES = (N_SEQ, PIECE + 16, HD)
CUM = (ROWS, HD)
FAR = 160


def call(kernel, name, in_specs, outs, scratch, semaphores, mib, flops, moved, aliases=None):
    return pl.pallas_call(
        kernel,
        in_specs=in_specs,
        out_specs=[spec for spec, _ in outs],
        out_shape=[made for _, made in outs],
        scratch_shapes=[pltpu.VMEM(dims, kind) for dims, kind in scratch]
        + [pltpu.SemaphoreType.DMA((count, HL)) for count in semaphores],
        input_output_aliases=aliases or {},
        compiler_params=pltpu.CompilerParams(vmem_limit_bytes=mib << 20),
        cost_estimate=pl.CostEstimate(
            flops=int(flops), bytes_accessed=int(moved) << 20, transcendentals=0
        ),
        name=name,
    )


def summarize(decay_rows, keys, values):
    return call(
        summary_kernel, "summary", [VMEM, HBM, HBM],
        [
            (VMEM, shape(SENT_PIECES, BF16)), (VMEM, shape(STATE, F32)),
            (VMEM, shape((HL, ROWS), F32)), (VMEM, shape((HL, 8, HD), F32)),
        ],
        [(HEAD_PROMPT, BF16), (HEAD_PROMPT, BF16)], [2], 52, 3e8, 4,
    )(decay_rows, keys, values)


def inside(cum_rows, queries, keys, values):
    return call(
        within_kernel, "within", [VMEM] + [HBM] * 3,
        [
            (HBM, shape((FAR, ROWS, HD), BF16)), (HBM, shape(HEAD_PROMPT, BF16)),
            (VMEM, shape((8, HD), F32)),
        ],
        [(HEAD_ROWS, BF16)] * 5 + [(HEAD_PROMPT, BF16)], [3, 3], 52, 4e9, 16,
    )(cum_rows, queries, keys, values)


def forward_scan(parents, got, after):
    return call(
        forward_scan_kernel, "forward_scan", [SMEM, VMEM, HBM],
        [(VMEM, shape(TWO_PIECES, BF16)), (VMEM, shape((2 * N_SEQ, HD), F32))],
        [], [], 12, 1e6, 1,
    )(parents, got, after)


def attend(ends, gains, d_out, starts, term, within):
    return call(
        attend_kernel, "attend", [VMEM] * 5 + [HBM],
        [
            (VMEM, shape(HEAD_ROWS, BF16)), (VMEM, shape(HEAD_ROWS, BF16)),
            (VMEM, shape((HL, 16, HD), F32)), (HBM, shape((FAR, ROWS, HD), BF16)),
            (HBM, shape((6 * FAR, HD, HD), BF16)),
        ],
        [(HEAD_ROWS, BF16), ((HL * BLOCKS, HD, HD), BF16), (CUM, F32), (CUM, F32)],
        [2, 2], 36, 3e8, 10,
    )(ends, gains, d_out, starts, term, within)


def grads(ends, gains, stats, scaled_queries, d_out, attended):
    return call(
        grad_kernel, "grad", [VMEM] * 6, [(VMEM, shape(TWO_PIECES, BF16))],
        [(CUM, F32), (CUM, F32)], [], 20, 3e8, 10,
    )(ends, gains, stats, scaled_queries, d_out, attended)[0]


def local_grads(cum_rows, stats, gains, queries, keys, values, d_out, attended, states):
    return call(
        local_grads_kernel, "local_grads", [VMEM] * 3 + [HBM] * 6,
        [
            (HBM, WIDE), (HBM, WIDE), (HBM, WIDE), (HBM, WIDE),
            (HBM, shape((4 * FAR, HD, HD), F32)), (VMEM, shape((8, HD), F32)),
        ],
        [(HEAD_ROWS, BF16)] * 5 + [((HL * BLOCKS, HD, HD), BF16)] + [(HEAD_ROWS, BF16)] * 4
        + [(STATE, F32), (CUM, F32), (CUM, F32)],
        [6, 5], 53, 6e9, 24,
    )(cum_rows, stats, gains, queries, keys, values, d_out, attended, states)


def far_grads(cum_rows, ends, far, scaled_keys, values, term, near_keys, near_values):
    return call(
        far_grads_kernel, "far_grads", [VMEM] * 5 + [HBM] * 3,
        [(HBM, WIDE), (HBM, WIDE)],
        [(STATE, F32)] + [(HEAD_PROMPT, BF16)] * 4, [3, 2], 36, 3e8, 10, {6: 0, 7: 1},
    )(cum_rows, ends, far, scaled_keys, values, term, near_keys, near_values)


def backward_scan(got, decays, after):
    return call(
        backward_scan_kernel, "backward_scan", [VMEM, VMEM, HBM],
        [(VMEM, shape(PIECES, BF16))], [], [], 12, 1e6, 1,
    )(got, decays, after)[0]


def everyone(array, axis):
    return lax.all_to_all(array, axis, 0, 0, tiled=True)


def local(queries, keys, values, log_decay, gain, parents, d_out):
    gains = gain.reshape(HL, HD)
    decay_rows = jnp.swapaxes(log_decay, 1, 2)
    send, first_term, cum_rows, block_ends = summarize(decay_rows, keys, values)
    got = everyone(send, "seq")
    within, scaled_keys, done = inside(cum_rows, queries, keys, values)
    send, decays = forward_scan(parents, got, done)
    starts = everyone(send, "seq")
    near_queries, attended, stats, kept, states = attend(
        block_ends, gains, d_out, starts, first_term, within
    )
    stats = everyone(stats, "head")
    send = grads(block_ends, gains, stats, near_queries, d_out, attended)
    got = everyone(send, "seq")
    out, d_queries, d_keys, d_values, last_term, done = local_grads(
        cum_rows, stats, gains, queries, keys, values, d_out, kept, states
    )
    far = everyone(backward_scan(got, decays, done), "seq")
    d_keys, d_values = far_grads(
        cum_rows, block_ends, far, scaled_keys, values, last_term, d_keys, d_values
    )
    return (out, d_queries, d_keys, d_values)


def solution(mesh):
    cut = P("seq", None, "head")
    return jax.shard_map(
        local,
        mesh=mesh,
        in_specs=(cut, cut, cut, cut, P("head"), P(), cut),
        out_specs=(cut, cut, cut, cut),
        check_vma=False,
    )
```

```python
import functools

import jax
import jax.numpy as jnp
from jax import lax
from jax.experimental import pallas as pl
from jax.experimental.pallas import tpu as pltpu
from jax.sharding import PartitionSpec as P

H = 64
HD = 128
BLK = 256
PROMPTS = 2
P_DEV = 512
ROWS = 768
HL = 8
N_SEQ = 32
SPAN = N_SEQ // PROMPTS
COLS = HL * HD
RING = 8
RINGS = N_SEQ // RING
PACK = 16
BLOCKS = ROWS // BLK
TILES = ROWS // HD
EPS = 1e-05

F32 = jnp.float32
BF16 = jnp.bfloat16


def dot(a, b, dims):
    return lax.dot_general(a, b, (dims, ((), ())), preferred_element_type=F32)


def mm(a, b):
    return dot(a, b, ((1,), (0,)))


def mm_nt(a, b):
    return dot(a, b, ((1,), (1,)))


def mm_tn(a, b):
    return dot(a, b, ((0,), (0,)))


def rows(number):
    return slice(number * BLK, (number + 1) * BLK)


def tile_rows(tile):
    return slice(tile * HD, (tile + 1) * HD)


def down(row):
    return jnp.broadcast_to(row, (HD, BLK)).T


def twice(block):
    return jnp.concatenate([block, block], axis=1)


def rounded_product(block, factor):
    return (block.astype(F32) * factor).astype(BF16)


def lanes(head):
    return pl.ds(pl.multiple_of(head * HD, HD), HD)


def of_rows(ref, count=ROWS, first=0):
    if len(ref.shape) == 3:
        return lambda head: ref.at[0, pl.ds(first, count), lanes(head)]
    return lambda head: ref.at[pl.ds(first, count), lanes(head)]


def of_lead(ref, count=1, first=0):
    if count == 1:
        return lambda head: ref.at[head + first]
    return lambda head: ref.at[pl.ds(head * count, count)]


def of_head_rows(ref, count, first):
    return lambda head: ref.at[head, pl.ds(first, count)]


class Copies:
    def __init__(self, pairs, sems):
        self.pairs, self.sems = pairs, sems

    def each(self, head):
        return [
            pltpu.make_async_copy(src(head), dst(head), self.sems.at[number, head])
            for number, (src, dst) in enumerate(self.pairs)
        ]

    def start(self, head):
        for copy in self.each(head):
            copy.start()

    def wait(self, head):
        for copy in self.each(head):
            copy.wait()


def over_heads(fetch, body, leave=None, started=False):
    if fetch is not None and not started:
        for head in range(HL):
            fetch.start(head)

    def step(head, carry):
        if fetch is not None:
            fetch.wait(head)
        body(head)
        if leave is not None:
            leave.start(head)
        return carry

    lax.fori_loop(0, HL, step, 0)
    if leave is not None:
        for head in range(HL):
            leave.wait(head)


def split(value):
    coarse = value.astype(BF16)
    rest = value - coarse.astype(F32)
    middle = rest.astype(BF16)
    return coarse, middle, (rest - middle.astype(F32)).astype(BF16)


def packed(decay):
    coarse, middle, _ = split(jnp.broadcast_to(decay, (PACK, HD)))
    row_ids = lax.broadcasted_iota(jnp.int32, (PACK, HD), 0)
    return jnp.where(
        row_ids == 0, coarse.astype(F32), jnp.where(row_ids == 1, middle.astype(F32), 0.0)
    ).astype(BF16)


def unpacked(block):
    both = block.astype(F32)
    return both[0:1, :] + both[1:2, :]


def summary_kernel(
    decay_ref, keys_ref, values_ref,
    send_ref, term_ref, cum_rows_ref, ends_ref,
    keys_buf, values_buf, in_sems,
):
    fetch = Copies(
        [
            (of_rows(keys_ref, P_DEV), of_lead(keys_buf)),
            (of_rows(values_ref, P_DEV), of_lead(values_buf)),
        ],
        in_sems,
    )
    for head in range(HL):
        fetch.start(head)
    before = lax.broadcasted_iota(jnp.int32, (BLK, BLK), 0)
    after = lax.broadcasted_iota(jnp.int32, (BLK, BLK), 1)
    upper = jnp.where(before <= after, 1.0, 0.0).astype(BF16)
    stacked = jnp.concatenate(
        [decay_ref[0, :, rows(number)] for number in range(BLOCKS)], axis=0
    )
    coarse, middle, fine = (mm(part, upper) for part in split(stacked))
    cumulative = (fine + middle) + coarse
    for number in range(BLOCKS):
        total = cumulative[number * HL : (number + 1) * HL]
        cum_rows_ref[:, rows(number)] = total
        ends_ref[:, number, :] = jnp.broadcast_to(jnp.exp(total[:, BLK - 1 : BLK]), (HL, HD))

    def body(head):
        terms = []
        for number in range(2):
            row = cum_rows_ref[pl.ds(head, 1), rows(number)]
            factor = jnp.exp(row[:, BLK - 1 : BLK] - row)
            turned = keys_buf[head, rows(number), :].T
            key_scaled = rounded_product(turned, factor)
            terms.append(mm(key_scaled, values_buf[head, rows(number), :]))
        term_ref[head] = terms[0]
        end_decays = ends_ref[head]
        summary = end_decays[1:2, :] * terms[0] + terms[1]
        decay = end_decays[0:1, :] * end_decays[1:2, :]
        send_ref[head, 0:HD, :] = summary.astype(BF16)
        send_ref[head, HD : HD + PACK, :] = packed(decay)

    def step(head, carry):
        fetch.wait(head)
        body(head)
        return carry

    lax.fori_loop(0, HL, step, 0)


def within_kernel(
    cum_rows_ref, queries_ref, keys_ref, values_ref,
    within_ref, scaled_keys_ref, done_ref,
    queries_buf, keys_buf, values_buf, within_buf, scaled_queries_buf, scaled_keys_buf,
    in_sems, out_sems,
):
    fetch = Copies(
        [
            (of_rows(queries_ref), of_lead(queries_buf)),
            (of_rows(keys_ref), of_lead(keys_buf)),
            (of_rows(values_ref), of_lead(values_buf)),
        ],
        in_sems,
    )
    leave = Copies(
        [
            (of_lead(within_buf), of_lead(within_ref)),
            (of_lead(scaled_queries_buf), of_lead(within_ref, first=HL)),
            (of_lead(scaled_keys_buf), of_lead(scaled_keys_ref)),
        ],
        out_sems,
    )
    done_ref[...] = jnp.zeros_like(done_ref)
    row_ids = lax.broadcasted_iota(jnp.int32, (BLK, BLK), 0)
    col_ids = lax.broadcasted_iota(jnp.int32, (BLK, BLK), 1)

    def body(head):
        for number in range(BLOCKS):
            part = rows(number)
            queries = queries_buf[head, part, :]
            keys = keys_buf[head, part, :]
            row = cum_rows_ref[pl.ds(head, 1), part]
            gaps = twice(down(row)) - row
            mask = jnp.where(row_ids >= col_ids, jnp.exp(gaps), 0.0)
            weights = (mm_nt(queries, keys) * mask).astype(BF16)
            within_buf[head, part, :] = mm(weights, values_buf[head, part, :]).astype(BF16)
            scaled_queries_buf[head, part, :] = rounded_product(queries, down(jnp.exp(row)))
            if number < 2:
                factor = down(jnp.exp(row[:, BLK - 1 : BLK] - row))
                scaled_keys_buf[head, part, :] = rounded_product(keys, factor)

    over_heads(fetch, body, leave)


def ring_place():
    ring = lax.axis_index("seq") // RING
    return ring, ring % 2 == 1, ring // 2


def ring_prefix_kernel(got_ref, _after, part_ref, decay_ref, send_ref):
    carry = jnp.zeros((HD, HD), F32)
    before = jnp.ones((1, HD), F32)
    for place in range(RING):
        decay = unpacked(got_ref[place, HD : HD + PACK, :])
        decay_ref[place : place + 1, :] = decay
        decay_ref[RING + place : RING + place + 1, :] = before
        part_ref[place] = carry
        carry = decay * carry + got_ref[place, 0:HD, :].astype(F32)
        before = before * decay
    part_ref[RING] = carry
    decay_ref[2 * RING : 3 * RING, :] = jnp.broadcast_to(before, (RING, HD))
    send_ref[0:HD, :] = carry.astype(BF16)
    send_ref[HD : HD + PACK, :] = packed(before)


def ring_starts_kernel(
    parents_ref, part_ref, decay_ref, mate_ref, same_ref, cross_ref, send_ref, mate_decay_ref
):
    ring, upper, prompt = ring_place()
    own, own_decay = part_ref[RING], decay_ref[2 * RING : 2 * RING + 1, :]
    (mate, mate_decay), (same, same_decay), (cross, cross_decay) = (
        (ref[0:HD, :].astype(F32), unpacked(ref[HD : HD + PACK, :]))
        for ref in (mate_ref, same_ref, cross_ref)
    )
    mate_decay_ref[...] = jnp.broadcast_to(mate_decay, mate_decay_ref.shape)
    here = jnp.where(upper, own_decay * mate + own, mate_decay * own + mate)
    there = jnp.where(upper, same_decay * cross + same, cross_decay * same + cross)
    totals = (jnp.where(prompt == 0, here, there), jnp.where(prompt == 0, there, here))
    carry = jnp.where(upper, mate, 0.0)
    for place in range(RING):
        start = decay_ref[RING + place : RING + place + 1, :] * carry + part_ref[place]
        parent = parents_ref[ring * RING + place] // SPAN
        send_ref[place, 0:HD, :] = start.astype(BF16)
        send_ref[place, HD : 2 * HD, :] = jnp.where(parent == 0, totals[0], totals[1]).astype(BF16)


def attend_kernel(
    ends_ref, gain_ref, d_out_ref, starts_ref, term_ref, within_ref,
    queries_ref, attended_ref, stats_ref, kept_ref, states_ref,
    within_buf, states_buf, squares_ref, products_ref, in_sems, out_sems,
):
    fetch = Copies(
        [
            (of_lead(within_ref, first=HL), of_lead(queries_ref)),
            (of_lead(within_ref), of_lead(within_buf)),
        ],
        in_sems,
    )
    leave = Copies(
        [
            (of_lead(attended_ref), of_lead(kept_ref)),
            (of_lead(states_buf, BLOCKS), of_lead(states_ref, BLOCKS)),
        ],
        out_sems,
    )
    for head in range(HL):
        fetch.start(head)
    squares_ref[...] = jnp.zeros_like(squares_ref)
    products_ref[...] = jnp.zeros_like(products_ref)

    def body(head):
        first = starts_ref[head, 0:HD, :]
        reply = starts_ref[head, HD : 2 * HD, :]
        end_decay = ends_ref[head][0:1, :]
        second = (end_decay * first.astype(F32) + term_ref[head]).astype(BF16)
        gain = gain_ref[pl.ds(head, 1), :]
        for number, start in enumerate((first, second, reply)):
            part = rows(number)
            states_buf[head * BLOCKS + number] = start
            attended = within_buf[head, part, :].astype(F32) + mm(
                queries_ref[head, part, :], start
            )
            attended_ref[head, part, :] = attended.astype(BF16)
            weighted = gain * d_out_ref[0, part, lanes(head)].astype(F32)
            squares_ref[part, :] += attended * attended
            products_ref[part, :] += weighted * attended

    over_heads(fetch, body, leave, started=True)
    stats_ref[...] = jnp.zeros_like(stats_ref)
    for tile in range(TILES):
        for base, sums_ref in ((0, squares_ref), (8, products_ref)):
            row = jnp.sum(sums_ref[tile_rows(tile), :].T, axis=0, keepdims=True)
            stats_ref[:, base + tile : base + tile + 1, :] = jnp.broadcast_to(
                row[None], (HL, 1, HD)
            )


def row_factors(stats_ref, inverse_ref, slope_ref):
    total = stats_ref[0]
    for source in range(1, HL):
        total = total + stats_ref[source]
    turned = jnp.concatenate([total, jnp.zeros((HD - 16, HD), F32)], axis=0).T
    for tile in range(TILES):
        squares = turned[:, tile : tile + 1]
        products = turned[:, 8 + tile : 9 + tile]
        inverse = lax.rsqrt(squares / (H * HD) + EPS)
        slope = inverse * inverse * inverse * products / (H * HD)
        inverse_ref[tile_rows(tile), :] = jnp.broadcast_to(inverse, (HD, HD))
        slope_ref[tile_rows(tile), :] = jnp.broadcast_to(slope, (HD, HD))


def grad_kernel(
    ends_ref, gain_ref, stats_ref, queries_ref, d_out_ref, attended_ref,
    send_ref, inverse_ref, slope_ref,
):
    row_factors(stats_ref, inverse_ref, slope_ref)

    def body(head):
        gain = gain_ref[pl.ds(head, 1), :]
        terms = []
        for number in range(BLOCKS):
            part = rows(number)
            weighted = gain * d_out_ref[0, part, lanes(head)].astype(F32)
            grad = (
                inverse_ref[part, :] * weighted
                - attended_ref[head, part, :].astype(F32) * slope_ref[part, :]
            ).astype(BF16)
            terms.append(mm_tn(queries_ref[head, part, :], grad))
        local_sum = ends_ref[head][0:1, :] * terms[1] + terms[0]
        send_ref[head, 0:HD, :] = local_sum.astype(BF16)
        send_ref[head, HD : 2 * HD, :] = terms[2].astype(BF16)

    over_heads(None, body)


def ring_suffix_kernel(
    parents_ref, got_ref, decay_ref, _after, part_ref, later_ref, mate_send_ref, far_send_ref
):
    ring, _, prompt = ring_place()
    carry = jnp.zeros((HD, HD), F32)
    after = jnp.ones((1, HD), F32)
    mine = jnp.zeros((HD, HD), F32)
    theirs = jnp.zeros((HD, HD), F32)
    for place in reversed(range(RING)):
        decay = decay_ref[place : place + 1, :]
        part_ref[place] = carry
        later_ref[place : place + 1, :] = after
        carry = decay * carry + got_ref[place, 0:HD, :].astype(F32)
        after = after * decay
        start_grad = got_ref[place, HD : 2 * HD, :].astype(F32)
        ours = parents_ref[ring * RING + place] // SPAN == prompt
        mine = mine + jnp.where(ours, start_grad, 0.0)
        theirs = theirs + jnp.where(ours, 0.0, start_grad)
    part_ref[RING] = mine
    mate_send_ref[0:HD, :] = carry.astype(BF16)
    mate_send_ref[HD : 2 * HD, :] = mine.astype(BF16)
    far_send_ref[...] = theirs.astype(BF16)


def ring_ends_kernel(
    part_ref, later_ref, mate_decay_ref, mate_ref, same_ref, cross_ref, _after, send_ref
):
    _, upper, _ = ring_place()
    branch = (
        part_ref[RING]
        + mate_ref[HD : 2 * HD, :].astype(F32)
        + (same_ref[...].astype(F32) + cross_ref[...].astype(F32))
    )
    above = mate_decay_ref[0:1, :] * branch + mate_ref[0:HD, :].astype(F32)
    carry = jnp.where(upper, branch, above)
    for place in range(RING):
        send_ref[place] = (later_ref[place : place + 1, :] * carry + part_ref[place]).astype(BF16)


def local_grads_kernel(
    blocks, cum_rows_ref, stats_ref, gain_ref,
    queries_ref, keys_ref, values_ref, d_out_ref, attended_ref, states_ref, *refs
):
    first, count = blocks[0] * BLK, len(blocks) * BLK
    if first:
        refs = refs[4:]
    out_ref, d_queries_ref, d_keys_ref, d_values_ref = refs[:4]
    term_ref = None if first else refs[4]
    (
        done_ref, queries_buf, keys_buf, values_buf, d_out_buf, attended_buf, states_buf,
        out_buf, d_queries_buf, d_keys_buf, d_values_buf, term_buf,
        inverse_ref, slope_ref, in_sems, out_sems,
    ) = refs[-16:]
    fetch = Copies(
        [
            (of_rows(d_out_ref, count, first), of_lead(d_out_buf)),
            (of_head_rows(attended_ref, count, first), of_lead(attended_buf)),
            (of_rows(queries_ref, count, first), of_lead(queries_buf)),
            (of_rows(keys_ref, count, first), of_lead(keys_buf)),
            (of_rows(values_ref, count, first), of_lead(values_buf)),
            (of_lead(states_ref, BLOCKS), of_lead(states_buf, BLOCKS)),
        ],
        in_sems,
    )
    leaving = [
        (of_lead(out_buf), of_rows(out_ref, count, first)),
        (of_lead(d_queries_buf), of_rows(d_queries_ref, count, first)),
        (of_lead(d_keys_buf), of_rows(d_keys_ref, count, first)),
        (of_lead(d_values_buf), of_rows(d_values_ref, count, first)),
    ]
    if not first:
        leaving.append((of_lead(term_buf), of_lead(term_ref)))
    leave = Copies(leaving, out_sems)
    for head in range(HL):
        fetch.start(head)
    done_ref[...] = jnp.zeros_like(done_ref)
    row_factors(stats_ref, inverse_ref, slope_ref)
    row_ids = lax.broadcasted_iota(jnp.int32, (BLK, BLK), 0)
    col_ids = lax.broadcasted_iota(jnp.int32, (BLK, BLK), 1)

    def body(head):
        gain = gain_ref[pl.ds(head, 1), :]
        for number in blocks:
            part = rows(number - blocks[0])
            whole = rows(number)
            queries = queries_buf[head, part, :]
            keys = keys_buf[head, part, :]
            values = values_buf[head, part, :]
            attended = attended_buf[head, part, :].astype(F32)
            inverse = inverse_ref[whole, :]
            weighted = gain * d_out_buf[head, part, :].astype(F32)
            grad = (inverse * weighted - attended * slope_ref[whole, :]).astype(BF16)
            out_buf[head, part, :] = (attended * inverse * gain).astype(BF16)
            row = cum_rows_ref[pl.ds(head, 1), whole]
            gaps = row - twice(down(row))
            mask = jnp.where(col_ids >= row_ids, jnp.exp(gaps), 0.0)
            weights = (mm_nt(keys, queries) * mask).astype(BF16)
            score_grad = (mm_nt(values, grad) * mask).astype(BF16)
            growth = down(jnp.exp(row))
            start = states_buf[head * BLOCKS + number]
            grad_queries = mm_tn(score_grad, keys) + growth * mm_nt(grad, start)
            d_queries_buf[head, part, :] = grad_queries.astype(BF16)
            if number == 1:
                term_buf[head] = mm_tn(rounded_product(queries, growth), grad)
            d_keys_buf[head, part, :] = mm(score_grad, queries).astype(BF16)
            d_values_buf[head, part, :] = mm(weights, grad).astype(BF16)

    over_heads(fetch, body, leave, started=True)


def far_grads_kernel(
    cum_rows_ref, ends_ref, far_ref, scaled_keys_ref, values_ref, term_ref,
    near_keys_ref, near_values_ref, d_keys_ref, d_values_ref,
    term_buf, near_keys_buf, near_values_buf, d_keys_buf, d_values_buf, in_sems, out_sems,
):
    fetch = Copies(
        [
            (of_lead(term_ref), of_lead(term_buf)),
            (of_rows(near_keys_ref, P_DEV), of_lead(near_keys_buf)),
            (of_rows(near_values_ref, P_DEV), of_lead(near_values_buf)),
        ],
        in_sems,
    )
    leave = Copies(
        [
            (of_lead(d_keys_buf), of_rows(d_keys_ref, P_DEV)),
            (of_lead(d_values_buf), of_rows(d_values_ref, P_DEV)),
        ],
        out_sems,
    )

    def body(head):
        second = far_ref[head]
        first = (ends_ref[head][1:2, :] * second.astype(F32) + term_buf[head]).astype(BF16)
        for number, end_grad in enumerate((first, second)):
            part = rows(number)
            row = cum_rows_ref[pl.ds(head, 1), part]
            factor = down(jnp.exp(row[:, BLK - 1 : BLK] - row))
            grad_values = near_values_buf[head, part, :].astype(F32) + mm(
                scaled_keys_ref[head, part, :], end_grad
            )
            grad_keys = near_keys_buf[head, part, :].astype(F32) + factor * mm_nt(
                values_ref[0, part, lanes(head)], end_grad
            )
            d_values_buf[head, part, :] = grad_values.astype(BF16)
            d_keys_buf[head, part, :] = grad_keys.astype(BF16)

    over_heads(fetch, body, leave)


def shape(dims, kind):
    return jax.ShapeDtypeStruct(dims, kind)


HBM = pl.BlockSpec(memory_space=pltpu.HBM)
SMEM = pl.BlockSpec(memory_space=pltpu.SMEM)
VMEM = pl.BlockSpec(memory_space=pltpu.VMEM)
WIDE = shape((1, ROWS, COLS), BF16)
HEAD_ROWS = (HL, ROWS, HD)
HEAD_PROMPT = (HL, P_DEV, HD)
HEAD_REPLY = (HL, BLK, HD)
STATE = (HL, HD, HD)
TWO_STATES = (HL, 2 * HD, HD)
SENT_STATE = (HL, HD + PACK, HD)
PART = (RING + 1, HD, HD)
CUM = (ROWS, HD)
FAR = 160


def call(kernel, name, in_specs, outs, scratch, semaphores, mib, flops, moved, aliases=None):
    return pl.pallas_call(
        kernel,
        in_specs=in_specs,
        out_specs=[spec for spec, _ in outs],
        out_shape=[made for _, made in outs],
        scratch_shapes=[pltpu.VMEM(dims, kind) for dims, kind in scratch]
        + [pltpu.SemaphoreType.DMA((count, HL)) for count in semaphores],
        input_output_aliases=aliases or {},
        compiler_params=pltpu.CompilerParams(vmem_limit_bytes=mib << 20),
        cost_estimate=pl.CostEstimate(
            flops=int(flops), bytes_accessed=int(moved) << 20, transcendentals=0
        ),
        name=name,
    )


def summarize(decay_rows, keys, values):
    return call(
        summary_kernel, "summary", [VMEM, HBM, HBM],
        [
            (VMEM, shape(SENT_STATE, BF16)), (VMEM, shape(STATE, F32)),
            (VMEM, shape((HL, ROWS), F32)), (VMEM, shape((HL, 8, HD), F32)),
        ],
        [(HEAD_PROMPT, BF16), (HEAD_PROMPT, BF16)], [2], 52, 3e8, 4,
    )(decay_rows, keys, values)


def inside(cum_rows, queries, keys, values):
    return call(
        within_kernel, "within", [VMEM] + [HBM] * 3,
        [
            (HBM, shape((FAR, ROWS, HD), BF16)), (HBM, shape(HEAD_PROMPT, BF16)),
            (VMEM, shape((8, HD), F32)),
        ],
        [(HEAD_ROWS, BF16)] * 5 + [(HEAD_PROMPT, BF16)], [3, 3], 52, 4e9, 16,
    )(cum_rows, queries, keys, values)


def ring_prefix(got, after):
    return call(
        ring_prefix_kernel, "ring_prefix", [VMEM, HBM],
        [
            (VMEM, shape(PART, F32)), (VMEM, shape((3 * RING, HD), F32)),
            (VMEM, shape((HD + PACK, HD), BF16)),
        ],
        [], [], 12, 1e6, 1,
    )(got, after)


def ring_starts(parents, part, decays, mate, same, cross):
    return call(
        ring_starts_kernel, "ring_starts", [SMEM] + [VMEM] * 5,
        [(VMEM, shape(TWO_STATES, BF16)), (VMEM, shape((8, HD), F32))],
        [], [], 12, 1e6, 1,
    )(parents, part, decays, mate, same, cross)


def ring_suffix(parents, got, decays, after):
    return call(
        ring_suffix_kernel, "ring_suffix", [SMEM, VMEM, VMEM, HBM],
        [
            (VMEM, shape(PART, F32)), (VMEM, shape((RING, HD), F32)),
            (VMEM, shape((2 * HD, HD), BF16)), (VMEM, shape((HD, HD), BF16)),
        ],
        [], [], 12, 1e6, 1,
    )(parents, got, decays, after)


def ring_ends(part, later, mate_decay, mate, same, cross, after):
    return call(
        ring_ends_kernel, "ring_ends", [VMEM] * 6 + [HBM],
        [(VMEM, shape(STATE, BF16))], [], [], 12, 1e6, 1,
    )(part, later, mate_decay, mate, same, cross, after)[0]


def attend(ends, gains, d_out, starts, term, within):
    return call(
        attend_kernel, "attend", [VMEM] * 5 + [HBM],
        [
            (VMEM, shape(HEAD_ROWS, BF16)), (VMEM, shape(HEAD_ROWS, BF16)),
            (VMEM, shape((HL, 16, HD), F32)), (HBM, shape((FAR, ROWS, HD), BF16)),
            (HBM, shape((6 * FAR, HD, HD), BF16)),
        ],
        [(HEAD_ROWS, BF16), ((HL * BLOCKS, HD, HD), BF16), (CUM, F32), (CUM, F32)],
        [2, 2], 36, 3e8, 10,
    )(ends, gains, d_out, starts, term, within)


def grads(ends, gains, stats, scaled_queries, d_out, attended):
    return call(
        grad_kernel, "grad", [VMEM] * 6, [(VMEM, shape(TWO_STATES, BF16))],
        [(CUM, F32), (CUM, F32)], [], 20, 3e8, 10,
    )(ends, gains, stats, scaled_queries, d_out, attended)[0]


def local_grads(
    blocks, cum_rows, stats, gains, queries, keys, values, d_out, attended, states, *partly
):
    some = (HL, len(blocks) * BLK, HD)
    term = [] if partly else [(HBM, shape((4 * FAR, HD, HD), F32))]
    left = 4 + len(term)
    return call(
        functools.partial(local_grads_kernel, blocks), "reply_grads" if partly else "local_grads",
        [VMEM] * 3 + [HBM] * (6 + len(partly)),
        [(HBM, WIDE)] * 4 + term + [(VMEM, shape((8, HD), F32))],
        [(some, BF16)] * 5 + [((HL * BLOCKS, HD, HD), BF16)] + [(some, BF16)] * 4
        + [(STATE, F32), (CUM, F32), (CUM, F32)],
        [6, left], 53, 2e9 * len(blocks), 8 * len(blocks),
        {9 + number: number for number in range(len(partly))},
    )(cum_rows, stats, gains, queries, keys, values, d_out, attended, states, *partly)


def far_grads(cum_rows, ends, far, scaled_keys, values, term, near_keys, near_values):
    return call(
        far_grads_kernel, "far_grads", [VMEM] * 5 + [HBM] * 3,
        [(HBM, WIDE), (HBM, WIDE)],
        [(STATE, F32)] + [(HEAD_PROMPT, BF16)] * 4, [3, 2], 36, 3e8, 10, {6: 0, 7: 1},
    )(cum_rows, ends, far, scaled_keys, values, term, near_keys, near_values)


def around(array):
    groups = [[ring * RING + place for place in range(RING)] for ring in range(RINGS)]
    return lax.all_to_all(array, "seq", 0, 0, axis_index_groups=groups, tiled=True)


def across(array, step):
    pairs = [(index, index ^ (step * RING)) for index in range(N_SEQ)]
    return lax.ppermute(array, "seq", pairs)


def everyone(array):
    return lax.all_to_all(array, "head", 0, 0, tiled=True)


def local(queries, keys, values, log_decay, gain, parents, d_out):
    gains = gain.reshape(HL, HD)
    decay_rows = jnp.swapaxes(log_decay, 1, 2)
    send, first_term, cum_rows, block_ends = summarize(decay_rows, keys, values)
    got = around(send)
    within, scaled_keys, done = inside(cum_rows, queries, keys, values)
    part, decays, send = ring_prefix(got, done)
    send, mate_decay = ring_starts(
        parents, part, decays, across(send, 1), across(send, 2), across(send, 3)
    )
    starts = around(send)
    near_queries, attended, stats, kept, states = attend(
        block_ends, gains, d_out, starts, first_term, within
    )
    stats = everyone(stats)
    send = grads(block_ends, gains, stats, near_queries, d_out, attended)
    got = around(send)
    operands = (cum_rows, stats, gains, queries, keys, values, d_out, kept, states)
    *partly, last_term, done = local_grads((0, 1), *operands)
    part, later, mate_send, far_send = ring_suffix(parents, got, decays, done)
    mate, same, cross = across(mate_send, 1), across(far_send, 2), across(far_send, 3)
    out, d_queries, d_keys, d_values, done = local_grads((2,), *operands, *partly)
    far = around(ring_ends(part, later, mate_decay, mate, same, cross, done))
    d_keys, d_values = far_grads(
        cum_rows, block_ends, far, scaled_keys, values, last_term, d_keys, d_values
    )
    return (out, d_queries, d_keys, d_values)


def solution(mesh):
    cut = P("seq", None, "head")
    return jax.shard_map(
        local,
        mesh=mesh,
        in_specs=(cut, cut, cut, cut, P("head"), P(), cut),
        out_specs=(cut, cut, cut, cut),
        check_vma=False,
    )
```

```python
import jax
import jax.numpy as jnp
from jax import lax
from jax.experimental import pallas as pl
from jax.experimental.pallas import tpu as pltpu
from jax.sharding import PartitionSpec as P

H = 64
HD = 128
BLK = 256
PROMPTS = 2
P_DEV = 512
ROWS = 768
HL = 8
N_SEQ = 32
SPAN = N_SEQ // PROMPTS
COLS = HL * HD
PIECE = HL * HD // N_SEQ
PARTS = HD // PIECE
BLOCKS = ROWS // BLK
TILES = ROWS // HD
EPS = 1e-05
GROUP = 2

F32 = jnp.float32
BF16 = jnp.bfloat16


def dot(a, b, dims):
    return lax.dot_general(a, b, (dims, ((), ())), preferred_element_type=F32)


def mm(a, b):
    return dot(a, b, ((1,), (0,)))


def mm_nt(a, b):
    return dot(a, b, ((1,), (1,)))


def mm_tn(a, b):
    return dot(a, b, ((0,), (0,)))


def rows(number):
    return slice(number * BLK, (number + 1) * BLK)


def tile_rows(tile):
    return slice(tile * HD, (tile + 1) * HD)


def down(row):
    return jnp.broadcast_to(row, (HD, BLK)).T


def twice(block):
    return jnp.concatenate([block, block], axis=1)


def rounded_product(block, factor):
    return (block.astype(F32) * factor).astype(BF16)


def lanes(head):
    return pl.ds(pl.multiple_of(head * HD, HD), HD)


def of_rows(ref, count=ROWS, first=0):
    if len(ref.shape) == 3:
        return lambda head: ref.at[0, pl.ds(first, count), lanes(head)]
    return lambda head: ref.at[pl.ds(first, count), lanes(head)]


def of_lead(ref, count=1, first=0):
    if count == 1:
        return lambda head: ref.at[head + first]
    return lambda head: ref.at[pl.ds(head * count, count)]


class Copies:
    def __init__(self, pairs, sems):
        self.pairs, self.sems = pairs, sems

    def each(self, head):
        return [
            pltpu.make_async_copy(src(head), dst(head), self.sems.at[number, head])
            for number, (src, dst) in enumerate(self.pairs)
        ]

    def start(self, head):
        for copy in self.each(head):
            copy.start()

    def begin(self):
        for head in range(HL):
            self.start(head)

    def wait(self, head):
        for copy in self.each(head):
            copy.wait()


def over_heads(fetch, body, leave=None, started=False, group=GROUP):
    if fetch is not None and not started:
        fetch.begin()

    def step(number, carry):
        heads = [number * group + place for place in range(group)]
        for head in heads:
            if fetch is not None:
                fetch.wait(head)
        for head in heads:
            body(head)
        for head in heads:
            if leave is not None:
                leave.start(head)
        return carry

    lax.fori_loop(0, HL // group, step, 0)
    if leave is not None:
        for head in range(HL):
            leave.wait(head)


def split(value):
    coarse = value.astype(BF16)
    rest = value - coarse.astype(F32)
    middle = rest.astype(BF16)
    return coarse, middle, (rest - middle.astype(F32)).astype(BF16)


def summary_kernel(
    decay_ref, keys_ref, values_ref,
    send_ref, term_ref, cum_rows_ref, ends_ref,
    keys_buf, values_buf, in_sems,
):
    fetch = Copies(
        [
            (of_rows(keys_ref, P_DEV), of_lead(keys_buf)),
            (of_rows(values_ref, P_DEV), of_lead(values_buf)),
        ],
        in_sems,
    )
    fetch.begin()
    before = lax.broadcasted_iota(jnp.int32, (BLK, BLK), 0)
    after = lax.broadcasted_iota(jnp.int32, (BLK, BLK), 1)
    upper = jnp.where(before <= after, 1.0, 0.0).astype(BF16)
    stacked = jnp.concatenate(
        [decay_ref[0, :, rows(number)] for number in range(BLOCKS)], axis=0
    )
    coarse, middle, fine = (mm(part, upper) for part in split(stacked))
    cumulative = (fine + middle) + coarse
    for number in range(BLOCKS):
        total = cumulative[number * HL : (number + 1) * HL]
        cum_rows_ref[:, rows(number)] = total
        ends_ref[:, number, :] = jnp.broadcast_to(jnp.exp(total[:, BLK - 1 : BLK]), (HL, HD))
    row_ids = lax.broadcasted_iota(jnp.int32, (16, HD), 0)

    def body(head):
        terms = []
        for number in range(2):
            row = cum_rows_ref[pl.ds(head, 1), rows(number)]
            factor = jnp.exp(row[:, BLK - 1 : BLK] - row)
            turned = keys_buf[head, rows(number), :].T
            key_scaled = rounded_product(turned, factor)
            terms.append(mm(key_scaled, values_buf[head, rows(number), :]))
        term_ref[head] = terms[0]
        end_decays = ends_ref[head]
        summary = end_decays[1:2, :] * terms[0] + terms[1]
        decay = jnp.broadcast_to(end_decays[0:1, :] * end_decays[1:2, :], (16, HD))
        coarse, middle, _ = split(decay)
        packed = jnp.where(
            row_ids == 0, coarse.astype(F32), jnp.where(row_ids == 1, middle.astype(F32), 0.0)
        ).astype(BF16)
        for piece in range(PARTS):
            at = head * PARTS + piece
            send_ref[at, 0:PIECE, :] = summary[piece * PIECE : (piece + 1) * PIECE].astype(BF16)
            send_ref[at, PIECE : PIECE + 16, :] = packed

    over_heads(fetch, body, started=True, group=4)


def within_kernel(
    cum_rows_ref, queries_ref, keys_ref, values_ref,
    within_ref, scaled_keys_ref, done_ref,
    queries_buf, keys_buf, values_buf, within_buf, scaled_queries_buf, scaled_keys_buf,
    in_sems, out_sems,
):
    fetch = Copies(
        [
            (of_rows(queries_ref), of_lead(queries_buf)),
            (of_rows(keys_ref), of_lead(keys_buf)),
            (of_rows(values_ref), of_lead(values_buf)),
        ],
        in_sems,
    )
    leave = Copies(
        [
            (of_lead(within_buf), of_lead(within_ref)),
            (of_lead(scaled_queries_buf), of_lead(within_ref, first=HL)),
            (of_lead(scaled_keys_buf), of_lead(scaled_keys_ref)),
        ],
        out_sems,
    )
    done_ref[...] = jnp.zeros_like(done_ref)
    row_ids = lax.broadcasted_iota(jnp.int32, (BLK, BLK), 0)
    col_ids = lax.broadcasted_iota(jnp.int32, (BLK, BLK), 1)

    def body(head):
        for number in range(BLOCKS):
            part = rows(number)
            queries = queries_buf[head, part, :]
            keys = keys_buf[head, part, :]
            row = cum_rows_ref[pl.ds(head, 1), part]
            gaps = twice(down(row)) - row
            mask = jnp.where(row_ids >= col_ids, jnp.exp(gaps), 0.0)
            weights = (mm_nt(queries, keys) * mask).astype(BF16)
            within_buf[head, part, :] = mm(weights, values_buf[head, part, :]).astype(BF16)
            scaled_queries_buf[head, part, :] = rounded_product(queries, down(jnp.exp(row)))
            if number < 2:
                factor = down(jnp.exp(row[:, BLK - 1 : BLK] - row))
                scaled_keys_buf[head, part, :] = rounded_product(keys, factor)

    over_heads(fetch, body, leave, group=4)


def forward_scan_kernel(parents_ref, got_ref, _after, send_ref, decay_ref):
    totals = []
    for prompt in range(PROMPTS):
        carry = jnp.zeros((PIECE, HD), F32)
        for index in range(prompt * SPAN, (prompt + 1) * SPAN):
            packed = got_ref[index, PIECE : PIECE + 16, :].astype(F32)
            decay = packed[0:1, :] + packed[1:2, :]
            decay_ref[index : index + 1, :] = decay
            send_ref[index, 0:PIECE, :] = carry.astype(BF16)
            carry = decay * carry + got_ref[index, 0:PIECE, :].astype(F32)
        totals.append(carry)
    for index in range(N_SEQ):
        prompt = parents_ref[index] // SPAN
        chosen = jnp.where(prompt == 0, totals[0], totals[1])
        decay_ref[N_SEQ + index : N_SEQ + index + 1, :] = jnp.full((1, HD), prompt, F32)
        send_ref[index, PIECE : 2 * PIECE, :] = chosen.astype(BF16)


def attend_kernel(
    ends_ref, gain_ref, d_out_ref, starts_ref, term_ref, within_ref,
    queries_ref, attended_ref, stats_ref, kept_ref, states_ref,
    within_buf, states_buf, squares_ref, products_ref, in_sems, out_sems,
):
    fetch = Copies(
        [
            (of_lead(within_ref, first=HL), of_lead(queries_ref)),
            (of_lead(within_ref), of_lead(within_buf)),
        ],
        in_sems,
    )
    leave = Copies(
        [
            (of_lead(attended_ref), of_lead(kept_ref)),
            (of_lead(states_buf, BLOCKS), of_lead(states_ref, BLOCKS)),
        ],
        out_sems,
    )
    fetch.begin()
    squares_ref[...] = jnp.zeros_like(squares_ref)
    products_ref[...] = jnp.zeros_like(products_ref)

    def body(head):
        got = starts_ref[pl.ds(head * PARTS, PARTS)]
        first = got[:, 0:PIECE, :].reshape(HD, HD)
        reply = got[:, PIECE : 2 * PIECE, :].reshape(HD, HD)
        end_decay = ends_ref[head][0:1, :]
        second = (end_decay * first.astype(F32) + term_ref[head]).astype(BF16)
        gain = gain_ref[pl.ds(head, 1), :]
        for number, start in enumerate((first, second, reply)):
            part = rows(number)
            states_buf[head * BLOCKS + number] = start
            attended = within_buf[head, part, :].astype(F32) + mm(
                queries_ref[head, part, :], start
            )
            attended_ref[head, part, :] = attended.astype(BF16)
            weighted = gain * d_out_ref[0, part, lanes(head)].astype(F32)
            squares_ref[part, :] += attended * attended
            products_ref[part, :] += weighted * attended

    over_heads(fetch, body, leave, started=True)
    stats_ref[...] = jnp.zeros_like(stats_ref)
    for tile in range(TILES):
        for base, sums_ref in ((0, squares_ref), (8, products_ref)):
            row = jnp.sum(sums_ref[tile_rows(tile), :].T, axis=0, keepdims=True)
            stats_ref[:, base + tile : base + tile + 1, :] = jnp.broadcast_to(
                row[None], (HL, 1, HD)
            )


def row_factors(stats_ref, inverse_ref, slope_ref):
    total = stats_ref[0]
    for source in range(1, HL):
        total = total + stats_ref[source]
    turned = jnp.concatenate([total, jnp.zeros((HD - 16, HD), F32)], axis=0).T
    for tile in range(TILES):
        squares = turned[:, tile : tile + 1]
        products = turned[:, 8 + tile : 9 + tile]
        inverse = lax.rsqrt(squares / (H * HD) + EPS)
        slope = inverse * inverse * inverse * products / (H * HD)
        inverse_ref[tile_rows(tile), :] = jnp.broadcast_to(inverse, (HD, HD))
        slope_ref[tile_rows(tile), :] = jnp.broadcast_to(slope, (HD, HD))


def grad_kernel(
    ends_ref, gain_ref, stats_ref, queries_ref, d_out_ref, attended_ref,
    send_ref, inverse_ref, slope_ref,
):
    row_factors(stats_ref, inverse_ref, slope_ref)

    def body(head):
        gain = gain_ref[pl.ds(head, 1), :]
        terms = []
        for number in range(BLOCKS):
            part = rows(number)
            weighted = gain * d_out_ref[0, part, lanes(head)].astype(F32)
            grad = (
                inverse_ref[part, :] * weighted
                - attended_ref[head, part, :].astype(F32) * slope_ref[part, :]
            ).astype(BF16)
            terms.append(mm_tn(queries_ref[head, part, :], grad))
        local_sum = ends_ref[head][0:1, :] * terms[1] + terms[0]
        for piece in range(PARTS):
            at = head * PARTS + piece
            part = slice(piece * PIECE, (piece + 1) * PIECE)
            send_ref[at, 0:PIECE, :] = local_sum[part].astype(BF16)
            send_ref[at, PIECE : 2 * PIECE, :] = terms[2][part].astype(BF16)

    over_heads(None, body, group=HL)


def backward_scan_kernel(got_ref, decay_ref, _after, send_ref):
    branches = [jnp.zeros((PIECE, HD), F32) for _ in range(PROMPTS)]
    for index in range(N_SEQ):
        prompt = decay_ref[N_SEQ + index : N_SEQ + index + 1, :]
        start_grad = got_ref[index, PIECE : 2 * PIECE, :].astype(F32)
        for each in range(PROMPTS):
            branches[each] = branches[each] + jnp.where(prompt == each, start_grad, 0.0)
    for prompt in range(PROMPTS):
        carry = branches[prompt]
        for index in reversed(range(prompt * SPAN, (prompt + 1) * SPAN)):
            send_ref[index] = carry.astype(BF16)
            carry = decay_ref[index : index + 1, :] * carry + got_ref[index, 0:PIECE, :].astype(F32)


def local_grads_kernel(
    cum_rows_ref, stats_ref, gain_ref,
    queries_ref, keys_ref, values_ref, d_out_ref, attended_ref, states_ref,
    out_ref, d_queries_ref, d_keys_ref, d_values_ref, term_ref, done_ref,
    queries_buf, keys_buf, values_buf, d_out_buf, attended_buf, states_buf,
    out_buf, d_queries_buf, d_keys_buf, d_values_buf, term_buf,
    inverse_ref, slope_ref, in_sems, out_sems,
):
    fetch = Copies(
        [
            (of_rows(d_out_ref), of_lead(d_out_buf)),
            (of_lead(attended_ref), of_lead(attended_buf)),
            (of_rows(queries_ref), of_lead(queries_buf)),
            (of_rows(keys_ref), of_lead(keys_buf)),
            (of_rows(values_ref), of_lead(values_buf)),
            (of_lead(states_ref, BLOCKS), of_lead(states_buf, BLOCKS)),
        ],
        in_sems,
    )
    leave = Copies(
        [
            (of_lead(out_buf), of_rows(out_ref)),
            (of_lead(d_queries_buf), of_rows(d_queries_ref)),
            (of_lead(d_keys_buf), of_rows(d_keys_ref)),
            (of_lead(d_values_buf), of_rows(d_values_ref)),
            (of_lead(term_buf), of_lead(term_ref)),
        ],
        out_sems,
    )
    fetch.begin()
    done_ref[...] = jnp.zeros_like(done_ref)
    row_factors(stats_ref, inverse_ref, slope_ref)
    row_ids = lax.broadcasted_iota(jnp.int32, (BLK, BLK), 0)
    col_ids = lax.broadcasted_iota(jnp.int32, (BLK, BLK), 1)

    def body(head):
        gain = gain_ref[pl.ds(head, 1), :]
        for number in range(BLOCKS):
            part = rows(number)
            queries = queries_buf[head, part, :]
            keys = keys_buf[head, part, :]
            values = values_buf[head, part, :]
            attended = attended_buf[head, part, :].astype(F32)
            inverse = inverse_ref[part, :]
            weighted = gain * d_out_buf[head, part, :].astype(F32)
            grad = (inverse * weighted - attended * slope_ref[part, :]).astype(BF16)
            out_buf[head, part, :] = (attended * inverse * gain).astype(BF16)
            row = cum_rows_ref[pl.ds(head, 1), part]
            gaps = row - twice(down(row))
            mask = jnp.where(col_ids >= row_ids, jnp.exp(gaps), 0.0)
            weights = (mm_nt(keys, queries) * mask).astype(BF16)
            score_grad = (mm_nt(values, grad) * mask).astype(BF16)
            growth = down(jnp.exp(row))
            start = states_buf[head * BLOCKS + number]
            grad_queries = mm_tn(score_grad, keys) + growth * mm_nt(grad, start)
            d_queries_buf[head, part, :] = grad_queries.astype(BF16)
            if number == 1:
                term_buf[head] = mm_tn(rounded_product(queries, growth), grad)
            d_keys_buf[head, part, :] = mm(score_grad, queries).astype(BF16)
            d_values_buf[head, part, :] = mm(weights, grad).astype(BF16)

    over_heads(fetch, body, leave, started=True)


def far_grads_kernel(
    cum_rows_ref, ends_ref, far_ref, scaled_keys_ref, values_ref, term_ref,
    near_keys_ref, near_values_ref, d_keys_ref, d_values_ref,
    term_buf, near_keys_buf, near_values_buf, d_keys_buf, d_values_buf, in_sems, out_sems,
):
    fetch = Copies(
        [
            (of_lead(term_ref), of_lead(term_buf)),
            (of_rows(near_keys_ref, P_DEV), of_lead(near_keys_buf)),
            (of_rows(near_values_ref, P_DEV), of_lead(near_values_buf)),
        ],
        in_sems,
    )
    leave = Copies(
        [
            (of_lead(d_keys_buf), of_rows(d_keys_ref, P_DEV)),
            (of_lead(d_values_buf), of_rows(d_values_ref, P_DEV)),
        ],
        out_sems,
    )

    def body(head):
        second = far_ref[pl.ds(head * PARTS, PARTS)].reshape(HD, HD)
        first = (ends_ref[head][1:2, :] * second.astype(F32) + term_buf[head]).astype(BF16)
        for number, end_grad in enumerate((first, second)):
            part = rows(number)
            row = cum_rows_ref[pl.ds(head, 1), part]
            factor = down(jnp.exp(row[:, BLK - 1 : BLK] - row))
            grad_values = near_values_buf[head, part, :].astype(F32) + mm(
                scaled_keys_ref[head, part, :], end_grad
            )
            grad_keys = near_keys_buf[head, part, :].astype(F32) + factor * mm_nt(
                values_ref[0, part, lanes(head)], end_grad
            )
            d_values_buf[head, part, :] = grad_values.astype(BF16)
            d_keys_buf[head, part, :] = grad_keys.astype(BF16)

    over_heads(fetch, body, leave)


def shape(dims, kind):
    return jax.ShapeDtypeStruct(dims, kind)


HBM = pl.BlockSpec(memory_space=pltpu.HBM)
SMEM = pl.BlockSpec(memory_space=pltpu.SMEM)
VMEM = pl.BlockSpec(memory_space=pltpu.VMEM)
WIDE = shape((1, ROWS, COLS), BF16)
HEAD_ROWS = (HL, ROWS, HD)
HEAD_PROMPT = (HL, P_DEV, HD)
HEAD_REPLY = (HL, BLK, HD)
STATE = (HL, HD, HD)
PIECES = (N_SEQ, PIECE, HD)
TWO_PIECES = (N_SEQ, 2 * PIECE, HD)
SENT_PIECES = (N_SEQ, PIECE + 16, HD)
CUM = (ROWS, HD)
FAR = 160


def call(kernel, name, in_specs, outs, scratch, semaphores, mib, flops, moved, aliases=None):
    return pl.pallas_call(
        kernel,
        in_specs=in_specs,
        out_specs=[spec for spec, _ in outs],
        out_shape=[made for _, made in outs],
        scratch_shapes=[pltpu.VMEM(dims, kind) for dims, kind in scratch]
        + [pltpu.SemaphoreType.DMA((count, HL)) for count in semaphores],
        input_output_aliases=aliases or {},
        compiler_params=pltpu.CompilerParams(vmem_limit_bytes=mib << 20),
        cost_estimate=pl.CostEstimate(
            flops=int(flops), bytes_accessed=int(moved) << 20, transcendentals=0
        ),
        name=name,
    )


def summarize(decay_rows, keys, values):
    return call(
        summary_kernel, "summary", [VMEM, HBM, HBM],
        [
            (VMEM, shape(SENT_PIECES, BF16)), (VMEM, shape(STATE, F32)),
            (VMEM, shape((HL, ROWS), F32)), (VMEM, shape((HL, 8, HD), F32)),
        ],
        [(HEAD_PROMPT, BF16), (HEAD_PROMPT, BF16)], [2], 52, 3e8, 4,
    )(decay_rows, keys, values)


def inside(cum_rows, queries, keys, values):
    return call(
        within_kernel, "within", [VMEM] + [HBM] * 3,
        [
            (HBM, shape((FAR, ROWS, HD), BF16)), (HBM, shape(HEAD_PROMPT, BF16)),
            (VMEM, shape((8, HD), F32)),
        ],
        [(HEAD_ROWS, BF16)] * 5 + [(HEAD_PROMPT, BF16)], [3, 3], 52, 4e9, 16,
    )(cum_rows, queries, keys, values)


def forward_scan(parents, got, after):
    return call(
        forward_scan_kernel, "forward_scan", [SMEM, VMEM, HBM],
        [(VMEM, shape(TWO_PIECES, BF16)), (VMEM, shape((2 * N_SEQ, HD), F32))],
        [], [], 12, 1e6, 1,
    )(parents, got, after)


def attend(ends, gains, d_out, starts, term, within):
    return call(
        attend_kernel, "attend", [VMEM] * 5 + [HBM],
        [
            (VMEM, shape(HEAD_ROWS, BF16)), (VMEM, shape(HEAD_ROWS, BF16)),
            (VMEM, shape((HL, 16, HD), F32)), (HBM, shape((FAR, ROWS, HD), BF16)),
            (HBM, shape((6 * FAR, HD, HD), BF16)),
        ],
        [(HEAD_ROWS, BF16), ((HL * BLOCKS, HD, HD), BF16), (CUM, F32), (CUM, F32)],
        [2, 2], 36, 3e8, 10,
    )(ends, gains, d_out, starts, term, within)


def grads(ends, gains, stats, scaled_queries, d_out, attended):
    return call(
        grad_kernel, "grad", [VMEM] * 6, [(VMEM, shape(TWO_PIECES, BF16))],
        [(CUM, F32), (CUM, F32)], [], 20, 3e8, 10,
    )(ends, gains, stats, scaled_queries, d_out, attended)[0]


def local_grads(cum_rows, stats, gains, queries, keys, values, d_out, attended, states):
    return call(
        local_grads_kernel, "local_grads", [VMEM] * 3 + [HBM] * 6,
        [
            (HBM, WIDE), (HBM, WIDE), (HBM, WIDE), (HBM, WIDE),
            (HBM, shape((4 * FAR, HD, HD), F32)), (VMEM, shape((8, HD), F32)),
        ],
        [(HEAD_ROWS, BF16)] * 5 + [((HL * BLOCKS, HD, HD), BF16)] + [(HEAD_ROWS, BF16)] * 4
        + [(STATE, F32), (CUM, F32), (CUM, F32)],
        [6, 5], 53, 6e9, 24,
    )(cum_rows, stats, gains, queries, keys, values, d_out, attended, states)


def far_grads(cum_rows, ends, far, scaled_keys, values, term, near_keys, near_values):
    return call(
        far_grads_kernel, "far_grads", [VMEM] * 5 + [HBM] * 3,
        [(HBM, WIDE), (HBM, WIDE)],
        [(STATE, F32)] + [(HEAD_PROMPT, BF16)] * 4, [3, 2], 36, 3e8, 10, {6: 0, 7: 1},
    )(cum_rows, ends, far, scaled_keys, values, term, near_keys, near_values)


def backward_scan(got, decays, after):
    return call(
        backward_scan_kernel, "backward_scan", [VMEM, VMEM, HBM],
        [(VMEM, shape(PIECES, BF16))], [], [], 12, 1e6, 1,
    )(got, decays, after)[0]


def everyone(array, axis):
    return lax.all_to_all(array, axis, 0, 0, tiled=True)


def local(queries, keys, values, log_decay, gain, parents, d_out):
    gains = gain.reshape(HL, HD)
    decay_rows = jnp.swapaxes(log_decay, 1, 2)
    send, first_term, cum_rows, block_ends = summarize(decay_rows, keys, values)
    got = everyone(send, "seq")
    within, scaled_keys, done = inside(cum_rows, queries, keys, values)
    send, decays = forward_scan(parents, got, done)
    starts = everyone(send, "seq")
    near_queries, attended, stats, kept, states = attend(
        block_ends, gains, d_out, starts, first_term, within
    )
    stats = everyone(stats, "head")
    send = grads(block_ends, gains, stats, near_queries, d_out, attended)
    got = everyone(send, "seq")
    out, d_queries, d_keys, d_values, last_term, done = local_grads(
        cum_rows, stats, gains, queries, keys, values, d_out, kept, states
    )
    far = everyone(backward_scan(got, decays, done), "seq")
    d_keys, d_values = far_grads(
        cum_rows, block_ends, far, scaled_keys, values, last_term, d_keys, d_values
    )
    return (out, d_queries, d_keys, d_values)


def solution(mesh):
    cut = P("seq", None, "head")
    return jax.shard_map(
        local,
        mesh=mesh,
        in_specs=(cut, cut, cut, cut, P("head"), P(), cut),
        out_specs=(cut, cut, cut, cut),
        check_vma=False,
    )
```

```python
import jax
import jax.numpy as jnp
from jax import lax
from jax.experimental import pallas as pl
from jax.experimental.pallas import tpu as pltpu
from jax.sharding import PartitionSpec as P

H = 64
HD = 128
BLK = 256
PROMPTS = 2
P_DEV = 512
ROWS = 768
HL = 8
N_SEQ = 32
SPAN = N_SEQ // PROMPTS
COLS = HL * HD
PIECE = HL * HD // N_SEQ
PARTS = HD // PIECE
PACK = 16
BLOCKS = ROWS // BLK
TILES = ROWS // HD
EPS = 1e-05
GROUP = 2

F32 = jnp.float32
BF16 = jnp.bfloat16


def dot(a, b, dims):
    return lax.dot_general(a, b, (dims, ((), ())), preferred_element_type=F32)


def mm(a, b):
    return dot(a, b, ((1,), (0,)))


def mm_nt(a, b):
    return dot(a, b, ((1,), (1,)))


def mm_tn(a, b):
    return dot(a, b, ((0,), (0,)))


def rows(number):
    return slice(number * BLK, (number + 1) * BLK)


def tile_rows(tile):
    return slice(tile * HD, (tile + 1) * HD)


def down(row):
    return jnp.broadcast_to(row, (HD, BLK)).T


def twice(block):
    return jnp.concatenate([block, block], axis=1)


def rounded_product(block, factor):
    return (block.astype(F32) * factor).astype(BF16)


def lanes(head):
    return pl.ds(pl.multiple_of(head * HD, HD), HD)


def of_rows(ref, count=ROWS, first=0):
    if len(ref.shape) == 3:
        return lambda head: ref.at[0, pl.ds(first, count), lanes(head)]
    return lambda head: ref.at[pl.ds(first, count), lanes(head)]


def of_lead(ref, count=1, first=0):
    if count == 1:
        return lambda head: ref.at[head + first]
    return lambda head: ref.at[pl.ds(head * count, count)]


class Copies:
    def __init__(self, pairs, sems):
        self.pairs, self.sems = pairs, sems

    def each(self, head):
        return [
            pltpu.make_async_copy(src(head), dst(head), self.sems.at[number, head])
            for number, (src, dst) in enumerate(self.pairs)
        ]

    def start(self, head):
        for copy in self.each(head):
            copy.start()

    def begin(self):
        for head in range(HL):
            self.start(head)

    def wait(self, head):
        for copy in self.each(head):
            copy.wait()


def over_heads(fetch, body, leave=None, started=False, group=GROUP):
    if fetch is not None and not started:
        fetch.begin()

    def step(number, carry):
        heads = [number * group + place for place in range(group)]
        for head in heads:
            if fetch is not None:
                fetch.wait(head)
        for head in heads:
            body(head)
        for head in heads:
            if leave is not None:
                leave.start(head)
        return carry

    lax.fori_loop(0, HL // group, step, 0)
    if leave is not None:
        for head in range(HL):
            leave.wait(head)


def split(value):
    coarse = value.astype(BF16)
    rest = value - coarse.astype(F32)
    middle = rest.astype(BF16)
    return coarse, middle, (rest - middle.astype(F32)).astype(BF16)


def summary_kernel(
    decay_ref, keys_ref, values_ref,
    send_ref, term_ref, cum_rows_ref, ends_ref,
    keys_buf, values_buf, decay_buf, send_buf, in_sems, out_sems, decay_sem,
):
    fetch = Copies(
        [
            (of_rows(keys_ref, P_DEV), of_lead(keys_buf)),
            (of_rows(values_ref, P_DEV), of_lead(values_buf)),
        ],
        in_sems,
    )
    leave = Copies([(of_lead(send_buf, PARTS), of_lead(send_ref, PARTS))], out_sems)
    decay_copy = pltpu.make_async_copy(decay_ref, decay_buf, decay_sem.at[0, 0])
    decay_copy.start()
    fetch.begin()
    before = lax.broadcasted_iota(jnp.int32, (BLK, BLK), 0)
    after = lax.broadcasted_iota(jnp.int32, (BLK, BLK), 1)
    upper = jnp.where(before <= after, 1.0, 0.0).astype(BF16)
    decay_copy.wait()
    stacked = jnp.concatenate(
        [decay_buf[0, :, rows(number)] for number in range(BLOCKS)], axis=0
    )
    coarse, middle, fine = (mm(part, upper) for part in split(stacked))
    cumulative = (fine + middle) + coarse
    for number in range(BLOCKS):
        total = cumulative[number * HL : (number + 1) * HL]
        cum_rows_ref[:, rows(number)] = total
        ends_ref[:, number, :] = jnp.broadcast_to(jnp.exp(total[:, BLK - 1 : BLK]), (HL, HD))
    row_ids = lax.broadcasted_iota(jnp.int32, (PACK, HD), 0)

    def body(head):
        terms = []
        for number in range(2):
            row = cum_rows_ref[pl.ds(head, 1), rows(number)]
            factor = jnp.exp(row[:, BLK - 1 : BLK] - row)
            turned = keys_buf[head, rows(number), :].T
            key_scaled = rounded_product(turned, factor)
            terms.append(mm(key_scaled, values_buf[head, rows(number), :]))
        term_ref[head] = terms[0]
        end_decays = ends_ref[head]
        summary = end_decays[1:2, :] * terms[0] + terms[1]
        decay = jnp.broadcast_to(end_decays[0:1, :] * end_decays[1:2, :], (PACK, HD))
        coarse, middle, _ = split(decay)
        packed = jnp.where(
            row_ids == 0, coarse.astype(F32), jnp.where(row_ids == 1, middle.astype(F32), 0.0)
        ).astype(BF16)
        for piece in range(PARTS):
            at = head * PARTS + piece
            send_buf[at, 0:PIECE, :] = summary[piece * PIECE : (piece + 1) * PIECE].astype(BF16)
            send_buf[at, PIECE : PIECE + PACK, :] = packed

    over_heads(fetch, body, leave, started=True, group=4)


def within_kernel(
    cum_rows_ref, queries_ref, keys_ref, values_ref,
    within_ref, scaled_keys_ref, weights_ref, done_ref,
    queries_buf, keys_buf, values_buf, within_buf, scaled_queries_buf, scaled_keys_buf,
    weights_buf, in_sems, out_sems,
):
    fetch = Copies(
        [
            (of_rows(queries_ref), of_lead(queries_buf)),
            (of_rows(keys_ref), of_lead(keys_buf)),
            (of_rows(values_ref), of_lead(values_buf)),
        ],
        in_sems,
    )
    leave = Copies(
        [
            (of_lead(within_buf), of_lead(within_ref)),
            (of_lead(scaled_queries_buf), of_lead(within_ref, first=HL)),
            (of_lead(scaled_keys_buf), of_lead(scaled_keys_ref)),
            (of_lead(weights_buf), of_lead(weights_ref)),
        ],
        out_sems,
    )
    done_ref[...] = jnp.zeros_like(done_ref)
    row_ids = lax.broadcasted_iota(jnp.int32, (BLK, BLK), 0)
    col_ids = lax.broadcasted_iota(jnp.int32, (BLK, BLK), 1)

    def body(head):
        for number in range(BLOCKS):
            part = rows(number)
            queries = queries_buf[head, part, :]
            keys = keys_buf[head, part, :]
            row = cum_rows_ref[pl.ds(head, 1), part]
            gaps = row - twice(down(row))
            mask = jnp.where(col_ids >= row_ids, jnp.exp(gaps), 0.0)
            weights = (mm_nt(keys, queries) * mask).astype(BF16)
            weights_buf[head, part, :] = weights
            within_buf[head, part, :] = mm_tn(weights, values_buf[head, part, :]).astype(BF16)
            scaled_queries_buf[head, part, :] = rounded_product(queries, down(jnp.exp(row)))
            if number < 2:
                factor = down(jnp.exp(row[:, BLK - 1 : BLK] - row))
                scaled_keys_buf[head, part, :] = rounded_product(keys, factor)

    over_heads(fetch, body, leave, group=4)


def forward_scan_kernel(parents_ref, got_ref, _after, send_ref, decay_ref):
    totals = []
    for prompt in range(PROMPTS):
        carry = jnp.zeros((PIECE, HD), F32)
        for index in range(prompt * SPAN, (prompt + 1) * SPAN):
            packed = got_ref[index, PIECE : PIECE + PACK, :].astype(F32)
            decay = packed[0:1, :] + packed[1:2, :]
            decay_ref[index : index + 1, :] = decay
            send_ref[index, 0:PIECE, :] = carry.astype(BF16)
            carry = decay * carry + got_ref[index, 0:PIECE, :].astype(F32)
        totals.append(carry)
    for index in range(N_SEQ):
        prompt = parents_ref[index] // SPAN
        chosen = jnp.where(prompt == 0, totals[0], totals[1])
        decay_ref[N_SEQ + index : N_SEQ + index + 1, :] = jnp.full((1, HD), prompt, F32)
        send_ref[index, PIECE : 2 * PIECE, :] = chosen.astype(BF16)


def attend_kernel(
    ends_ref, gain_ref, d_out_ref, starts_ref, term_ref, within_ref,
    queries_ref, attended_ref, stats_ref, kept_ref, states_ref,
    within_buf, states_buf, squares_ref, products_ref, in_sems, out_sems,
):
    fetch = Copies(
        [
            (of_lead(within_ref, first=HL), of_lead(queries_ref)),
            (of_lead(within_ref), of_lead(within_buf)),
        ],
        in_sems,
    )
    leave = Copies(
        [
            (of_lead(attended_ref), of_lead(kept_ref)),
            (of_lead(states_buf, BLOCKS), of_lead(states_ref, BLOCKS)),
        ],
        out_sems,
    )
    fetch.begin()
    squares_ref[...] = jnp.zeros_like(squares_ref)
    products_ref[...] = jnp.zeros_like(products_ref)

    def body(head):
        got = starts_ref[pl.ds(head * PARTS, PARTS)]
        first = got[:, 0:PIECE, :].reshape(HD, HD)
        reply = got[:, PIECE : 2 * PIECE, :].reshape(HD, HD)
        end_decay = ends_ref[head][0:1, :]
        second = (end_decay * first.astype(F32) + term_ref[head]).astype(BF16)
        gain = gain_ref[pl.ds(head, 1), :]
        for number, start in enumerate((first, second, reply)):
            part = rows(number)
            states_buf[head * BLOCKS + number] = start
            attended = within_buf[head, part, :].astype(F32) + mm(
                queries_ref[head, part, :], start
            )
            attended_ref[head, part, :] = attended.astype(BF16)
            weighted = gain * d_out_ref[0, part, lanes(head)].astype(F32)
            squares_ref[part, :] += attended * attended
            products_ref[part, :] += weighted * attended

    over_heads(fetch, body, leave, started=True)
    stats_ref[...] = jnp.zeros_like(stats_ref)
    for tile in range(TILES):
        for base, sums_ref in ((0, squares_ref), (8, products_ref)):
            row = jnp.sum(sums_ref[tile_rows(tile), :].T, axis=0, keepdims=True)
            stats_ref[:, base + tile : base + tile + 1, :] = jnp.broadcast_to(
                row[None], (HL, 1, HD)
            )


def row_factors(stats_ref, inverse_ref, slope_ref):
    total = stats_ref[0]
    for source in range(1, HL):
        total = total + stats_ref[source]
    turned = jnp.concatenate([total, jnp.zeros((HD - 16, HD), F32)], axis=0).T
    for tile in range(TILES):
        squares = turned[:, tile : tile + 1]
        products = turned[:, 8 + tile : 9 + tile]
        inverse = lax.rsqrt(squares / (H * HD) + EPS)
        slope = inverse * inverse * inverse * products / (H * HD)
        inverse_ref[tile_rows(tile), :] = jnp.broadcast_to(inverse, (HD, HD))
        slope_ref[tile_rows(tile), :] = jnp.broadcast_to(slope, (HD, HD))


def grad_kernel(
    ends_ref, gain_ref, stats_ref, queries_ref, d_out_ref, attended_ref,
    send_ref, inverse_ref, slope_ref,
):
    row_factors(stats_ref, inverse_ref, slope_ref)

    def body(head):
        gain = gain_ref[pl.ds(head, 1), :]
        terms = []
        for number in range(BLOCKS):
            part = rows(number)
            weighted = gain * d_out_ref[0, part, lanes(head)].astype(F32)
            grad = (
                inverse_ref[part, :] * weighted
                - attended_ref[head, part, :].astype(F32) * slope_ref[part, :]
            ).astype(BF16)
            terms.append(mm_tn(queries_ref[head, part, :], grad))
        local_sum = ends_ref[head][0:1, :] * terms[1] + terms[0]
        for piece in range(PARTS):
            at = head * PARTS + piece
            part = slice(piece * PIECE, (piece + 1) * PIECE)
            send_ref[at, 0:PIECE, :] = local_sum[part].astype(BF16)
            send_ref[at, PIECE : 2 * PIECE, :] = terms[2][part].astype(BF16)

    over_heads(None, body, group=HL)


def backward_scan_kernel(got_ref, decay_ref, _after, send_ref):
    branches = [jnp.zeros((PIECE, HD), F32) for _ in range(PROMPTS)]
    for index in range(N_SEQ):
        prompt = decay_ref[N_SEQ + index : N_SEQ + index + 1, :]
        start_grad = got_ref[index, PIECE : 2 * PIECE, :].astype(F32)
        for each in range(PROMPTS):
            branches[each] = branches[each] + jnp.where(prompt == each, start_grad, 0.0)
    for prompt in range(PROMPTS):
        carry = branches[prompt]
        for index in reversed(range(prompt * SPAN, (prompt + 1) * SPAN)):
            send_ref[index] = carry.astype(BF16)
            carry = decay_ref[index : index + 1, :] * carry + got_ref[index, 0:PIECE, :].astype(F32)


def local_grads_kernel(
    cum_rows_ref, stats_ref, gain_ref,
    queries_ref, keys_ref, values_ref, d_out_ref, attended_ref, states_ref, weights_ref,
    out_ref, d_queries_ref, d_keys_ref, d_values_ref, term_ref, done_ref,
    queries_buf, keys_buf, values_buf, d_out_buf, attended_buf, states_buf, weights_buf,
    out_buf, d_queries_buf, d_keys_buf, d_values_buf, term_buf,
    inverse_ref, slope_ref, in_sems, out_sems,
):
    fetch = Copies(
        [
            (of_rows(d_out_ref), of_lead(d_out_buf)),
            (of_lead(attended_ref), of_lead(attended_buf)),
            (of_rows(queries_ref), of_lead(queries_buf)),
            (of_rows(keys_ref), of_lead(keys_buf)),
            (of_rows(values_ref), of_lead(values_buf)),
            (of_lead(states_ref, BLOCKS), of_lead(states_buf, BLOCKS)),
            (of_lead(weights_ref), of_lead(weights_buf)),
        ],
        in_sems,
    )
    leave = Copies(
        [
            (of_lead(out_buf), of_rows(out_ref)),
            (of_lead(d_queries_buf), of_rows(d_queries_ref)),
            (of_lead(d_keys_buf), of_rows(d_keys_ref)),
            (of_lead(d_values_buf), of_rows(d_values_ref)),
            (of_lead(term_buf), of_lead(term_ref)),
        ],
        out_sems,
    )
    fetch.begin()
    done_ref[...] = jnp.zeros_like(done_ref)
    row_factors(stats_ref, inverse_ref, slope_ref)
    row_ids = lax.broadcasted_iota(jnp.int32, (BLK, BLK), 0)
    col_ids = lax.broadcasted_iota(jnp.int32, (BLK, BLK), 1)

    def body(head):
        gain = gain_ref[pl.ds(head, 1), :]
        for number in range(BLOCKS):
            part = rows(number)
            queries = queries_buf[head, part, :]
            keys = keys_buf[head, part, :]
            values = values_buf[head, part, :]
            attended = attended_buf[head, part, :].astype(F32)
            inverse = inverse_ref[part, :]
            weighted = gain * d_out_buf[head, part, :].astype(F32)
            grad = (inverse * weighted - attended * slope_ref[part, :]).astype(BF16)
            out_buf[head, part, :] = (attended * inverse * gain).astype(BF16)
            row = cum_rows_ref[pl.ds(head, 1), part]
            gaps = row - twice(down(row))
            mask = jnp.where(col_ids >= row_ids, jnp.exp(gaps), 0.0)
            weights = weights_buf[head, part, :]
            score_grad = (mm_nt(values, grad) * mask).astype(BF16)
            growth = down(jnp.exp(row))
            start = states_buf[head * BLOCKS + number]
            grad_queries = mm_tn(score_grad, keys) + growth * mm_nt(grad, start)
            d_queries_buf[head, part, :] = grad_queries.astype(BF16)
            if number == 1:
                term_buf[head] = mm_tn(rounded_product(queries, growth), grad)
            d_keys_buf[head, part, :] = mm(score_grad, queries).astype(BF16)
            d_values_buf[head, part, :] = mm(weights, grad).astype(BF16)

    over_heads(fetch, body, leave, started=True)


def far_grads_kernel(
    cum_rows_ref, ends_ref, far_ref, scaled_keys_ref, values_ref, term_ref,
    near_keys_ref, near_values_ref, d_keys_ref, d_values_ref,
    term_buf, near_keys_buf, near_values_buf, d_keys_buf, d_values_buf, in_sems, out_sems,
):
    fetch = Copies(
        [
            (of_lead(term_ref), of_lead(term_buf)),
            (of_rows(near_keys_ref, P_DEV), of_lead(near_keys_buf)),
            (of_rows(near_values_ref, P_DEV), of_lead(near_values_buf)),
        ],
        in_sems,
    )
    leave = Copies(
        [
            (of_lead(d_keys_buf), of_rows(d_keys_ref, P_DEV)),
            (of_lead(d_values_buf), of_rows(d_values_ref, P_DEV)),
        ],
        out_sems,
    )

    def body(head):
        second = far_ref[pl.ds(head * PARTS, PARTS)].reshape(HD, HD)
        first = (ends_ref[head][1:2, :] * second.astype(F32) + term_buf[head]).astype(BF16)
        for number, end_grad in enumerate((first, second)):
            part = rows(number)
            row = cum_rows_ref[pl.ds(head, 1), part]
            factor = down(jnp.exp(row[:, BLK - 1 : BLK] - row))
            grad_values = near_values_buf[head, part, :].astype(F32) + mm(
                scaled_keys_ref[head, part, :], end_grad
            )
            grad_keys = near_keys_buf[head, part, :].astype(F32) + factor * mm_nt(
                values_ref[0, part, lanes(head)], end_grad
            )
            d_values_buf[head, part, :] = grad_values.astype(BF16)
            d_keys_buf[head, part, :] = grad_keys.astype(BF16)

    over_heads(fetch, body, leave)


def shape(dims, kind):
    return jax.ShapeDtypeStruct(dims, kind)


HBM = pl.BlockSpec(memory_space=pltpu.HBM)
SMEM = pl.BlockSpec(memory_space=pltpu.SMEM)
VMEM = pl.BlockSpec(memory_space=pltpu.VMEM)
WIDE = shape((1, ROWS, COLS), BF16)
HEAD_ROWS = (HL, ROWS, HD)
HEAD_PROMPT = (HL, P_DEV, HD)
HEAD_REPLY = (HL, BLK, HD)
STATE = (HL, HD, HD)
PIECES = (N_SEQ, PIECE, HD)
TWO_PIECES = (N_SEQ, 2 * PIECE, HD)
SENT_PIECES = (N_SEQ, PIECE + PACK, HD)
CUM = (ROWS, HD)
FAR = 100


def call(kernel, name, in_specs, outs, scratch, semaphores, mib, flops, moved, aliases=None):
    return pl.pallas_call(
        kernel,
        in_specs=in_specs,
        out_specs=[spec for spec, _ in outs],
        out_shape=[made for _, made in outs],
        scratch_shapes=[pltpu.VMEM(dims, kind) for dims, kind in scratch]
        + [pltpu.SemaphoreType.DMA((count, HL)) for count in semaphores],
        input_output_aliases=aliases or {},
        compiler_params=pltpu.CompilerParams(vmem_limit_bytes=mib << 20),
        cost_estimate=pl.CostEstimate(
            flops=int(flops), bytes_accessed=int(moved) << 20, transcendentals=0
        ),
        name=name,
    )


def summarize(decay_rows, keys, values):
    return call(
        summary_kernel, "summary", [HBM, HBM, HBM],
        [
            (HBM, shape(SENT_PIECES, BF16)), (VMEM, shape(STATE, F32)),
            (VMEM, shape((HL, ROWS), F32)), (VMEM, shape((HL, 8, HD), F32)),
        ],
        [(HEAD_PROMPT, BF16), (HEAD_PROMPT, BF16), ((1, HL, ROWS), F32), (SENT_PIECES, BF16)],
        [2, 1, 1], 52, 3e8, 4,
    )(decay_rows, keys, values)


def inside(cum_rows, queries, keys, values):
    return call(
        within_kernel, "within", [VMEM] + [HBM] * 3,
        [
            (HBM, shape((FAR, ROWS, HD), BF16)), (HBM, shape(HEAD_PROMPT, BF16)),
            (HBM, shape((FAR // 2, ROWS, BLK), BF16)), (VMEM, shape((8, HD), F32)),
        ],
        [(HEAD_ROWS, BF16)] * 5 + [(HEAD_PROMPT, BF16), ((HL, ROWS, BLK), BF16)],
        [3, 4], 52, 4e9, 16,
    )(cum_rows, queries, keys, values)


def forward_scan(parents, got, after):
    return call(
        forward_scan_kernel, "forward_scan", [SMEM, VMEM, HBM],
        [(VMEM, shape(TWO_PIECES, BF16)), (VMEM, shape((2 * N_SEQ, HD), F32))],
        [], [], 12, 1e6, 1,
    )(parents, got, after)


def attend(ends, gains, d_out, starts, term, within):
    return call(
        attend_kernel, "attend", [VMEM] * 5 + [HBM],
        [
            (VMEM, shape(HEAD_ROWS, BF16)), (VMEM, shape(HEAD_ROWS, BF16)),
            (VMEM, shape((HL, 16, HD), F32)), (HBM, shape((FAR, ROWS, HD), BF16)),
            (HBM, shape((6 * FAR, HD, HD), BF16)),
        ],
        [(HEAD_ROWS, BF16), ((HL * BLOCKS, HD, HD), BF16), (CUM, F32), (CUM, F32)],
        [2, 2], 46, 3e8, 10,
    )(ends, gains, d_out, starts, term, within)


def grads(ends, gains, stats, scaled_queries, d_out, attended):
    return call(
        grad_kernel, "grad", [VMEM] * 6, [(VMEM, shape(TWO_PIECES, BF16))],
        [(CUM, F32), (CUM, F32)], [], 20, 3e8, 10,
    )(ends, gains, stats, scaled_queries, d_out, attended)[0]


def local_grads(
    cum_rows, stats, gains, queries, keys, values, d_out, attended, states, weights
):
    return call(
        local_grads_kernel, "local_grads", [VMEM] * 3 + [HBM] * 7,
        [
            (HBM, WIDE), (HBM, WIDE), (HBM, WIDE), (HBM, WIDE),
            (HBM, shape((4 * FAR, HD, HD), F32)), (VMEM, shape((8, HD), F32)),
        ],
        [(HEAD_ROWS, BF16)] * 5 + [((HL * BLOCKS, HD, HD), BF16), ((HL, ROWS, BLK), BF16)]
        + [(HEAD_ROWS, BF16)] * 4
        + [(STATE, F32), (CUM, F32), (CUM, F32)],
        [7, 5], 53, 6e9, 24,
    )(cum_rows, stats, gains, queries, keys, values, d_out, attended, states, weights)


def far_grads(cum_rows, ends, far, scaled_keys, values, term, near_keys, near_values):
    return call(
        far_grads_kernel, "far_grads", [VMEM] * 5 + [HBM] * 3,
        [(HBM, WIDE), (HBM, WIDE)],
        [(STATE, F32)] + [(HEAD_PROMPT, BF16)] * 4, [3, 2], 44, 3e8, 10, {6: 0, 7: 1},
    )(cum_rows, ends, far, scaled_keys, values, term, near_keys, near_values)


def backward_scan(got, decays, after):
    return call(
        backward_scan_kernel, "backward_scan", [VMEM, VMEM, HBM],
        [(VMEM, shape(PIECES, BF16))], [], [], 12, 1e6, 1,
    )(got, decays, after)[0]


def everyone(array, axis):
    return lax.all_to_all(array, axis, 0, 0, tiled=True)


def local(queries, keys, values, log_decay, gain, parents, d_out):
    gains = gain.reshape(HL, HD)
    decay_rows = jnp.swapaxes(log_decay, 1, 2)
    send, first_term, cum_rows, block_ends = summarize(decay_rows, keys, values)
    got = everyone(send, "seq")
    within, scaled_keys, weights, done = inside(cum_rows, queries, keys, values)
    send, decays = forward_scan(parents, got, done)
    starts = everyone(send, "seq")
    near_queries, attended, stats, kept, states = attend(
        block_ends, gains, d_out, starts, first_term, within
    )
    stats = everyone(stats, "head")
    send = grads(block_ends, gains, stats, near_queries, d_out, attended)
    got = everyone(send, "seq")
    out, d_queries, d_keys, d_values, last_term, done = local_grads(
        cum_rows, stats, gains, queries, keys, values, d_out, kept, states, weights
    )
    far = everyone(backward_scan(got, decays, done), "seq")
    d_keys, d_values = far_grads(
        cum_rows, block_ends, far, scaled_keys, values, last_term, d_keys, d_values
    )
    return (out, d_queries, d_keys, d_values)


def solution(mesh):
    cut = P("seq", None, "head")
    return jax.shard_map(
        local,
        mesh=mesh,
        in_specs=(cut, cut, cut, cut, P("head"), P(), cut),
        out_specs=(cut, cut, cut, cut),
        check_vma=False,
    )
```

```python
import jax
import jax.numpy as jnp
from jax import lax
from jax.experimental import pallas as pl
from jax.experimental.pallas import tpu as pltpu
from jax.sharding import PartitionSpec as P

H = 64
HD = 128
BLK = 256
PROMPTS = 2
P_DEV = 512
ROWS = 768
HL = 8
N_SEQ = 32
SPAN = N_SEQ // PROMPTS
COLS = HL * HD
PIECE = HL * HD // N_SEQ
PARTS = HD // PIECE
PACK = 16
BLOCKS = ROWS // BLK
TILES = ROWS // HD
EPS = 1e-05
GROUP = 2

F32 = jnp.float32
BF16 = jnp.bfloat16


def dot(a, b, dims):
    return lax.dot_general(a, b, (dims, ((), ())), preferred_element_type=F32)


def mm(a, b):
    return dot(a, b, ((1,), (0,)))


def mm_nt(a, b):
    return dot(a, b, ((1,), (1,)))


def mm_tn(a, b):
    return dot(a, b, ((0,), (0,)))


def rows(number):
    return slice(number * BLK, (number + 1) * BLK)


def tile_rows(tile):
    return slice(tile * HD, (tile + 1) * HD)


def down(row):
    return jnp.broadcast_to(row, (HD, BLK)).T


def twice(block):
    return jnp.concatenate([block, block], axis=1)


def rounded_product(block, factor):
    return (block.astype(F32) * factor).astype(BF16)


def lanes(head):
    return pl.ds(pl.multiple_of(head * HD, HD), HD)


def of_rows(ref, count=ROWS, first=0):
    if len(ref.shape) == 3:
        return lambda head: ref.at[0, pl.ds(first, count), lanes(head)]
    return lambda head: ref.at[pl.ds(first, count), lanes(head)]


def of_lead(ref, count=1, first=0):
    if count == 1:
        return lambda head: ref.at[head + first]
    return lambda head: ref.at[pl.ds(head * count, count)]


class Copies:
    def __init__(self, pairs, sems):
        self.pairs, self.sems = pairs, sems

    def each(self, head):
        return [
            pltpu.make_async_copy(src(head), dst(head), self.sems.at[number, head])
            for number, (src, dst) in enumerate(self.pairs)
        ]

    def start(self, head):
        for copy in self.each(head):
            copy.start()

    def begin(self):
        for head in range(HL):
            self.start(head)

    def wait(self, head):
        for copy in self.each(head):
            copy.wait()


def over_heads(fetch, body, leave=None, started=False, group=GROUP):
    if fetch is not None and not started:
        fetch.begin()

    def step(number, carry):
        heads = [number * group + place for place in range(group)]
        for head in heads:
            if fetch is not None:
                fetch.wait(head)
        for head in heads:
            body(head)
        for head in heads:
            if leave is not None:
                leave.start(head)
        return carry

    lax.fori_loop(0, HL // group, step, 0)
    if leave is not None:
        for head in range(HL):
            leave.wait(head)


def split(value):
    coarse = value.astype(BF16)
    rest = value - coarse.astype(F32)
    middle = rest.astype(BF16)
    return coarse, middle, (rest - middle.astype(F32)).astype(BF16)


def summary_kernel(
    decay_ref, keys_ref, values_ref,
    send_ref, term_ref, cum_rows_ref, ends_ref,
    keys_buf, values_buf, decay_buf, send_buf, in_sems, out_sems, decay_sem,
):
    fetch = Copies(
        [
            (of_rows(keys_ref, P_DEV), of_lead(keys_buf)),
            (of_rows(values_ref, P_DEV), of_lead(values_buf)),
        ],
        in_sems,
    )
    leave = Copies([(of_lead(send_buf, PARTS), of_lead(send_ref, PARTS))], out_sems)
    decay_copy = pltpu.make_async_copy(decay_ref, decay_buf, decay_sem.at[0, 0])
    decay_copy.start()
    fetch.begin()
    before = lax.broadcasted_iota(jnp.int32, (BLK, BLK), 0)
    after = lax.broadcasted_iota(jnp.int32, (BLK, BLK), 1)
    upper = jnp.where(before <= after, 1.0, 0.0).astype(BF16)
    decay_copy.wait()
    stacked = jnp.concatenate(
        [decay_buf[0, :, rows(number)] for number in range(BLOCKS)], axis=0
    )
    coarse, middle, fine = (mm(part, upper) for part in split(stacked))
    cumulative = (fine + middle) + coarse
    for number in range(BLOCKS):
        total = cumulative[number * HL : (number + 1) * HL]
        cum_rows_ref[:, rows(number)] = total
        ends_ref[:, number, :] = jnp.broadcast_to(jnp.exp(total[:, BLK - 1 : BLK]), (HL, HD))
    row_ids = lax.broadcasted_iota(jnp.int32, (PACK, HD), 0)

    def body(head):
        terms = []
        for number in range(2):
            row = cum_rows_ref[pl.ds(head, 1), rows(number)]
            factor = jnp.exp(row[:, BLK - 1 : BLK] - row)
            turned = keys_buf[head, rows(number), :].T
            key_scaled = rounded_product(turned, factor)
            terms.append(mm(key_scaled, values_buf[head, rows(number), :]))
        term_ref[head] = terms[0]
        end_decays = ends_ref[head]
        summary = end_decays[1:2, :] * terms[0] + terms[1]
        decay = jnp.broadcast_to(end_decays[0:1, :] * end_decays[1:2, :], (PACK, HD))
        coarse, middle, _ = split(decay)
        packed = jnp.where(
            row_ids == 0, coarse.astype(F32), jnp.where(row_ids == 1, middle.astype(F32), 0.0)
        ).astype(BF16)
        for piece in range(PARTS):
            at = head * PARTS + piece
            send_buf[at, 0:PIECE, :] = summary[piece * PIECE : (piece + 1) * PIECE].astype(BF16)
            send_buf[at, PIECE : PIECE + PACK, :] = packed

    over_heads(fetch, body, leave, started=True, group=4)


def within_kernel(
    cum_rows_ref, queries_ref, keys_ref, values_ref,
    within_ref, weights_ref, done_ref,
    queries_buf, keys_buf, values_buf, within_buf, scaled_queries_buf, weights_buf, in_sems, out_sems,
):
    fetch = Copies(
        [
            (of_rows(queries_ref), of_lead(queries_buf)),
            (of_rows(keys_ref), of_lead(keys_buf)),
            (of_rows(values_ref), of_lead(values_buf)),
        ],
        in_sems,
    )
    leave = Copies(
        [
            (of_lead(within_buf), of_lead(within_ref)),
            (of_lead(scaled_queries_buf), of_lead(within_ref, first=HL)),
            (of_lead(weights_buf), of_lead(weights_ref)),
        ],
        out_sems,
    )
    done_ref[...] = jnp.zeros_like(done_ref)
    row_ids = lax.broadcasted_iota(jnp.int32, (BLK, BLK), 0)
    col_ids = lax.broadcasted_iota(jnp.int32, (BLK, BLK), 1)

    def body(head):
        for number in range(BLOCKS):
            part = rows(number)
            queries = queries_buf[head, part, :]
            keys = keys_buf[head, part, :]
            row = cum_rows_ref[pl.ds(head, 1), part]
            gaps = row - twice(down(row))
            mask = jnp.where(col_ids >= row_ids, jnp.exp(gaps), 0.0)
            weights = (mm_nt(keys, queries) * mask).astype(BF16)
            weights_buf[head, part, :] = weights
            within_buf[head, part, :] = mm_tn(weights, values_buf[head, part, :]).astype(BF16)
            scaled_queries_buf[head, part, :] = rounded_product(queries, down(jnp.exp(row)))

    over_heads(fetch, body, leave, group=4)


def scaled_keys_kernel(
    cum_rows_ref, keys_ref, _after, scaled_keys_ref, done_ref,
    keys_buf, scaled_keys_buf, in_sems, out_sems,
):
    fetch = Copies([(of_rows(keys_ref, P_DEV), of_lead(keys_buf))], in_sems)
    leave = Copies([(of_lead(scaled_keys_buf), of_lead(scaled_keys_ref))], out_sems)
    done_ref[...] = jnp.zeros_like(done_ref)

    def body(head):
        for number in range(2):
            part = rows(number)
            row = cum_rows_ref[pl.ds(head, 1), part]
            factor = down(jnp.exp(row[:, BLK - 1 : BLK] - row))
            scaled_keys_buf[head, part, :] = rounded_product(keys_buf[head, part, :], factor)

    over_heads(fetch, body, leave)


def forward_scan_kernel(parents_ref, got_ref, _after, send_ref, decay_ref):
    totals = []
    for prompt in range(PROMPTS):
        carry = jnp.zeros((PIECE, HD), F32)
        for index in range(prompt * SPAN, (prompt + 1) * SPAN):
            packed = got_ref[index, PIECE : PIECE + PACK, :].astype(F32)
            decay = packed[0:1, :] + packed[1:2, :]
            decay_ref[index : index + 1, :] = decay
            send_ref[index, 0:PIECE, :] = carry.astype(BF16)
            carry = decay * carry + got_ref[index, 0:PIECE, :].astype(F32)
        totals.append(carry)
    for index in range(N_SEQ):
        prompt = parents_ref[index] // SPAN
        chosen = jnp.where(prompt == 0, totals[0], totals[1])
        decay_ref[N_SEQ + index : N_SEQ + index + 1, :] = jnp.full((1, HD), prompt, F32)
        send_ref[index, PIECE : 2 * PIECE, :] = chosen.astype(BF16)


def attend_kernel(
    ends_ref, gain_ref, d_out_ref, starts_ref, term_ref, within_ref, _after,
    queries_ref, attended_ref, stats_ref, kept_ref, states_ref,
    within_buf, states_buf, squares_ref, products_ref, in_sems, out_sems,
):
    fetch = Copies(
        [
            (of_lead(within_ref, first=HL), of_lead(queries_ref)),
            (of_lead(within_ref), of_lead(within_buf)),
        ],
        in_sems,
    )
    leave = Copies(
        [
            (of_lead(attended_ref), of_lead(kept_ref)),
            (of_lead(states_buf, BLOCKS), of_lead(states_ref, BLOCKS)),
        ],
        out_sems,
    )
    fetch.begin()
    squares_ref[...] = jnp.zeros_like(squares_ref)
    products_ref[...] = jnp.zeros_like(products_ref)

    def body(head):
        got = starts_ref[pl.ds(head * PARTS, PARTS)]
        first = got[:, 0:PIECE, :].reshape(HD, HD)
        reply = got[:, PIECE : 2 * PIECE, :].reshape(HD, HD)
        end_decay = ends_ref[head][0:1, :]
        second = (end_decay * first.astype(F32) + term_ref[head]).astype(BF16)
        gain = gain_ref[pl.ds(head, 1), :]
        for number, start in enumerate((first, second, reply)):
            part = rows(number)
            states_buf[head * BLOCKS + number] = start
            attended = within_buf[head, part, :].astype(F32) + mm(
                queries_ref[head, part, :], start
            )
            attended_ref[head, part, :] = attended.astype(BF16)
            weighted = gain * d_out_ref[0, part, lanes(head)].astype(F32)
            squares_ref[part, :] += attended * attended
            products_ref[part, :] += weighted * attended

    over_heads(fetch, body, leave, started=True)
    stats_ref[...] = jnp.zeros_like(stats_ref)
    for tile in range(TILES):
        for base, sums_ref in ((0, squares_ref), (8, products_ref)):
            row = jnp.sum(sums_ref[tile_rows(tile), :].T, axis=0, keepdims=True)
            stats_ref[:, base + tile : base + tile + 1, :] = jnp.broadcast_to(
                row[None], (HL, 1, HD)
            )


def row_factors(stats_ref, inverse_ref, slope_ref):
    total = stats_ref[0]
    for source in range(1, HL):
        total = total + stats_ref[source]
    turned = jnp.concatenate([total, jnp.zeros((HD - 16, HD), F32)], axis=0).T
    for tile in range(TILES):
        squares = turned[:, tile : tile + 1]
        products = turned[:, 8 + tile : 9 + tile]
        inverse = lax.rsqrt(squares / (H * HD) + EPS)
        slope = inverse * inverse * inverse * products / (H * HD)
        inverse_ref[tile_rows(tile), :] = jnp.broadcast_to(inverse, (HD, HD))
        slope_ref[tile_rows(tile), :] = jnp.broadcast_to(slope, (HD, HD))


def grad_kernel(
    ends_ref, gain_ref, stats_ref, queries_ref, d_out_ref, attended_ref,
    send_ref, inverse_ref, slope_ref,
):
    row_factors(stats_ref, inverse_ref, slope_ref)

    def body(head):
        gain = gain_ref[pl.ds(head, 1), :]
        terms = []
        for number in range(BLOCKS):
            part = rows(number)
            weighted = gain * d_out_ref[0, part, lanes(head)].astype(F32)
            grad = (
                inverse_ref[part, :] * weighted
                - attended_ref[head, part, :].astype(F32) * slope_ref[part, :]
            ).astype(BF16)
            terms.append(mm_tn(queries_ref[head, part, :], grad))
        local_sum = ends_ref[head][0:1, :] * terms[1] + terms[0]
        for piece in range(PARTS):
            at = head * PARTS + piece
            part = slice(piece * PIECE, (piece + 1) * PIECE)
            send_ref[at, 0:PIECE, :] = local_sum[part].astype(BF16)
            send_ref[at, PIECE : 2 * PIECE, :] = terms[2][part].astype(BF16)

    over_heads(None, body, group=HL)


def backward_scan_kernel(got_ref, decay_ref, _after, send_ref):
    branches = [jnp.zeros((PIECE, HD), F32) for _ in range(PROMPTS)]
    for index in range(N_SEQ):
        prompt = decay_ref[N_SEQ + index : N_SEQ + index + 1, :]
        start_grad = got_ref[index, PIECE : 2 * PIECE, :].astype(F32)
        for each in range(PROMPTS):
            branches[each] = branches[each] + jnp.where(prompt == each, start_grad, 0.0)
    for prompt in range(PROMPTS):
        carry = branches[prompt]
        for index in reversed(range(prompt * SPAN, (prompt + 1) * SPAN)):
            send_ref[index] = carry.astype(BF16)
            carry = decay_ref[index : index + 1, :] * carry + got_ref[index, 0:PIECE, :].astype(F32)


def local_grads_kernel(
    cum_rows_ref, stats_ref, gain_ref,
    queries_ref, keys_ref, values_ref, d_out_ref, attended_ref, states_ref, weights_ref,
    out_ref, d_queries_ref, d_keys_ref, d_values_ref, term_ref, done_ref,
    queries_buf, keys_buf, values_buf, d_out_buf, attended_buf, states_buf, weights_buf,
    out_buf, d_queries_buf, d_keys_buf, d_values_buf, term_buf,
    inverse_ref, slope_ref, in_sems, out_sems,
):
    fetch = Copies(
        [
            (of_rows(d_out_ref), of_lead(d_out_buf)),
            (of_lead(attended_ref), of_lead(attended_buf)),
            (of_rows(queries_ref), of_lead(queries_buf)),
            (of_rows(keys_ref), of_lead(keys_buf)),
            (of_rows(values_ref), of_lead(values_buf)),
            (of_lead(states_ref, BLOCKS), of_lead(states_buf, BLOCKS)),
            (of_lead(weights_ref), of_lead(weights_buf)),
        ],
        in_sems,
    )
    leave = Copies(
        [
            (of_lead(out_buf), of_rows(out_ref)),
            (of_lead(d_queries_buf), of_rows(d_queries_ref)),
            (of_lead(d_keys_buf), of_rows(d_keys_ref)),
            (of_lead(d_values_buf), of_rows(d_values_ref)),
            (of_lead(term_buf), of_lead(term_ref)),
        ],
        out_sems,
    )
    fetch.begin()
    done_ref[...] = jnp.zeros_like(done_ref)
    row_factors(stats_ref, inverse_ref, slope_ref)
    row_ids = lax.broadcasted_iota(jnp.int32, (BLK, BLK), 0)
    col_ids = lax.broadcasted_iota(jnp.int32, (BLK, BLK), 1)

    def body(head):
        gain = gain_ref[pl.ds(head, 1), :]
        for number in range(BLOCKS):
            part = rows(number)
            queries = queries_buf[head, part, :]
            keys = keys_buf[head, part, :]
            values = values_buf[head, part, :]
            attended = attended_buf[head, part, :].astype(F32)
            inverse = inverse_ref[part, :]
            weighted = gain * d_out_buf[head, part, :].astype(F32)
            grad = (inverse * weighted - attended * slope_ref[part, :]).astype(BF16)
            out_buf[head, part, :] = (attended * inverse * gain).astype(BF16)
            row = cum_rows_ref[pl.ds(head, 1), part]
            gaps = row - twice(down(row))
            mask = jnp.where(col_ids >= row_ids, jnp.exp(gaps), 0.0)
            weights = weights_buf[head, part, :]
            score_grad = (mm_nt(values, grad) * mask).astype(BF16)
            growth = down(jnp.exp(row))
            start = states_buf[head * BLOCKS + number]
            grad_queries = mm_tn(score_grad, keys) + growth * mm_nt(grad, start)
            d_queries_buf[head, part, :] = grad_queries.astype(BF16)
            if number == 1:
                term_buf[head] = mm_tn(rounded_product(queries, growth), grad)
            d_keys_buf[head, part, :] = mm(score_grad, queries).astype(BF16)
            d_values_buf[head, part, :] = mm(weights, grad).astype(BF16)

    over_heads(fetch, body, leave, started=True)


def far_grads_kernel(
    cum_rows_ref, ends_ref, far_ref, scaled_keys_ref, values_ref, term_ref,
    near_keys_ref, near_values_ref, d_keys_ref, d_values_ref,
    term_buf, near_keys_buf, near_values_buf, d_keys_buf, d_values_buf, in_sems, out_sems,
):
    fetch = Copies(
        [
            (of_lead(term_ref), of_lead(term_buf)),
            (of_rows(near_keys_ref, P_DEV), of_lead(near_keys_buf)),
            (of_rows(near_values_ref, P_DEV), of_lead(near_values_buf)),
        ],
        in_sems,
    )
    leave = Copies(
        [
            (of_lead(d_keys_buf), of_rows(d_keys_ref, P_DEV)),
            (of_lead(d_values_buf), of_rows(d_values_ref, P_DEV)),
        ],
        out_sems,
    )

    def body(head):
        second = far_ref[pl.ds(head * PARTS, PARTS)].reshape(HD, HD)
        first = (ends_ref[head][1:2, :] * second.astype(F32) + term_buf[head]).astype(BF16)
        for number, end_grad in enumerate((first, second)):
            part = rows(number)
            row = cum_rows_ref[pl.ds(head, 1), part]
            factor = down(jnp.exp(row[:, BLK - 1 : BLK] - row))
            grad_values = near_values_buf[head, part, :].astype(F32) + mm(
                scaled_keys_ref[head, part, :], end_grad
            )
            grad_keys = near_keys_buf[head, part, :].astype(F32) + factor * mm_nt(
                values_ref[0, part, lanes(head)], end_grad
            )
            d_values_buf[head, part, :] = grad_values.astype(BF16)
            d_keys_buf[head, part, :] = grad_keys.astype(BF16)

    over_heads(fetch, body, leave)


def shape(dims, kind):
    return jax.ShapeDtypeStruct(dims, kind)


HBM = pl.BlockSpec(memory_space=pltpu.HBM)
SMEM = pl.BlockSpec(memory_space=pltpu.SMEM)
VMEM = pl.BlockSpec(memory_space=pltpu.VMEM)
WIDE = shape((1, ROWS, COLS), BF16)
HEAD_ROWS = (HL, ROWS, HD)
HEAD_PROMPT = (HL, P_DEV, HD)
HEAD_REPLY = (HL, BLK, HD)
STATE = (HL, HD, HD)
PIECES = (N_SEQ, PIECE, HD)
TWO_PIECES = (N_SEQ, 2 * PIECE, HD)
SENT_PIECES = (N_SEQ, PIECE + PACK, HD)
CUM = (ROWS, HD)
FAR = 100


def call(kernel, name, in_specs, outs, scratch, semaphores, mib, flops, moved, aliases=None):
    return pl.pallas_call(
        kernel,
        in_specs=in_specs,
        out_specs=[spec for spec, _ in outs],
        out_shape=[made for _, made in outs],
        scratch_shapes=[pltpu.VMEM(dims, kind) for dims, kind in scratch]
        + [pltpu.SemaphoreType.DMA((count, HL)) for count in semaphores],
        input_output_aliases=aliases or {},
        compiler_params=pltpu.CompilerParams(vmem_limit_bytes=mib << 20),
        cost_estimate=pl.CostEstimate(
            flops=int(flops), bytes_accessed=int(moved) << 20, transcendentals=0
        ),
        name=name,
    )


def summarize(decay_rows, keys, values):
    return call(
        summary_kernel, "summary", [HBM, HBM, HBM],
        [
            (HBM, shape(SENT_PIECES, BF16)), (VMEM, shape(STATE, F32)),
            (VMEM, shape((HL, ROWS), F32)), (VMEM, shape((HL, 8, HD), F32)),
        ],
        [(HEAD_PROMPT, BF16), (HEAD_PROMPT, BF16), ((1, HL, ROWS), F32), (SENT_PIECES, BF16)],
        [2, 1, 1], 52, 3e8, 4,
    )(decay_rows, keys, values)


def inside(cum_rows, queries, keys, values):
    return call(
        within_kernel, "within", [VMEM] + [HBM] * 3,
        [
            (HBM, shape((FAR, ROWS, HD), BF16)), (HBM, shape((FAR // 2, ROWS, BLK), BF16)),
            (VMEM, shape((8, HD), F32)),
        ],
        [(HEAD_ROWS, BF16)] * 5 + [((HL, ROWS, BLK), BF16)], [3, 3], 53, 4e9, 16,
    )(cum_rows, queries, keys, values)


def scale_keys(cum_rows, keys, after):
    return call(
        scaled_keys_kernel, "scaled_keys", [VMEM, HBM, HBM],
        [(HBM, shape(HEAD_PROMPT, BF16)), (VMEM, shape((8, HD), F32))],
        [(HEAD_PROMPT, BF16)] * 2, [1, 1], 53, 2e9, 8,
    )(cum_rows, keys, after)


def forward_scan(parents, got, after):
    return call(
        forward_scan_kernel, "forward_scan", [SMEM, VMEM, HBM],
        [(VMEM, shape(TWO_PIECES, BF16)), (VMEM, shape((2 * N_SEQ, HD), F32))],
        [], [], 12, 1e6, 1,
    )(parents, got, after)


def attend(ends, gains, d_out, starts, term, within, after):
    return call(
        attend_kernel, "attend", [VMEM] * 5 + [HBM] * 2,
        [
            (VMEM, shape(HEAD_ROWS, BF16)), (VMEM, shape(HEAD_ROWS, BF16)),
            (VMEM, shape((HL, 16, HD), F32)), (HBM, shape((FAR, ROWS, HD), BF16)),
            (HBM, shape((6 * FAR, HD, HD), BF16)),
        ],
        [(HEAD_ROWS, BF16), ((HL * BLOCKS, HD, HD), BF16), (CUM, F32), (CUM, F32)],
        [2, 2], 46, 3e8, 10,
    )(ends, gains, d_out, starts, term, within, after)


def grads(ends, gains, stats, scaled_queries, d_out, attended):
    return call(
        grad_kernel, "grad", [VMEM] * 6, [(VMEM, shape(TWO_PIECES, BF16))],
        [(CUM, F32), (CUM, F32)], [], 20, 3e8, 10,
    )(ends, gains, stats, scaled_queries, d_out, attended)[0]


def local_grads(
    cum_rows, stats, gains, queries, keys, values, d_out, attended, states, weights
):
    return call(
        local_grads_kernel, "local_grads", [VMEM] * 3 + [HBM] * 7,
        [
            (HBM, WIDE), (HBM, WIDE), (HBM, WIDE), (HBM, WIDE),
            (HBM, shape((4 * FAR, HD, HD), F32)), (VMEM, shape((8, HD), F32)),
        ],
        [(HEAD_ROWS, BF16)] * 5 + [((HL * BLOCKS, HD, HD), BF16), ((HL, ROWS, BLK), BF16)]
        + [(HEAD_ROWS, BF16)] * 4
        + [(STATE, F32), (CUM, F32), (CUM, F32)],
        [7, 5], 53, 6e9, 24,
    )(cum_rows, stats, gains, queries, keys, values, d_out, attended, states, weights)


def far_grads(cum_rows, ends, far, scaled_keys, values, term, near_keys, near_values):
    return call(
        far_grads_kernel, "far_grads", [VMEM] * 5 + [HBM] * 3,
        [(HBM, WIDE), (HBM, WIDE)],
        [(STATE, F32)] + [(HEAD_PROMPT, BF16)] * 4, [3, 2], 44, 3e8, 10, {6: 0, 7: 1},
    )(cum_rows, ends, far, scaled_keys, values, term, near_keys, near_values)


def backward_scan(got, decays, after):
    return call(
        backward_scan_kernel, "backward_scan", [VMEM, VMEM, HBM],
        [(VMEM, shape(PIECES, BF16))], [], [], 12, 1e6, 1,
    )(got, decays, after)[0]


def everyone(array, axis):
    return lax.all_to_all(array, axis, 0, 0, tiled=True)


def local(queries, keys, values, log_decay, gain, parents, d_out):
    gains = gain.reshape(HL, HD)
    decay_rows = jnp.swapaxes(log_decay, 1, 2)
    send, first_term, cum_rows, block_ends = summarize(decay_rows, keys, values)
    got = everyone(send, "seq")
    within, weights, done = inside(cum_rows, queries, keys, values)
    send, decays = forward_scan(parents, got, done)
    starts = everyone(send, "seq")
    scaled_keys, done = scale_keys(cum_rows, keys, decays)
    near_queries, attended, stats, kept, states = attend(
        block_ends, gains, d_out, starts, first_term, within, done
    )
    stats = everyone(stats, "head")
    send = grads(block_ends, gains, stats, near_queries, d_out, attended)
    got = everyone(send, "seq")
    out, d_queries, d_keys, d_values, last_term, done = local_grads(
        cum_rows, stats, gains, queries, keys, values, d_out, kept, states, weights
    )
    far = everyone(backward_scan(got, decays, done), "seq")
    d_keys, d_values = far_grads(
        cum_rows, block_ends, far, scaled_keys, values, last_term, d_keys, d_values
    )
    return (out, d_queries, d_keys, d_values)


def solution(mesh):
    cut = P("seq", None, "head")
    return jax.shard_map(
        local,
        mesh=mesh,
        in_specs=(cut, cut, cut, cut, P("head"), P(), cut),
        out_specs=(cut, cut, cut, cut),
        check_vma=False,
    )
```

```python
import jax
import jax.numpy as jnp
from jax import lax
from jax.experimental import pallas as pl
from jax.experimental.pallas import tpu as pltpu
from jax.sharding import PartitionSpec as P

H = 64
HD = 128
BLK = 256
PROMPTS = 2
P_DEV = 512
ROWS = 768
HL = 8
N_SEQ = 32
SPAN = N_SEQ // PROMPTS
COLS = HL * HD
PIECE = HL * HD // N_SEQ
PARTS = HD // PIECE
PACK = 8
BLOCKS = ROWS // BLK
TILES = ROWS // HD
EPS = 1e-05
GROUP = 2

F32 = jnp.float32
BF16 = jnp.bfloat16


def dot(a, b, dims):
    return lax.dot_general(a, b, (dims, ((), ())), preferred_element_type=F32)


def mm(a, b):
    return dot(a, b, ((1,), (0,)))


def mm_nt(a, b):
    return dot(a, b, ((1,), (1,)))


def mm_tn(a, b):
    return dot(a, b, ((0,), (0,)))


def rows(number):
    return slice(number * BLK, (number + 1) * BLK)


def tile_rows(tile):
    return slice(tile * HD, (tile + 1) * HD)


def down(row):
    return jnp.broadcast_to(row, (HD, BLK)).T


def twice(block):
    return jnp.concatenate([block, block], axis=1)


def rounded_product(block, factor):
    return (block.astype(F32) * factor).astype(BF16)


def lanes(head):
    return pl.ds(pl.multiple_of(head * HD, HD), HD)


def of_rows(ref, count=ROWS, first=0):
    if len(ref.shape) == 3:
        return lambda head: ref.at[0, pl.ds(first, count), lanes(head)]
    return lambda head: ref.at[pl.ds(first, count), lanes(head)]


def of_lead(ref, count=1, first=0):
    if count == 1:
        return lambda head: ref.at[head + first]
    return lambda head: ref.at[pl.ds(head * count, count)]


class Copies:
    def __init__(self, pairs, sems):
        self.pairs, self.sems = pairs, sems

    def each(self, head):
        return [
            pltpu.make_async_copy(src(head), dst(head), self.sems.at[number, head])
            for number, (src, dst) in enumerate(self.pairs)
        ]

    def start(self, head):
        for copy in self.each(head):
            copy.start()

    def begin(self):
        for head in range(HL):
            self.start(head)

    def wait(self, head):
        for copy in self.each(head):
            copy.wait()


def over_heads(fetch, body, leave=None, started=False, group=GROUP):
    if fetch is not None and not started:
        fetch.begin()

    def step(number, carry):
        heads = [number * group + place for place in range(group)]
        for head in heads:
            if fetch is not None:
                fetch.wait(head)
        for head in heads:
            body(head)
        for head in heads:
            if leave is not None:
                leave.start(head)
        return carry

    lax.fori_loop(0, HL // group, step, 0)
    if leave is not None:
        for head in range(HL):
            leave.wait(head)


def split(value):
    coarse = value.astype(BF16)
    rest = value - coarse.astype(F32)
    middle = rest.astype(BF16)
    return coarse, middle, (rest - middle.astype(F32)).astype(BF16)


def summary_kernel(
    decay_ref, keys_ref, values_ref,
    send_ref, term_ref, cum_rows_ref, ends_ref,
    keys_buf, values_buf, decay_buf, send_buf, in_sems, out_sems, decay_sem,
):
    fetch = Copies(
        [
            (of_rows(keys_ref, P_DEV), of_lead(keys_buf)),
            (of_rows(values_ref, P_DEV), of_lead(values_buf)),
        ],
        in_sems,
    )
    leave = Copies([(of_lead(send_buf, PARTS), of_lead(send_ref, PARTS))], out_sems)
    decay_copy = pltpu.make_async_copy(decay_ref, decay_buf, decay_sem.at[0, 0])
    decay_copy.start()
    fetch.begin()
    before = lax.broadcasted_iota(jnp.int32, (BLK, BLK), 0)
    after = lax.broadcasted_iota(jnp.int32, (BLK, BLK), 1)
    upper = jnp.where(before <= after, 1.0, 0.0).astype(BF16)
    decay_copy.wait()
    stacked = jnp.concatenate(
        [decay_buf[0, :, rows(number)] for number in range(BLOCKS)], axis=0
    )
    coarse, middle, fine = (mm(part, upper) for part in split(stacked))
    cumulative = (fine + middle) + coarse
    for number in range(BLOCKS):
        total = cumulative[number * HL : (number + 1) * HL]
        cum_rows_ref[:, rows(number)] = total
        ends_ref[:, number, :] = jnp.broadcast_to(jnp.exp(total[:, BLK - 1 : BLK]), (HL, HD))
    row_ids = lax.broadcasted_iota(jnp.int32, (PACK, HD), 0)

    def body(head):
        terms = []
        for number in range(2):
            row = cum_rows_ref[pl.ds(head, 1), rows(number)]
            factor = jnp.exp(row[:, BLK - 1 : BLK] - row)
            turned = keys_buf[head, rows(number), :].T
            key_scaled = rounded_product(turned, factor)
            terms.append(mm(key_scaled, values_buf[head, rows(number), :]))
        term_ref[head] = terms[0]
        end_decays = ends_ref[head]
        summary = end_decays[1:2, :] * terms[0] + terms[1]
        decay = jnp.broadcast_to(end_decays[0:1, :] * end_decays[1:2, :], (PACK, HD))
        coarse, middle, _ = split(decay)
        packed = jnp.where(
            row_ids == 0, coarse.astype(F32), jnp.where(row_ids == 1, middle.astype(F32), 0.0)
        ).astype(BF16)
        for piece in range(PARTS):
            at = head * PARTS + piece
            send_buf[at, 0:PIECE, :] = summary[piece * PIECE : (piece + 1) * PIECE].astype(BF16)
            send_buf[at, PIECE : PIECE + PACK, :] = packed

    over_heads(fetch, body, leave, started=True, group=4)


def within_kernel(
    cum_rows_ref, queries_ref, keys_ref, values_ref,
    within_ref, scaled_keys_ref, weights_ref, done_ref,
    queries_buf, keys_buf, values_buf, within_buf, scaled_queries_buf, scaled_keys_buf,
    weights_buf, in_sems, out_sems,
):
    fetch = Copies(
        [
            (of_rows(queries_ref), of_lead(queries_buf)),
            (of_rows(keys_ref), of_lead(keys_buf)),
            (of_rows(values_ref), of_lead(values_buf)),
        ],
        in_sems,
    )
    leave = Copies(
        [
            (of_lead(within_buf), of_lead(within_ref)),
            (of_lead(scaled_queries_buf), of_lead(within_ref, first=HL)),
            (of_lead(scaled_keys_buf), of_lead(scaled_keys_ref)),
            (of_lead(weights_buf), of_lead(weights_ref)),
        ],
        out_sems,
    )
    done_ref[...] = jnp.zeros_like(done_ref)
    row_ids = lax.broadcasted_iota(jnp.int32, (BLK, BLK), 0)
    col_ids = lax.broadcasted_iota(jnp.int32, (BLK, BLK), 1)

    def body(head):
        for number in range(BLOCKS):
            part = rows(number)
            queries = queries_buf[head, part, :]
            keys = keys_buf[head, part, :]
            row = cum_rows_ref[pl.ds(head, 1), part]
            gaps = row - twice(down(row))
            mask = jnp.where(col_ids >= row_ids, jnp.exp(gaps), 0.0)
            weights = (mm_nt(keys, queries) * mask).astype(BF16)
            weights_buf[head, part, :] = weights
            within_buf[head, part, :] = mm_tn(weights, values_buf[head, part, :]).astype(BF16)
            scaled_queries_buf[head, part, :] = rounded_product(queries, down(jnp.exp(row)))
            if number < 2:
                factor = down(jnp.exp(row[:, BLK - 1 : BLK] - row))
                scaled_keys_buf[head, part, :] = rounded_product(keys, factor)

    over_heads(fetch, body, leave, group=4)


def forward_scan_kernel(parents_ref, got_ref, _after, send_ref, decay_ref):
    totals = []
    for prompt in range(PROMPTS):
        carry = jnp.zeros((PIECE, HD), F32)
        for index in range(prompt * SPAN, (prompt + 1) * SPAN):
            packed = got_ref[index, PIECE : PIECE + PACK, :].astype(F32)
            decay = packed[0:1, :] + packed[1:2, :]
            decay_ref[index : index + 1, :] = decay
            send_ref[index, 0:PIECE, :] = carry.astype(BF16)
            carry = decay * carry + got_ref[index, 0:PIECE, :].astype(F32)
        totals.append(carry)
    for index in range(N_SEQ):
        prompt = parents_ref[index] // SPAN
        chosen = jnp.where(prompt == 0, totals[0], totals[1])
        decay_ref[N_SEQ + index : N_SEQ + index + 1, :] = jnp.full((1, HD), prompt, F32)
        send_ref[index, PIECE : 2 * PIECE, :] = chosen.astype(BF16)


def attend_kernel(
    ends_ref, gain_ref, d_out_ref, starts_ref, term_ref, within_ref,
    queries_ref, attended_ref, stats_ref, kept_ref, states_ref,
    within_buf, states_buf, squares_ref, products_ref, in_sems, out_sems,
):
    fetch = Copies(
        [
            (of_lead(within_ref, first=HL), of_lead(queries_ref)),
            (of_lead(within_ref), of_lead(within_buf)),
        ],
        in_sems,
    )
    leave = Copies(
        [
            (of_lead(attended_ref), of_lead(kept_ref)),
            (of_lead(states_buf, BLOCKS), of_lead(states_ref, BLOCKS)),
        ],
        out_sems,
    )
    fetch.begin()
    squares_ref[...] = jnp.zeros_like(squares_ref)
    products_ref[...] = jnp.zeros_like(products_ref)

    def body(head):
        got = starts_ref[pl.ds(head * PARTS, PARTS)]
        first = got[:, 0:PIECE, :].reshape(HD, HD)
        reply = got[:, PIECE : 2 * PIECE, :].reshape(HD, HD)
        end_decay = ends_ref[head][0:1, :]
        second = (end_decay * first.astype(F32) + term_ref[head]).astype(BF16)
        gain = gain_ref[pl.ds(head, 1), :]
        for number, start in enumerate((first, second, reply)):
            part = rows(number)
            states_buf[head * BLOCKS + number] = start
            attended = within_buf[head, part, :].astype(F32) + mm(
                queries_ref[head, part, :], start
            )
            attended_ref[head, part, :] = attended.astype(BF16)
            weighted = gain * d_out_ref[0, part, lanes(head)].astype(F32)
            squares_ref[part, :] += attended * attended
            products_ref[part, :] += weighted * attended

    over_heads(fetch, body, leave, started=True)
    stats_ref[...] = jnp.zeros_like(stats_ref)
    for tile in range(TILES):
        for base, sums_ref in ((0, squares_ref), (8, products_ref)):
            row = jnp.sum(sums_ref[tile_rows(tile), :].T, axis=0, keepdims=True)
            stats_ref[:, base + tile : base + tile + 1, :] = jnp.broadcast_to(
                row[None], (HL, 1, HD)
            )


def row_factors(stats_ref, inverse_ref, slope_ref):
    total = stats_ref[0]
    for source in range(1, HL):
        total = total + stats_ref[source]
    turned = jnp.concatenate([total, jnp.zeros((HD - 16, HD), F32)], axis=0).T
    for tile in range(TILES):
        squares = turned[:, tile : tile + 1]
        products = turned[:, 8 + tile : 9 + tile]
        inverse = lax.rsqrt(squares / (H * HD) + EPS)
        slope = inverse * inverse * inverse * products / (H * HD)
        inverse_ref[tile_rows(tile), :] = jnp.broadcast_to(inverse, (HD, HD))
        slope_ref[tile_rows(tile), :] = jnp.broadcast_to(slope, (HD, HD))


def grad_kernel(
    ends_ref, gain_ref, stats_ref, queries_ref, d_out_ref, attended_ref,
    send_ref, inverse_ref, slope_ref,
):
    row_factors(stats_ref, inverse_ref, slope_ref)

    def body(head):
        gain = gain_ref[pl.ds(head, 1), :]
        terms = []
        for number in range(BLOCKS):
            part = rows(number)
            weighted = gain * d_out_ref[0, part, lanes(head)].astype(F32)
            grad = (
                inverse_ref[part, :] * weighted
                - attended_ref[head, part, :].astype(F32) * slope_ref[part, :]
            ).astype(BF16)
            terms.append(mm_tn(queries_ref[head, part, :], grad))
        local_sum = ends_ref[head][0:1, :] * terms[1] + terms[0]
        for piece in range(PARTS):
            at = head * PARTS + piece
            part = slice(piece * PIECE, (piece + 1) * PIECE)
            send_ref[at, 0:PIECE, :] = local_sum[part].astype(BF16)
            send_ref[at, PIECE : 2 * PIECE, :] = terms[2][part].astype(BF16)

    over_heads(None, body, group=HL)


def backward_scan_kernel(got_ref, decay_ref, _after, send_ref):
    branches = [jnp.zeros((PIECE, HD), F32) for _ in range(PROMPTS)]
    for index in range(N_SEQ):
        prompt = decay_ref[N_SEQ + index : N_SEQ + index + 1, :]
        start_grad = got_ref[index, PIECE : 2 * PIECE, :].astype(F32)
        for each in range(PROMPTS):
            branches[each] = branches[each] + jnp.where(prompt == each, start_grad, 0.0)
    for prompt in range(PROMPTS):
        carry = branches[prompt]
        for index in reversed(range(prompt * SPAN, (prompt + 1) * SPAN)):
            send_ref[index] = carry.astype(BF16)
            carry = decay_ref[index : index + 1, :] * carry + got_ref[index, 0:PIECE, :].astype(F32)


def local_grads_kernel(
    cum_rows_ref, stats_ref, gain_ref,
    queries_ref, keys_ref, values_ref, d_out_ref, attended_ref, states_ref, weights_ref,
    out_ref, d_queries_ref, d_keys_ref, d_values_ref, term_ref, done_ref,
    queries_buf, keys_buf, values_buf, d_out_buf, attended_buf, states_buf, weights_buf,
    out_buf, d_queries_buf, d_keys_buf, d_values_buf, term_buf,
    inverse_ref, slope_ref, in_sems, out_sems,
):
    fetch = Copies(
        [
            (of_rows(d_out_ref), of_lead(d_out_buf)),
            (of_lead(attended_ref), of_lead(attended_buf)),
            (of_rows(queries_ref), of_lead(queries_buf)),
            (of_rows(keys_ref), of_lead(keys_buf)),
            (of_rows(values_ref), of_lead(values_buf)),
            (of_lead(states_ref, BLOCKS), of_lead(states_buf, BLOCKS)),
            (of_lead(weights_ref), of_lead(weights_buf)),
        ],
        in_sems,
    )
    leave = Copies(
        [
            (of_lead(out_buf), of_rows(out_ref)),
            (of_lead(d_queries_buf), of_rows(d_queries_ref)),
            (of_lead(d_keys_buf), of_rows(d_keys_ref)),
            (of_lead(d_values_buf), of_rows(d_values_ref)),
            (of_lead(term_buf), of_lead(term_ref)),
        ],
        out_sems,
    )
    fetch.begin()
    done_ref[...] = jnp.zeros_like(done_ref)
    row_factors(stats_ref, inverse_ref, slope_ref)
    row_ids = lax.broadcasted_iota(jnp.int32, (BLK, BLK), 0)
    col_ids = lax.broadcasted_iota(jnp.int32, (BLK, BLK), 1)

    def body(head):
        gain = gain_ref[pl.ds(head, 1), :]
        for number in range(BLOCKS):
            part = rows(number)
            queries = queries_buf[head, part, :]
            keys = keys_buf[head, part, :]
            values = values_buf[head, part, :]
            attended = attended_buf[head, part, :].astype(F32)
            inverse = inverse_ref[part, :]
            weighted = gain * d_out_buf[head, part, :].astype(F32)
            grad = (inverse * weighted - attended * slope_ref[part, :]).astype(BF16)
            out_buf[head, part, :] = (attended * inverse * gain).astype(BF16)
            row = cum_rows_ref[pl.ds(head, 1), part]
            gaps = row - twice(down(row))
            mask = jnp.where(col_ids >= row_ids, jnp.exp(gaps), 0.0)
            weights = weights_buf[head, part, :]
            score_grad = (mm_nt(values, grad) * mask).astype(BF16)
            growth = down(jnp.exp(row))
            start = states_buf[head * BLOCKS + number]
            grad_queries = mm_tn(score_grad, keys) + growth * mm_nt(grad, start)
            d_queries_buf[head, part, :] = grad_queries.astype(BF16)
            if number == 1:
                term_buf[head] = mm_tn(rounded_product(queries, growth), grad)
            d_keys_buf[head, part, :] = mm(score_grad, queries).astype(BF16)
            d_values_buf[head, part, :] = mm(weights, grad).astype(BF16)

    over_heads(fetch, body, leave, started=True)


def far_grads_kernel(
    cum_rows_ref, ends_ref, far_ref, scaled_keys_ref, values_ref, term_ref,
    near_keys_ref, near_values_ref, d_keys_ref, d_values_ref,
    term_buf, near_keys_buf, near_values_buf, d_keys_buf, d_values_buf, in_sems, out_sems,
):
    fetch = Copies(
        [
            (of_lead(term_ref), of_lead(term_buf)),
            (of_rows(near_keys_ref, P_DEV), of_lead(near_keys_buf)),
            (of_rows(near_values_ref, P_DEV), of_lead(near_values_buf)),
        ],
        in_sems,
    )
    leave = Copies(
        [
            (of_lead(d_keys_buf), of_rows(d_keys_ref, P_DEV)),
            (of_lead(d_values_buf), of_rows(d_values_ref, P_DEV)),
        ],
        out_sems,
    )

    def body(head):
        second = far_ref[pl.ds(head * PARTS, PARTS)].reshape(HD, HD)
        first = (ends_ref[head][1:2, :] * second.astype(F32) + term_buf[head]).astype(BF16)
        for number, end_grad in enumerate((first, second)):
            part = rows(number)
            row = cum_rows_ref[pl.ds(head, 1), part]
            factor = down(jnp.exp(row[:, BLK - 1 : BLK] - row))
            grad_values = near_values_buf[head, part, :].astype(F32) + mm(
                scaled_keys_ref[head, part, :], end_grad
            )
            grad_keys = near_keys_buf[head, part, :].astype(F32) + factor * mm_nt(
                values_ref[0, part, lanes(head)], end_grad
            )
            d_values_buf[head, part, :] = grad_values.astype(BF16)
            d_keys_buf[head, part, :] = grad_keys.astype(BF16)

    over_heads(fetch, body, leave)


def shape(dims, kind):
    return jax.ShapeDtypeStruct(dims, kind)


HBM = pl.BlockSpec(memory_space=pltpu.HBM)
SMEM = pl.BlockSpec(memory_space=pltpu.SMEM)
VMEM = pl.BlockSpec(memory_space=pltpu.VMEM)
WIDE = shape((1, ROWS, COLS), BF16)
HEAD_ROWS = (HL, ROWS, HD)
HEAD_PROMPT = (HL, P_DEV, HD)
HEAD_REPLY = (HL, BLK, HD)
STATE = (HL, HD, HD)
PIECES = (N_SEQ, PIECE, HD)
TWO_PIECES = (N_SEQ, 2 * PIECE, HD)
SENT_PIECES = (N_SEQ, PIECE + PACK, HD)
CUM = (ROWS, HD)
FAR = 100


def call(kernel, name, in_specs, outs, scratch, semaphores, mib, flops, moved, aliases=None):
    return pl.pallas_call(
        kernel,
        in_specs=in_specs,
        out_specs=[spec for spec, _ in outs],
        out_shape=[made for _, made in outs],
        scratch_shapes=[pltpu.VMEM(dims, kind) for dims, kind in scratch]
        + [pltpu.SemaphoreType.DMA((count, HL)) for count in semaphores],
        input_output_aliases=aliases or {},
        compiler_params=pltpu.CompilerParams(vmem_limit_bytes=mib << 20),
        cost_estimate=pl.CostEstimate(
            flops=int(flops), bytes_accessed=int(moved) << 20, transcendentals=0
        ),
        name=name,
    )


def summarize(decay_rows, keys, values):
    return call(
        summary_kernel, "summary", [HBM, HBM, HBM],
        [
            (HBM, shape(SENT_PIECES, BF16)), (VMEM, shape(STATE, F32)),
            (VMEM, shape((HL, ROWS), F32)), (VMEM, shape((HL, 8, HD), F32)),
        ],
        [(HEAD_PROMPT, BF16), (HEAD_PROMPT, BF16), ((1, HL, ROWS), F32), (SENT_PIECES, BF16)],
        [2, 1, 1], 52, 3e8, 4,
    )(decay_rows, keys, values)


def inside(cum_rows, queries, keys, values):
    return call(
        within_kernel, "within", [VMEM] + [HBM] * 3,
        [
            (HBM, shape((FAR, ROWS, HD), BF16)), (HBM, shape(HEAD_PROMPT, BF16)),
            (HBM, shape((FAR // 2, ROWS, BLK), BF16)), (VMEM, shape((8, HD), F32)),
        ],
        [(HEAD_ROWS, BF16)] * 5 + [(HEAD_PROMPT, BF16), ((HL, ROWS, BLK), BF16)],
        [3, 4], 52, 4e9, 16,
    )(cum_rows, queries, keys, values)


def forward_scan(parents, got, after):
    return call(
        forward_scan_kernel, "forward_scan", [SMEM, VMEM, HBM],
        [(VMEM, shape(TWO_PIECES, BF16)), (VMEM, shape((2 * N_SEQ, HD), F32))],
        [], [], 12, 1e6, 1,
    )(parents, got, after)


def attend(ends, gains, d_out, starts, term, within):
    return call(
        attend_kernel, "attend", [VMEM] * 5 + [HBM],
        [
            (VMEM, shape(HEAD_ROWS, BF16)), (VMEM, shape(HEAD_ROWS, BF16)),
            (VMEM, shape((HL, 16, HD), F32)), (HBM, shape((FAR, ROWS, HD), BF16)),
            (HBM, shape((6 * FAR, HD, HD), BF16)),
        ],
        [(HEAD_ROWS, BF16), ((HL * BLOCKS, HD, HD), BF16), (CUM, F32), (CUM, F32)],
        [2, 2], 46, 3e8, 10,
    )(ends, gains, d_out, starts, term, within)


def grads(ends, gains, stats, scaled_queries, d_out, attended):
    return call(
        grad_kernel, "grad", [VMEM] * 6, [(VMEM, shape(TWO_PIECES, BF16))],
        [(CUM, F32), (CUM, F32)], [], 20, 3e8, 10,
    )(ends, gains, stats, scaled_queries, d_out, attended)[0]


def local_grads(
    cum_rows, stats, gains, queries, keys, values, d_out, attended, states, weights
):
    return call(
        local_grads_kernel, "local_grads", [VMEM] * 3 + [HBM] * 7,
        [
            (HBM, WIDE), (HBM, WIDE), (HBM, WIDE), (HBM, WIDE),
            (HBM, shape((4 * FAR, HD, HD), F32)), (VMEM, shape((8, HD), F32)),
        ],
        [(HEAD_ROWS, BF16)] * 5 + [((HL * BLOCKS, HD, HD), BF16), ((HL, ROWS, BLK), BF16)]
        + [(HEAD_ROWS, BF16)] * 4
        + [(STATE, F32), (CUM, F32), (CUM, F32)],
        [7, 5], 53, 6e9, 24,
    )(cum_rows, stats, gains, queries, keys, values, d_out, attended, states, weights)


def far_grads(cum_rows, ends, far, scaled_keys, values, term, near_keys, near_values):
    return call(
        far_grads_kernel, "far_grads", [VMEM] * 5 + [HBM] * 3,
        [(HBM, WIDE), (HBM, WIDE)],
        [(STATE, F32)] + [(HEAD_PROMPT, BF16)] * 4, [3, 2], 44, 3e8, 10, {6: 0, 7: 1},
    )(cum_rows, ends, far, scaled_keys, values, term, near_keys, near_values)


def backward_scan(got, decays, after):
    return call(
        backward_scan_kernel, "backward_scan", [VMEM, VMEM, HBM],
        [(VMEM, shape(PIECES, BF16))], [], [], 12, 1e6, 1,
    )(got, decays, after)[0]


def everyone(array, axis):
    return lax.all_to_all(array, axis, 0, 0, tiled=True)


def local(queries, keys, values, log_decay, gain, parents, d_out):
    gains = gain.reshape(HL, HD)
    decay_rows = jnp.swapaxes(log_decay, 1, 2)
    send, first_term, cum_rows, block_ends = summarize(decay_rows, keys, values)
    got = everyone(send, "seq")
    within, scaled_keys, weights, done = inside(cum_rows, queries, keys, values)
    send, decays = forward_scan(parents, got, done)
    starts = everyone(send, "seq")
    near_queries, attended, stats, kept, states = attend(
        block_ends, gains, d_out, starts, first_term, within
    )
    stats = everyone(stats, "head")
    send = grads(block_ends, gains, stats, near_queries, d_out, attended)
    got = everyone(send, "seq")
    out, d_queries, d_keys, d_values, last_term, done = local_grads(
        cum_rows, stats, gains, queries, keys, values, d_out, kept, states, weights
    )
    far = everyone(backward_scan(got, decays, done), "seq")
    d_keys, d_values = far_grads(
        cum_rows, block_ends, far, scaled_keys, values, last_term, d_keys, d_values
    )
    return (out, d_queries, d_keys, d_values)


def solution(mesh):
    cut = P("seq", None, "head")
    return jax.shard_map(
        local,
        mesh=mesh,
        in_specs=(cut, cut, cut, cut, P("head"), P(), cut),
        out_specs=(cut, cut, cut, cut),
        check_vma=False,
    )
```

```python
import jax
import jax.numpy as jnp
from jax import lax
from jax.experimental import pallas as pl
from jax.experimental.pallas import tpu as pltpu
from jax.sharding import PartitionSpec as P

H = 64
HD = 128
BLK = 256
PROMPTS = 2
P_DEV = 512
ROWS = 768
HL = 8
N_SEQ = 32
SPAN = N_SEQ // PROMPTS
COLS = HL * HD
PIECE = HL * HD // N_SEQ
PARTS = HD // PIECE
PACK = 8
BLOCKS = ROWS // BLK
TILES = ROWS // HD
EPS = 1e-05
GROUP = 2

F32 = jnp.float32
BF16 = jnp.bfloat16


def dot(a, b, dims):
    return lax.dot_general(a, b, (dims, ((), ())), preferred_element_type=F32)


def mm(a, b):
    return dot(a, b, ((1,), (0,)))


def mm_nt(a, b):
    return dot(a, b, ((1,), (1,)))


def mm_tn(a, b):
    return dot(a, b, ((0,), (0,)))


def rows(number):
    return slice(number * BLK, (number + 1) * BLK)


def tile_rows(tile):
    return slice(tile * HD, (tile + 1) * HD)


def down(row):
    return jnp.broadcast_to(row, (HD, BLK)).T


def twice(block):
    return jnp.concatenate([block, block], axis=1)


def rounded_product(block, factor):
    return (block.astype(F32) * factor).astype(BF16)


def lanes(head):
    return pl.ds(pl.multiple_of(head * HD, HD), HD)


def of_rows(ref, count=ROWS, first=0):
    if len(ref.shape) == 3:
        return lambda head: ref.at[0, pl.ds(first, count), lanes(head)]
    return lambda head: ref.at[pl.ds(first, count), lanes(head)]


def of_lead(ref, count=1, first=0):
    if count == 1:
        return lambda head: ref.at[head + first]
    return lambda head: ref.at[pl.ds(head * count, count)]


class Copies:
    def __init__(self, pairs, sems):
        self.pairs, self.sems = pairs, sems

    def each(self, head):
        return [
            pltpu.make_async_copy(src(head), dst(head), self.sems.at[number, head])
            for number, (src, dst) in enumerate(self.pairs)
        ]

    def start(self, head):
        for copy in self.each(head):
            copy.start()

    def begin(self):
        for head in range(HL):
            self.start(head)

    def wait(self, head):
        for copy in self.each(head):
            copy.wait()


def over_heads(fetch, body, leave=None, started=False, group=GROUP):
    if fetch is not None and not started:
        fetch.begin()

    def step(number, carry):
        heads = [number * group + place for place in range(group)]
        for head in heads:
            if fetch is not None:
                fetch.wait(head)
        for head in heads:
            body(head)
        for head in heads:
            if leave is not None:
                leave.start(head)
        return carry

    lax.fori_loop(0, HL // group, step, 0)
    if leave is not None:
        for head in range(HL):
            leave.wait(head)


def split(value):
    coarse = value.astype(BF16)
    rest = value - coarse.astype(F32)
    middle = rest.astype(BF16)
    return coarse, middle, (rest - middle.astype(F32)).astype(BF16)


def summary_kernel(
    decay_ref, keys_ref, values_ref,
    send_ref, term_ref, cum_rows_ref, ends_ref,
    keys_buf, values_buf, decay_buf, send_buf, in_sems, out_sems, decay_sem,
):
    fetch = Copies(
        [
            (of_rows(keys_ref, P_DEV), of_lead(keys_buf)),
            (of_rows(values_ref, P_DEV), of_lead(values_buf)),
        ],
        in_sems,
    )
    leave = Copies([(of_lead(send_buf, PARTS), of_lead(send_ref, PARTS))], out_sems)
    decay_copy = pltpu.make_async_copy(decay_ref, decay_buf, decay_sem.at[0, 0])
    decay_copy.start()
    fetch.begin()
    before = lax.broadcasted_iota(jnp.int32, (BLK, BLK), 0)
    after = lax.broadcasted_iota(jnp.int32, (BLK, BLK), 1)
    upper = jnp.where(before <= after, 1.0, 0.0).astype(BF16)
    decay_copy.wait()
    stacked = jnp.concatenate(
        [decay_buf[0, :, rows(number)] for number in range(BLOCKS)], axis=0
    )
    coarse, middle, fine = (mm(part, upper) for part in split(stacked))
    cumulative = (fine + middle) + coarse
    for number in range(BLOCKS):
        total = cumulative[number * HL : (number + 1) * HL]
        cum_rows_ref[:, rows(number)] = total
        ends_ref[:, number, :] = jnp.broadcast_to(jnp.exp(total[:, BLK - 1 : BLK]), (HL, HD))
    row_ids = lax.broadcasted_iota(jnp.int32, (PACK, HD), 0)

    def body(head):
        terms = []
        for number in range(2):
            row = cum_rows_ref[pl.ds(head, 1), rows(number)]
            factor = jnp.exp(row[:, BLK - 1 : BLK] - row)
            turned = keys_buf[head, rows(number), :].T
            key_scaled = rounded_product(turned, factor)
            terms.append(mm(key_scaled, values_buf[head, rows(number), :]))
        term_ref[head] = terms[0]
        end_decays = ends_ref[head]
        summary = end_decays[1:2, :] * terms[0] + terms[1]
        decay = jnp.broadcast_to(end_decays[0:1, :] * end_decays[1:2, :], (PACK, HD))
        coarse, middle, _ = split(decay)
        packed = jnp.where(
            row_ids == 0, coarse.astype(F32), jnp.where(row_ids == 1, middle.astype(F32), 0.0)
        ).astype(BF16)
        for piece in range(PARTS):
            at = head * PARTS + piece
            send_buf[at, 0:PIECE, :] = summary[piece * PIECE : (piece + 1) * PIECE].astype(BF16)
            send_buf[at, PIECE : PIECE + PACK, :] = packed

    over_heads(fetch, body, leave, started=True, group=4)


def within_kernel(
    cum_rows_ref, queries_ref, keys_ref, values_ref,
    within_ref, scaled_keys_ref, weights_ref, done_ref,
    queries_buf, keys_buf, values_buf, within_buf, scaled_queries_buf, scaled_keys_buf,
    weights_buf, in_sems, out_sems,
):
    fetch = Copies(
        [
            (of_rows(queries_ref), of_lead(queries_buf)),
            (of_rows(keys_ref), of_lead(keys_buf)),
            (of_rows(values_ref), of_lead(values_buf)),
        ],
        in_sems,
    )
    leave = Copies(
        [
            (of_lead(within_buf), of_lead(within_ref)),
            (of_lead(scaled_queries_buf), of_lead(within_ref, first=HL)),
            (of_lead(scaled_keys_buf), of_lead(scaled_keys_ref)),
            (of_lead(weights_buf), of_lead(weights_ref)),
        ],
        out_sems,
    )
    done_ref[...] = jnp.zeros_like(done_ref)
    row_ids = lax.broadcasted_iota(jnp.int32, (BLK, BLK), 0)
    col_ids = lax.broadcasted_iota(jnp.int32, (BLK, BLK), 1)

    def body(head):
        for number in range(BLOCKS):
            part = rows(number)
            queries = queries_buf[head, part, :]
            keys = keys_buf[head, part, :]
            row = cum_rows_ref[pl.ds(head, 1), part]
            values = values_buf[head, part, :]
            if number < 2:
                gaps = twice(down(row)) - row
                mask = jnp.where(row_ids >= col_ids, jnp.exp(gaps), 0.0)
                weights = (mm_nt(queries, keys) * mask).astype(BF16)
                within = mm(weights, values)
            else:
                gaps = row - twice(down(row))
                mask = jnp.where(col_ids >= row_ids, jnp.exp(gaps), 0.0)
                weights = (mm_nt(keys, queries) * mask).astype(BF16)
                weights_buf[head] = weights
                within = mm_tn(weights, values)
            within_buf[head, part, :] = within.astype(BF16)
            scaled_queries_buf[head, part, :] = rounded_product(queries, down(jnp.exp(row)))
            if number < 2:
                factor = down(jnp.exp(row[:, BLK - 1 : BLK] - row))
                scaled_keys_buf[head, part, :] = rounded_product(keys, factor)

    over_heads(fetch, body, leave, group=4)


def forward_scan_kernel(parents_ref, got_ref, _after, send_ref, decay_ref):
    totals = []
    for prompt in range(PROMPTS):
        carry = jnp.zeros((PIECE, HD), F32)
        for index in range(prompt * SPAN, (prompt + 1) * SPAN):
            packed = got_ref[index, PIECE : PIECE + PACK, :].astype(F32)
            decay = packed[0:1, :] + packed[1:2, :]
            decay_ref[index : index + 1, :] = decay
            send_ref[index, 0:PIECE, :] = carry.astype(BF16)
            carry = decay * carry + got_ref[index, 0:PIECE, :].astype(F32)
        totals.append(carry)
    for index in range(N_SEQ):
        prompt = parents_ref[index] // SPAN
        chosen = jnp.where(prompt == 0, totals[0], totals[1])
        decay_ref[N_SEQ + index : N_SEQ + index + 1, :] = jnp.full((1, HD), prompt, F32)
        send_ref[index, PIECE : 2 * PIECE, :] = chosen.astype(BF16)


def attend_kernel(
    ends_ref, gain_ref, d_out_ref, starts_ref, term_ref, within_ref,
    queries_ref, attended_ref, stats_ref, kept_ref, states_ref,
    within_buf, states_buf, squares_ref, products_ref, in_sems, out_sems,
):
    fetch = Copies(
        [
            (of_lead(within_ref, first=HL), of_lead(queries_ref)),
            (of_lead(within_ref), of_lead(within_buf)),
        ],
        in_sems,
    )
    leave = Copies(
        [
            (of_lead(attended_ref), of_lead(kept_ref)),
            (of_lead(states_buf, BLOCKS), of_lead(states_ref, BLOCKS)),
        ],
        out_sems,
    )
    fetch.begin()
    squares_ref[...] = jnp.zeros_like(squares_ref)
    products_ref[...] = jnp.zeros_like(products_ref)

    def body(head):
        got = starts_ref[pl.ds(head * PARTS, PARTS)]
        first = got[:, 0:PIECE, :].reshape(HD, HD)
        reply = got[:, PIECE : 2 * PIECE, :].reshape(HD, HD)
        end_decay = ends_ref[head][0:1, :]
        second = (end_decay * first.astype(F32) + term_ref[head]).astype(BF16)
        gain = gain_ref[pl.ds(head, 1), :]
        for number, start in enumerate((first, second, reply)):
            part = rows(number)
            states_buf[head * BLOCKS + number] = start
            attended = within_buf[head, part, :].astype(F32) + mm(
                queries_ref[head, part, :], start
            )
            attended_ref[head, part, :] = attended.astype(BF16)
            weighted = gain * d_out_ref[0, part, lanes(head)].astype(F32)
            squares_ref[part, :] += attended * attended
            products_ref[part, :] += weighted * attended

    over_heads(fetch, body, leave, started=True)
    stats_ref[...] = jnp.zeros_like(stats_ref)
    for tile in range(TILES):
        for base, sums_ref in ((0, squares_ref), (8, products_ref)):
            row = jnp.sum(sums_ref[tile_rows(tile), :].T, axis=0, keepdims=True)
            stats_ref[:, base + tile : base + tile + 1, :] = jnp.broadcast_to(
                row[None], (HL, 1, HD)
            )


def row_factors(stats_ref, inverse_ref, slope_ref):
    total = stats_ref[0]
    for source in range(1, HL):
        total = total + stats_ref[source]
    turned = jnp.concatenate([total, jnp.zeros((HD - 16, HD), F32)], axis=0).T
    for tile in range(TILES):
        squares = turned[:, tile : tile + 1]
        products = turned[:, 8 + tile : 9 + tile]
        inverse = lax.rsqrt(squares / (H * HD) + EPS)
        slope = inverse * inverse * inverse * products / (H * HD)
        inverse_ref[tile_rows(tile), :] = jnp.broadcast_to(inverse, (HD, HD))
        slope_ref[tile_rows(tile), :] = jnp.broadcast_to(slope, (HD, HD))


def grad_kernel(
    ends_ref, gain_ref, stats_ref, queries_ref, d_out_ref, attended_ref,
    send_ref, inverse_ref, slope_ref,
):
    row_factors(stats_ref, inverse_ref, slope_ref)

    def body(head):
        gain = gain_ref[pl.ds(head, 1), :]
        terms = []
        for number in range(BLOCKS):
            part = rows(number)
            weighted = gain * d_out_ref[0, part, lanes(head)].astype(F32)
            grad = (
                inverse_ref[part, :] * weighted
                - attended_ref[head, part, :].astype(F32) * slope_ref[part, :]
            ).astype(BF16)
            terms.append(mm_tn(queries_ref[head, part, :], grad))
        local_sum = ends_ref[head][0:1, :] * terms[1] + terms[0]
        for piece in range(PARTS):
            at = head * PARTS + piece
            part = slice(piece * PIECE, (piece + 1) * PIECE)
            send_ref[at, 0:PIECE, :] = local_sum[part].astype(BF16)
            send_ref[at, PIECE : 2 * PIECE, :] = terms[2][part].astype(BF16)

    over_heads(None, body, group=HL)


def backward_scan_kernel(got_ref, decay_ref, _after, send_ref):
    branches = [jnp.zeros((PIECE, HD), F32) for _ in range(PROMPTS)]
    for index in range(N_SEQ):
        prompt = decay_ref[N_SEQ + index : N_SEQ + index + 1, :]
        start_grad = got_ref[index, PIECE : 2 * PIECE, :].astype(F32)
        for each in range(PROMPTS):
            branches[each] = branches[each] + jnp.where(prompt == each, start_grad, 0.0)
    for prompt in range(PROMPTS):
        carry = branches[prompt]
        for index in reversed(range(prompt * SPAN, (prompt + 1) * SPAN)):
            send_ref[index] = carry.astype(BF16)
            carry = decay_ref[index : index + 1, :] * carry + got_ref[index, 0:PIECE, :].astype(F32)


def local_grads_kernel(
    cum_rows_ref, stats_ref, gain_ref,
    queries_ref, keys_ref, values_ref, d_out_ref, attended_ref, states_ref, weights_ref,
    out_ref, d_queries_ref, d_keys_ref, d_values_ref, term_ref, done_ref,
    queries_buf, keys_buf, values_buf, d_out_buf, attended_buf, states_buf, weights_buf,
    out_buf, d_queries_buf, d_keys_buf, d_values_buf, term_buf,
    inverse_ref, slope_ref, in_sems, out_sems,
):
    fetch = Copies(
        [
            (of_rows(d_out_ref), of_lead(d_out_buf)),
            (of_lead(attended_ref), of_lead(attended_buf)),
            (of_rows(queries_ref), of_lead(queries_buf)),
            (of_rows(keys_ref), of_lead(keys_buf)),
            (of_rows(values_ref), of_lead(values_buf)),
            (of_lead(states_ref, BLOCKS), of_lead(states_buf, BLOCKS)),
            (of_lead(weights_ref), of_lead(weights_buf)),
        ],
        in_sems,
    )
    leave = Copies(
        [
            (of_lead(out_buf), of_rows(out_ref)),
            (of_lead(d_queries_buf), of_rows(d_queries_ref)),
            (of_lead(d_keys_buf), of_rows(d_keys_ref)),
            (of_lead(d_values_buf), of_rows(d_values_ref)),
            (of_lead(term_buf), of_lead(term_ref)),
        ],
        out_sems,
    )
    fetch.begin()
    done_ref[...] = jnp.zeros_like(done_ref)
    row_factors(stats_ref, inverse_ref, slope_ref)
    row_ids = lax.broadcasted_iota(jnp.int32, (BLK, BLK), 0)
    col_ids = lax.broadcasted_iota(jnp.int32, (BLK, BLK), 1)

    def body(head):
        gain = gain_ref[pl.ds(head, 1), :]
        for number in range(BLOCKS):
            part = rows(number)
            queries = queries_buf[head, part, :]
            keys = keys_buf[head, part, :]
            values = values_buf[head, part, :]
            attended = attended_buf[head, part, :].astype(F32)
            inverse = inverse_ref[part, :]
            weighted = gain * d_out_buf[head, part, :].astype(F32)
            grad = (inverse * weighted - attended * slope_ref[part, :]).astype(BF16)
            out_buf[head, part, :] = (attended * inverse * gain).astype(BF16)
            row = cum_rows_ref[pl.ds(head, 1), part]
            gaps = row - twice(down(row))
            mask = jnp.where(col_ids >= row_ids, jnp.exp(gaps), 0.0)
            if number < 2:
                weights = (mm_nt(keys, queries) * mask).astype(BF16)
            else:
                weights = weights_buf[head]
            score_grad = (mm_nt(values, grad) * mask).astype(BF16)
            growth = down(jnp.exp(row))
            start = states_buf[head * BLOCKS + number]
            grad_queries = mm_tn(score_grad, keys) + growth * mm_nt(grad, start)
            d_queries_buf[head, part, :] = grad_queries.astype(BF16)
            if number == 1:
                term_buf[head] = mm_tn(rounded_product(queries, growth), grad)
            d_keys_buf[head, part, :] = mm(score_grad, queries).astype(BF16)
            d_values_buf[head, part, :] = mm(weights, grad).astype(BF16)

    over_heads(fetch, body, leave, started=True)


def far_grads_kernel(
    cum_rows_ref, ends_ref, far_ref, scaled_keys_ref, values_ref, term_ref,
    near_keys_ref, near_values_ref, d_keys_ref, d_values_ref,
    term_buf, near_keys_buf, near_values_buf, d_keys_buf, d_values_buf, in_sems, out_sems,
):
    fetch = Copies(
        [
            (of_lead(term_ref), of_lead(term_buf)),
            (of_rows(near_keys_ref, P_DEV), of_lead(near_keys_buf)),
            (of_rows(near_values_ref, P_DEV), of_lead(near_values_buf)),
        ],
        in_sems,
    )
    leave = Copies(
        [
            (of_lead(d_keys_buf), of_rows(d_keys_ref, P_DEV)),
            (of_lead(d_values_buf), of_rows(d_values_ref, P_DEV)),
        ],
        out_sems,
    )

    def body(head):
        second = far_ref[pl.ds(head * PARTS, PARTS)].reshape(HD, HD)
        first = (ends_ref[head][1:2, :] * second.astype(F32) + term_buf[head]).astype(BF16)
        for number, end_grad in enumerate((first, second)):
            part = rows(number)
            row = cum_rows_ref[pl.ds(head, 1), part]
            factor = down(jnp.exp(row[:, BLK - 1 : BLK] - row))
            grad_values = near_values_buf[head, part, :].astype(F32) + mm(
                scaled_keys_ref[head, part, :], end_grad
            )
            grad_keys = near_keys_buf[head, part, :].astype(F32) + factor * mm_nt(
                values_ref[0, part, lanes(head)], end_grad
            )
            d_values_buf[head, part, :] = grad_values.astype(BF16)
            d_keys_buf[head, part, :] = grad_keys.astype(BF16)

    over_heads(fetch, body, leave)


def shape(dims, kind):
    return jax.ShapeDtypeStruct(dims, kind)


HBM = pl.BlockSpec(memory_space=pltpu.HBM)
SMEM = pl.BlockSpec(memory_space=pltpu.SMEM)
VMEM = pl.BlockSpec(memory_space=pltpu.VMEM)
WIDE = shape((1, ROWS, COLS), BF16)
HEAD_ROWS = (HL, ROWS, HD)
HEAD_PROMPT = (HL, P_DEV, HD)
HEAD_REPLY = (HL, BLK, HD)
STATE = (HL, HD, HD)
PIECES = (N_SEQ, PIECE, HD)
TWO_PIECES = (N_SEQ, 2 * PIECE, HD)
SENT_PIECES = (N_SEQ, PIECE + PACK, HD)
CUM = (ROWS, HD)
FAR = 100


def call(kernel, name, in_specs, outs, scratch, semaphores, mib, flops, moved, aliases=None):
    return pl.pallas_call(
        kernel,
        in_specs=in_specs,
        out_specs=[spec for spec, _ in outs],
        out_shape=[made for _, made in outs],
        scratch_shapes=[pltpu.VMEM(dims, kind) for dims, kind in scratch]
        + [pltpu.SemaphoreType.DMA((count, HL)) for count in semaphores],
        input_output_aliases=aliases or {},
        compiler_params=pltpu.CompilerParams(vmem_limit_bytes=mib << 20),
        cost_estimate=pl.CostEstimate(
            flops=int(flops), bytes_accessed=int(moved) << 20, transcendentals=0
        ),
        name=name,
    )


def summarize(decay_rows, keys, values):
    return call(
        summary_kernel, "summary", [HBM, HBM, HBM],
        [
            (HBM, shape(SENT_PIECES, BF16)), (VMEM, shape(STATE, F32)),
            (VMEM, shape((HL, ROWS), F32)), (VMEM, shape((HL, 8, HD), F32)),
        ],
        [(HEAD_PROMPT, BF16), (HEAD_PROMPT, BF16), ((1, HL, ROWS), F32), (SENT_PIECES, BF16)],
        [2, 1, 1], 52, 3e8, 4,
    )(decay_rows, keys, values)


def inside(cum_rows, queries, keys, values):
    return call(
        within_kernel, "within", [VMEM] + [HBM] * 3,
        [
            (HBM, shape((FAR, ROWS, HD), BF16)), (HBM, shape(HEAD_PROMPT, BF16)),
            (HBM, shape((FAR * 3 // 2, BLK, BLK), BF16)), (VMEM, shape((8, HD), F32)),
        ],
        [(HEAD_ROWS, BF16)] * 5 + [(HEAD_PROMPT, BF16), ((HL, BLK, BLK), BF16)],
        [3, 4], 52, 4e9, 16,
    )(cum_rows, queries, keys, values)


def forward_scan(parents, got, after):
    return call(
        forward_scan_kernel, "forward_scan", [SMEM, VMEM, HBM],
        [(VMEM, shape(TWO_PIECES, BF16)), (VMEM, shape((2 * N_SEQ, HD), F32))],
        [], [], 12, 1e6, 1,
    )(parents, got, after)


def attend(ends, gains, d_out, starts, term, within):
    return call(
        attend_kernel, "attend", [VMEM] * 5 + [HBM],
        [
            (VMEM, shape(HEAD_ROWS, BF16)), (VMEM, shape(HEAD_ROWS, BF16)),
            (VMEM, shape((HL, 16, HD), F32)), (HBM, shape((FAR, ROWS, HD), BF16)),
            (HBM, shape((6 * FAR, HD, HD), BF16)),
        ],
        [(HEAD_ROWS, BF16), ((HL * BLOCKS, HD, HD), BF16), (CUM, F32), (CUM, F32)],
        [2, 2], 46, 3e8, 10,
    )(ends, gains, d_out, starts, term, within)


def grads(ends, gains, stats, scaled_queries, d_out, attended):
    return call(
        grad_kernel, "grad", [VMEM] * 6, [(VMEM, shape(TWO_PIECES, BF16))],
        [(CUM, F32), (CUM, F32)], [], 20, 3e8, 10,
    )(ends, gains, stats, scaled_queries, d_out, attended)[0]


def local_grads(
    cum_rows, stats, gains, queries, keys, values, d_out, attended, states, weights
):
    return call(
        local_grads_kernel, "local_grads", [VMEM] * 3 + [HBM] * 7,
        [
            (HBM, WIDE), (HBM, WIDE), (HBM, WIDE), (HBM, WIDE),
            (HBM, shape((4 * FAR, HD, HD), F32)), (VMEM, shape((8, HD), F32)),
        ],
        [(HEAD_ROWS, BF16)] * 5 + [((HL * BLOCKS, HD, HD), BF16), ((HL, BLK, BLK), BF16)]
        + [(HEAD_ROWS, BF16)] * 4
        + [(STATE, F32), (CUM, F32), (CUM, F32)],
        [7, 5], 53, 6e9, 24,
    )(cum_rows, stats, gains, queries, keys, values, d_out, attended, states, weights)


def far_grads(cum_rows, ends, far, scaled_keys, values, term, near_keys, near_values):
    return call(
        far_grads_kernel, "far_grads", [VMEM] * 5 + [HBM] * 3,
        [(HBM, WIDE), (HBM, WIDE)],
        [(STATE, F32)] + [(HEAD_PROMPT, BF16)] * 4, [3, 2], 44, 3e8, 10, {6: 0, 7: 1},
    )(cum_rows, ends, far, scaled_keys, values, term, near_keys, near_values)


def backward_scan(got, decays, after):
    return call(
        backward_scan_kernel, "backward_scan", [VMEM, VMEM, HBM],
        [(VMEM, shape(PIECES, BF16))], [], [], 12, 1e6, 1,
    )(got, decays, after)[0]


def everyone(array, axis):
    return lax.all_to_all(array, axis, 0, 0, tiled=True)


def local(queries, keys, values, log_decay, gain, parents, d_out):
    gains = gain.reshape(HL, HD)
    decay_rows = jnp.swapaxes(log_decay, 1, 2)
    send, first_term, cum_rows, block_ends = summarize(decay_rows, keys, values)
    got = everyone(send, "seq")
    within, scaled_keys, weights, done = inside(cum_rows, queries, keys, values)
    send, decays = forward_scan(parents, got, done)
    starts = everyone(send, "seq")
    near_queries, attended, stats, kept, states = attend(
        block_ends, gains, d_out, starts, first_term, within
    )
    stats = everyone(stats, "head")
    send = grads(block_ends, gains, stats, near_queries, d_out, attended)
    got = everyone(send, "seq")
    out, d_queries, d_keys, d_values, last_term, done = local_grads(
        cum_rows, stats, gains, queries, keys, values, d_out, kept, states, weights
    )
    far = everyone(backward_scan(got, decays, done), "seq")
    d_keys, d_values = far_grads(
        cum_rows, block_ends, far, scaled_keys, values, last_term, d_keys, d_values
    )
    return (out, d_queries, d_keys, d_values)


def solution(mesh):
    cut = P("seq", None, "head")
    return jax.shard_map(
        local,
        mesh=mesh,
        in_specs=(cut, cut, cut, cut, P("head"), P(), cut),
        out_specs=(cut, cut, cut, cut),
        check_vma=False,
    )
```

```python
import jax
import jax.numpy as jnp
from jax import lax
from jax.experimental import pallas as pl
from jax.experimental.pallas import tpu as pltpu
from jax.sharding import PartitionSpec as P

H = 64
HD = 128
BLK = 256
PROMPTS = 2
P_DEV = 512
ROWS = 768
HL = 8
N_SEQ = 32
SPAN = N_SEQ // PROMPTS
COLS = HL * HD
PIECE = HL * HD // N_SEQ
PARTS = HD // PIECE
PACK = 8
BLOCKS = ROWS // BLK
TILES = ROWS // HD
EPS = 1e-05
GROUP = 2

F32 = jnp.float32
BF16 = jnp.bfloat16


def dot(a, b, dims):
    return lax.dot_general(a, b, (dims, ((), ())), preferred_element_type=F32)


def mm(a, b):
    return dot(a, b, ((1,), (0,)))


def mm_nt(a, b):
    return dot(a, b, ((1,), (1,)))


def mm_tn(a, b):
    return dot(a, b, ((0,), (0,)))


def rows(number):
    return slice(number * BLK, (number + 1) * BLK)


def tile_rows(tile):
    return slice(tile * HD, (tile + 1) * HD)


def down(row):
    return jnp.broadcast_to(row, (HD, BLK)).T


def twice(block):
    return jnp.concatenate([block, block], axis=1)


def rounded_product(block, factor):
    return (block.astype(F32) * factor).astype(BF16)


def lanes(head):
    return pl.ds(pl.multiple_of(head * HD, HD), HD)


def of_rows(ref, count=ROWS, first=0):
    if len(ref.shape) == 3:
        return lambda head: ref.at[0, pl.ds(first, count), lanes(head)]
    return lambda head: ref.at[pl.ds(first, count), lanes(head)]


def of_lead(ref, count=1, first=0):
    if count == 1:
        return lambda head: ref.at[head + first]
    return lambda head: ref.at[pl.ds(head * count, count)]


class Copies:
    def __init__(self, pairs, sems):
        self.pairs, self.sems = pairs, sems

    def each(self, head):
        return [
            pltpu.make_async_copy(src(head), dst(head), self.sems.at[number, head])
            for number, (src, dst) in enumerate(self.pairs)
        ]

    def start(self, head):
        for copy in self.each(head):
            copy.start()

    def begin(self):
        for head in range(HL):
            self.start(head)

    def wait(self, head):
        for copy in self.each(head):
            copy.wait()


def over_heads(fetch, body, leave=None, started=False, group=GROUP):
    if fetch is not None and not started:
        fetch.begin()

    def step(number, carry):
        heads = [number * group + place for place in range(group)]
        for head in heads:
            if fetch is not None:
                fetch.wait(head)
        for head in heads:
            body(head)
        for head in heads:
            if leave is not None:
                leave.start(head)
        return carry

    lax.fori_loop(0, HL // group, step, 0)
    if leave is not None:
        for head in range(HL):
            leave.wait(head)


def split(value):
    coarse = value.astype(BF16)
    rest = value - coarse.astype(F32)
    middle = rest.astype(BF16)
    return coarse, middle, (rest - middle.astype(F32)).astype(BF16)


def summary_kernel(
    decay_ref, keys_ref, values_ref,
    send_ref, term_ref, cum_rows_ref, ends_ref,
    keys_buf, values_buf, decay_buf, send_buf, in_sems, out_sems, decay_sem,
):
    fetch = Copies(
        [
            (of_rows(keys_ref, P_DEV), of_lead(keys_buf)),
            (of_rows(values_ref, P_DEV), of_lead(values_buf)),
        ],
        in_sems,
    )
    leave = Copies([(of_lead(send_buf, PARTS), of_lead(send_ref, PARTS))], out_sems)
    decay_copy = pltpu.make_async_copy(decay_ref, decay_buf, decay_sem.at[0, 0])
    decay_copy.start()
    fetch.begin()
    before = lax.broadcasted_iota(jnp.int32, (BLK, BLK), 0)
    after = lax.broadcasted_iota(jnp.int32, (BLK, BLK), 1)
    upper = jnp.where(before <= after, 1.0, 0.0).astype(BF16)
    decay_copy.wait()
    stacked = jnp.concatenate(
        [decay_buf[0, :, rows(number)] for number in range(BLOCKS)], axis=0
    )
    coarse, middle, fine = (mm(part, upper) for part in split(stacked))
    cumulative = (fine + middle) + coarse
    for number in range(BLOCKS):
        total = cumulative[number * HL : (number + 1) * HL]
        cum_rows_ref[:, rows(number)] = total
        ends_ref[:, number, :] = jnp.broadcast_to(jnp.exp(total[:, BLK - 1 : BLK]), (HL, HD))
    row_ids = lax.broadcasted_iota(jnp.int32, (PACK, HD), 0)

    def body(head):
        terms = []
        for number in range(2):
            row = cum_rows_ref[pl.ds(head, 1), rows(number)]
            factor = jnp.exp(row[:, BLK - 1 : BLK] - row)
            turned = keys_buf[head, rows(number), :].T
            key_scaled = rounded_product(turned, factor)
            terms.append(mm(key_scaled, values_buf[head, rows(number), :]))
        term_ref[head] = terms[0]
        end_decays = ends_ref[head]
        summary = end_decays[1:2, :] * terms[0] + terms[1]
        decay = jnp.broadcast_to(end_decays[0:1, :] * end_decays[1:2, :], (PACK, HD))
        coarse, middle, _ = split(decay)
        packed = jnp.where(
            row_ids == 0, coarse.astype(F32), jnp.where(row_ids == 1, middle.astype(F32), 0.0)
        ).astype(BF16)
        for piece in range(PARTS):
            at = head * PARTS + piece
            send_buf[at, 0:PIECE, :] = summary[piece * PIECE : (piece + 1) * PIECE].astype(BF16)
            send_buf[at, PIECE : PIECE + PACK, :] = packed

    over_heads(fetch, body, leave, started=True, group=4)


def within_kernel(
    cum_rows_ref, queries_ref, keys_ref, values_ref,
    within_ref, scaled_keys_ref, weights_ref, done_ref,
    queries_buf, keys_buf, values_buf, within_buf, scaled_queries_buf, scaled_keys_buf,
    weights_buf, in_sems, out_sems,
):
    fetch = Copies(
        [
            (of_rows(queries_ref), of_lead(queries_buf)),
            (of_rows(keys_ref), of_lead(keys_buf)),
            (of_rows(values_ref), of_lead(values_buf)),
        ],
        in_sems,
    )
    leave = Copies(
        [
            (of_lead(within_buf), of_lead(within_ref)),
            (of_lead(scaled_queries_buf), of_lead(within_ref, first=HL)),
            (of_lead(scaled_keys_buf), of_lead(scaled_keys_ref)),
            (of_lead(weights_buf), of_lead(weights_ref)),
        ],
        out_sems,
    )
    done_ref[...] = jnp.zeros_like(done_ref)
    row_ids = lax.broadcasted_iota(jnp.int32, (BLK, BLK), 0)
    col_ids = lax.broadcasted_iota(jnp.int32, (BLK, BLK), 1)

    def body(head):
        for number in range(BLOCKS):
            part = rows(number)
            queries = queries_buf[head, part, :]
            keys = keys_buf[head, part, :]
            row = cum_rows_ref[pl.ds(head, 1), part]
            values = values_buf[head, part, :]
            if number < 2:
                gaps = twice(down(row)) - row
                mask = jnp.where(row_ids >= col_ids, jnp.exp(gaps), 0.0)
                weights = (mm_nt(queries, keys) * mask).astype(BF16)
                within = mm(weights, values)
            else:
                gaps = row - twice(down(row))
                mask = jnp.where(col_ids >= row_ids, jnp.exp(gaps), 0.0)
                weights = (mm_nt(keys, queries) * mask).astype(BF16)
                weights_buf[head] = weights
                within = mm_tn(weights, values)
            within_buf[head, part, :] = within.astype(BF16)
            scaled_queries_buf[head, part, :] = rounded_product(queries, down(jnp.exp(row)))
            if number < 2:
                factor = down(jnp.exp(row[:, BLK - 1 : BLK] - row))
                scaled_keys_buf[head, part, :] = rounded_product(keys, factor)

    over_heads(fetch, body, leave, group=4)


def forward_scan_kernel(parents_ref, got_ref, _after, send_ref, decay_ref):
    totals = []
    for prompt in range(PROMPTS):
        carry = jnp.zeros((PIECE, HD), F32)
        for index in range(prompt * SPAN, (prompt + 1) * SPAN):
            packed = got_ref[index, PIECE : PIECE + PACK, :].astype(F32)
            decay = packed[0:1, :] + packed[1:2, :]
            decay_ref[index : index + 1, :] = decay
            send_ref[index, 0:PIECE, :] = carry.astype(BF16)
            carry = decay * carry + got_ref[index, 0:PIECE, :].astype(F32)
        totals.append(carry)
    for index in range(N_SEQ):
        prompt = parents_ref[index] // SPAN
        chosen = jnp.where(prompt == 0, totals[0], totals[1])
        decay_ref[N_SEQ + index : N_SEQ + index + 1, :] = jnp.full((1, HD), prompt, F32)
        send_ref[index, PIECE : 2 * PIECE, :] = chosen.astype(BF16)


def attend_kernel(
    ends_ref, gain_ref, d_out_ref, starts_ref, term_ref, within_ref,
    queries_ref, attended_ref, stats_ref, kept_ref, states_ref,
    within_buf, states_buf, squares_ref, products_ref, in_sems, out_sems,
):
    fetch = Copies(
        [
            (of_lead(within_ref, first=HL), of_lead(queries_ref)),
            (of_lead(within_ref), of_lead(within_buf)),
        ],
        in_sems,
    )
    leave = Copies(
        [
            (of_lead(attended_ref), of_lead(kept_ref)),
            (of_lead(states_buf, BLOCKS), of_lead(states_ref, BLOCKS)),
        ],
        out_sems,
    )
    fetch.begin()
    squares_ref[...] = jnp.zeros_like(squares_ref)
    products_ref[...] = jnp.zeros_like(products_ref)

    def body(head):
        got = starts_ref[pl.ds(head * PARTS, PARTS)]
        first = got[:, 0:PIECE, :].reshape(HD, HD)
        reply = got[:, PIECE : 2 * PIECE, :].reshape(HD, HD)
        end_decay = ends_ref[head][0:1, :]
        second = (end_decay * first.astype(F32) + term_ref[head]).astype(BF16)
        gain = gain_ref[pl.ds(head, 1), :]
        for number, start in enumerate((first, second, reply)):
            part = rows(number)
            states_buf[head * BLOCKS + number] = start
            attended = within_buf[head, part, :].astype(F32) + mm(
                queries_ref[head, part, :], start
            )
            attended_ref[head, part, :] = attended.astype(BF16)
            weighted = gain * d_out_ref[0, part, lanes(head)].astype(F32)
            squares_ref[part, :] += attended * attended
            products_ref[part, :] += weighted * attended

    over_heads(fetch, body, leave, started=True)
    stats_ref[...] = jnp.zeros_like(stats_ref)
    for tile in range(TILES):
        for base, sums_ref in ((0, squares_ref), (8, products_ref)):
            row = jnp.sum(sums_ref[tile_rows(tile), :].T, axis=0, keepdims=True)
            stats_ref[:, base + tile : base + tile + 1, :] = jnp.broadcast_to(
                row[None], (HL, 1, HD)
            )


def row_factors(stats_ref, inverse_ref, slope_ref):
    total = stats_ref[0]
    for source in range(1, HL):
        total = total + stats_ref[source]
    turned = jnp.concatenate([total, jnp.zeros((HD - 16, HD), F32)], axis=0).T
    for tile in range(TILES):
        squares = turned[:, tile : tile + 1]
        products = turned[:, 8 + tile : 9 + tile]
        inverse = lax.rsqrt(squares / (H * HD) + EPS)
        slope = inverse * inverse * inverse * products / (H * HD)
        inverse_ref[tile_rows(tile), :] = jnp.broadcast_to(inverse, (HD, HD))
        slope_ref[tile_rows(tile), :] = jnp.broadcast_to(slope, (HD, HD))


def grad_kernel(
    ends_ref, gain_ref, stats_ref, queries_ref, d_out_ref, attended_ref,
    send_ref, inverse_ref, slope_ref,
):
    row_factors(stats_ref, inverse_ref, slope_ref)

    def body(head):
        gain = gain_ref[pl.ds(head, 1), :]
        terms = []
        for number in range(BLOCKS):
            part = rows(number)
            weighted = gain * d_out_ref[0, part, lanes(head)].astype(F32)
            grad = (
                inverse_ref[part, :] * weighted
                - attended_ref[head, part, :].astype(F32) * slope_ref[part, :]
            ).astype(BF16)
            terms.append(mm_tn(queries_ref[head, part, :], grad))
        local_sum = ends_ref[head][0:1, :] * terms[1] + terms[0]
        for piece in range(PARTS):
            at = head * PARTS + piece
            part = slice(piece * PIECE, (piece + 1) * PIECE)
            send_ref[at, 0:PIECE, :] = local_sum[part].astype(BF16)
            send_ref[at, PIECE : 2 * PIECE, :] = terms[2][part].astype(BF16)

    over_heads(None, body, group=HL)


def backward_scan_kernel(got_ref, decay_ref, _after, send_ref):
    branches = [jnp.zeros((PIECE, HD), F32) for _ in range(PROMPTS)]
    for index in range(N_SEQ):
        prompt = decay_ref[N_SEQ + index : N_SEQ + index + 1, :]
        start_grad = got_ref[index, PIECE : 2 * PIECE, :].astype(F32)
        for each in range(PROMPTS):
            branches[each] = branches[each] + jnp.where(prompt == each, start_grad, 0.0)
    for prompt in range(PROMPTS):
        carry = branches[prompt]
        for index in reversed(range(prompt * SPAN, (prompt + 1) * SPAN)):
            send_ref[index] = carry.astype(BF16)
            carry = decay_ref[index : index + 1, :] * carry + got_ref[index, 0:PIECE, :].astype(F32)


def local_grads_kernel(
    cum_rows_ref, stats_ref, gain_ref,
    queries_ref, keys_ref, values_ref, d_out_ref, attended_ref, states_ref, weights_ref,
    out_ref, d_queries_ref, d_keys_ref, d_values_ref, term_ref, done_ref,
    queries_buf, keys_buf, values_buf, d_out_buf, attended_buf, states_buf, weights_buf,
    out_buf, d_queries_buf, d_keys_buf, d_values_buf, term_buf,
    inverse_ref, slope_ref, in_sems, out_sems,
):
    fetch = Copies(
        [
            (of_rows(d_out_ref), of_lead(d_out_buf)),
            (of_lead(attended_ref), of_lead(attended_buf)),
            (of_rows(queries_ref), of_lead(queries_buf)),
            (of_rows(keys_ref), of_lead(keys_buf)),
            (of_rows(values_ref), of_lead(values_buf)),
            (of_lead(states_ref, BLOCKS), of_lead(states_buf, BLOCKS)),
            (of_lead(weights_ref), of_lead(weights_buf)),
        ],
        in_sems,
    )
    leave = Copies(
        [
            (of_lead(out_buf), of_rows(out_ref)),
            (of_lead(d_queries_buf), of_rows(d_queries_ref)),
            (of_lead(d_keys_buf), of_rows(d_keys_ref)),
            (of_lead(d_values_buf), of_rows(d_values_ref)),
            (of_lead(term_buf), of_lead(term_ref)),
        ],
        out_sems,
    )
    fetch.begin()
    done_ref[...] = jnp.zeros_like(done_ref)
    row_factors(stats_ref, inverse_ref, slope_ref)
    row_ids = lax.broadcasted_iota(jnp.int32, (BLK, BLK), 0)
    col_ids = lax.broadcasted_iota(jnp.int32, (BLK, BLK), 1)

    def body(head):
        gain = gain_ref[pl.ds(head, 1), :]
        for number in range(BLOCKS):
            part = rows(number)
            queries = queries_buf[head, part, :]
            keys = keys_buf[head, part, :]
            values = values_buf[head, part, :]
            attended = attended_buf[head, part, :].astype(F32)
            inverse = inverse_ref[part, :]
            weighted = gain * d_out_buf[head, part, :].astype(F32)
            grad = (inverse * weighted - attended * slope_ref[part, :]).astype(BF16)
            out_buf[head, part, :] = (attended * inverse * gain).astype(BF16)
            row = cum_rows_ref[pl.ds(head, 1), part]
            gaps = row - twice(down(row))
            mask = jnp.where(col_ids >= row_ids, jnp.exp(gaps), 0.0)
            if number < 2:
                weights = (mm_nt(keys, queries) * mask).astype(BF16)
            else:
                weights = weights_buf[head]
            score_grad = (mm_nt(values, grad) * mask).astype(BF16)
            growth = down(jnp.exp(row))
            start = states_buf[head * BLOCKS + number]
            grad_queries = mm_tn(score_grad, keys) + growth * mm_nt(grad, start)
            d_queries_buf[head, part, :] = grad_queries.astype(BF16)
            if number == 1:
                term_buf[head] = mm_tn(rounded_product(queries, growth), grad)
            d_keys_buf[head, part, :] = mm(score_grad, queries).astype(BF16)
            d_values_buf[head, part, :] = mm(weights, grad).astype(BF16)

    over_heads(fetch, body, leave, started=True)


def far_grads_kernel(
    cum_rows_ref, ends_ref, far_ref, scaled_keys_ref, values_ref, term_ref,
    near_keys_ref, near_values_ref, d_keys_ref, d_values_ref,
    term_buf, near_keys_buf, near_values_buf, d_keys_buf, d_values_buf, in_sems, out_sems,
):
    fetch = Copies(
        [
            (of_lead(term_ref), of_lead(term_buf)),
            (of_rows(near_keys_ref, P_DEV), of_lead(near_keys_buf)),
            (of_rows(near_values_ref, P_DEV), of_lead(near_values_buf)),
        ],
        in_sems,
    )
    leave = Copies(
        [
            (of_lead(d_keys_buf), of_rows(d_keys_ref, P_DEV)),
            (of_lead(d_values_buf), of_rows(d_values_ref, P_DEV)),
        ],
        out_sems,
    )

    def body(head):
        second = far_ref[pl.ds(head * PARTS, PARTS)].reshape(HD, HD)
        first = (ends_ref[head][1:2, :] * second.astype(F32) + term_buf[head]).astype(BF16)
        for number, end_grad in enumerate((first, second)):
            part = rows(number)
            row = cum_rows_ref[pl.ds(head, 1), part]
            factor = down(jnp.exp(row[:, BLK - 1 : BLK] - row))
            grad_values = near_values_buf[head, part, :].astype(F32) + mm(
                scaled_keys_ref[head, part, :], end_grad
            )
            grad_keys = near_keys_buf[head, part, :].astype(F32) + factor * mm_nt(
                values_ref[0, part, lanes(head)], end_grad
            )
            d_values_buf[head, part, :] = grad_values.astype(BF16)
            d_keys_buf[head, part, :] = grad_keys.astype(BF16)

    over_heads(fetch, body, leave)


def shape(dims, kind):
    return jax.ShapeDtypeStruct(dims, kind)


HBM = pl.BlockSpec(memory_space=pltpu.HBM)
SMEM = pl.BlockSpec(memory_space=pltpu.SMEM)
VMEM = pl.BlockSpec(memory_space=pltpu.VMEM)
WIDE = shape((1, ROWS, COLS), BF16)
HEAD_ROWS = (HL, ROWS, HD)
HEAD_PROMPT = (HL, P_DEV, HD)
HEAD_REPLY = (HL, BLK, HD)
STATE = (HL, HD, HD)
PIECES = (N_SEQ, PIECE, HD)
TWO_PIECES = (N_SEQ, 2 * PIECE, HD)
SENT_PIECES = (N_SEQ, PIECE + PACK, HD)
CUM = (ROWS, HD)
FAR = 100


def call(kernel, name, in_specs, outs, scratch, semaphores, mib, flops, moved, aliases=None):
    return pl.pallas_call(
        kernel,
        in_specs=in_specs,
        out_specs=[spec for spec, _ in outs],
        out_shape=[made for _, made in outs],
        scratch_shapes=[pltpu.VMEM(dims, kind) for dims, kind in scratch]
        + [pltpu.SemaphoreType.DMA((count, HL)) for count in semaphores],
        input_output_aliases=aliases or {},
        compiler_params=pltpu.CompilerParams(vmem_limit_bytes=mib << 20),
        cost_estimate=pl.CostEstimate(
            flops=int(flops), bytes_accessed=int(moved) << 20, transcendentals=0
        ),
        name=name,
    )


def summarize(decay_rows, keys, values):
    return call(
        summary_kernel, "summary", [HBM, HBM, HBM],
        [
            (HBM, shape(SENT_PIECES, BF16)), (VMEM, shape(STATE, F32)),
            (VMEM, shape((HL, ROWS), F32)), (VMEM, shape((HL, 8, HD), F32)),
        ],
        [(HEAD_PROMPT, BF16), (HEAD_PROMPT, BF16), ((1, HL, ROWS), F32), (SENT_PIECES, BF16)],
        [2, 1, 1], 52, 3e8, 4,
    )(decay_rows, keys, values)


def inside(cum_rows, queries, keys, values):
    return call(
        within_kernel, "within", [VMEM] + [HBM] * 3,
        [
            (HBM, shape((FAR, ROWS, HD), BF16)), (HBM, shape(HEAD_PROMPT, BF16)),
            (HBM, shape((FAR * 3 // 2, BLK, BLK), BF16)), (VMEM, shape((8, HD), F32)),
        ],
        [(HEAD_ROWS, BF16)] * 5 + [(HEAD_PROMPT, BF16), ((HL, BLK, BLK), BF16)],
        [3, 4], 53, 4e9, 16,
    )(cum_rows, queries, keys, values)


def forward_scan(parents, got, after):
    return call(
        forward_scan_kernel, "forward_scan", [SMEM, VMEM, HBM],
        [(VMEM, shape(TWO_PIECES, BF16)), (VMEM, shape((2 * N_SEQ, HD), F32))],
        [], [], 12, 1e6, 1,
    )(parents, got, after)


def attend(ends, gains, d_out, starts, term, within):
    return call(
        attend_kernel, "attend", [VMEM] * 5 + [HBM],
        [
            (VMEM, shape(HEAD_ROWS, BF16)), (VMEM, shape(HEAD_ROWS, BF16)),
            (VMEM, shape((HL, 16, HD), F32)), (HBM, shape((FAR, ROWS, HD), BF16)),
            (HBM, shape((6 * FAR, HD, HD), BF16)),
        ],
        [(HEAD_ROWS, BF16), ((HL * BLOCKS, HD, HD), BF16), (CUM, F32), (CUM, F32)],
        [2, 2], 46, 3e8, 10,
    )(ends, gains, d_out, starts, term, within)


def grads(ends, gains, stats, scaled_queries, d_out, attended):
    return call(
        grad_kernel, "grad", [VMEM] * 6, [(VMEM, shape(TWO_PIECES, BF16))],
        [(CUM, F32), (CUM, F32)], [], 20, 3e8, 10,
    )(ends, gains, stats, scaled_queries, d_out, attended)[0]


def local_grads(
    cum_rows, stats, gains, queries, keys, values, d_out, attended, states, weights
):
    return call(
        local_grads_kernel, "local_grads", [VMEM] * 3 + [HBM] * 7,
        [
            (HBM, WIDE), (HBM, WIDE), (HBM, WIDE), (HBM, WIDE),
            (HBM, shape((4 * FAR, HD, HD), F32)), (VMEM, shape((8, HD), F32)),
        ],
        [(HEAD_ROWS, BF16)] * 5 + [((HL * BLOCKS, HD, HD), BF16), ((HL, BLK, BLK), BF16)]
        + [(HEAD_ROWS, BF16)] * 4
        + [(STATE, F32), (CUM, F32), (CUM, F32)],
        [7, 5], 53, 6e9, 24,
    )(cum_rows, stats, gains, queries, keys, values, d_out, attended, states, weights)


def far_grads(cum_rows, ends, far, scaled_keys, values, term, near_keys, near_values):
    return call(
        far_grads_kernel, "far_grads", [VMEM] * 5 + [HBM] * 3,
        [(HBM, WIDE), (HBM, WIDE)],
        [(STATE, F32)] + [(HEAD_PROMPT, BF16)] * 4, [3, 2], 44, 3e8, 10, {6: 0, 7: 1},
    )(cum_rows, ends, far, scaled_keys, values, term, near_keys, near_values)


def backward_scan(got, decays, after):
    return call(
        backward_scan_kernel, "backward_scan", [VMEM, VMEM, HBM],
        [(VMEM, shape(PIECES, BF16))], [], [], 12, 1e6, 1,
    )(got, decays, after)[0]


def everyone(array, axis):
    return lax.all_to_all(array, axis, 0, 0, tiled=True)


def local(queries, keys, values, log_decay, gain, parents, d_out):
    gains = gain.reshape(HL, HD)
    decay_rows = jnp.swapaxes(log_decay, 1, 2)
    send, first_term, cum_rows, block_ends = summarize(decay_rows, keys, values)
    got = everyone(send, "seq")
    within, scaled_keys, weights, done = inside(cum_rows, queries, keys, values)
    send, decays = forward_scan(parents, got, done)
    starts = everyone(send, "seq")
    near_queries, attended, stats, kept, states = attend(
        block_ends, gains, d_out, starts, first_term, within
    )
    stats = everyone(stats, "head")
    send = grads(block_ends, gains, stats, near_queries, d_out, attended)
    got = everyone(send, "seq")
    out, d_queries, d_keys, d_values, last_term, done = local_grads(
        cum_rows, stats, gains, queries, keys, values, d_out, kept, states, weights
    )
    far = everyone(backward_scan(got, decays, done), "seq")
    d_keys, d_values = far_grads(
        cum_rows, block_ends, far, scaled_keys, values, last_term, d_keys, d_values
    )
    return (out, d_queries, d_keys, d_values)


def solution(mesh):
    cut = P("seq", None, "head")
    return jax.shard_map(
        local,
        mesh=mesh,
        in_specs=(cut, cut, cut, cut, P("head"), P(), cut),
        out_specs=(cut, cut, cut, cut),
        check_vma=False,
    )
```

```python
import jax
import jax.numpy as jnp
from jax import lax
from jax.experimental import pallas as pl
from jax.experimental.pallas import tpu as pltpu
from jax.sharding import PartitionSpec as P

H = 64
HD = 128
BLK = 256
PROMPTS = 2
P_DEV = 512
ROWS = 768
HL = 8
N_SEQ = 32
SPAN = N_SEQ // PROMPTS
COLS = HL * HD
PIECE = HL * HD // N_SEQ
PARTS = HD // PIECE
PACK = 8
BLOCKS = ROWS // BLK
TILES = ROWS // HD
EPS = 1e-05
GROUP = 2

F32 = jnp.float32
BF16 = jnp.bfloat16


def dot(a, b, dims):
    return lax.dot_general(a, b, (dims, ((), ())), preferred_element_type=F32)


def mm(a, b):
    return dot(a, b, ((1,), (0,)))


def mm_nt(a, b):
    return dot(a, b, ((1,), (1,)))


def mm_tn(a, b):
    return dot(a, b, ((0,), (0,)))


def rows(number):
    return slice(number * BLK, (number + 1) * BLK)


def tile_rows(tile):
    return slice(tile * HD, (tile + 1) * HD)


def down(row):
    return jnp.broadcast_to(row, (HD, BLK)).T


def twice(block):
    return jnp.concatenate([block, block], axis=1)


def rounded_product(block, factor):
    return (block.astype(F32) * factor).astype(BF16)


def lanes(head):
    return pl.ds(pl.multiple_of(head * HD, HD), HD)


def of_rows(ref, count=ROWS, first=0):
    if len(ref.shape) == 3:
        return lambda head: ref.at[0, pl.ds(first, count), lanes(head)]
    return lambda head: ref.at[pl.ds(first, count), lanes(head)]


def of_lead(ref, count=1, first=0):
    if count == 1:
        return lambda head: ref.at[head + first]
    return lambda head: ref.at[pl.ds(head * count, count)]


class Copies:
    def __init__(self, pairs, sems):
        self.pairs, self.sems = pairs, sems

    def each(self, head):
        return [
            pltpu.make_async_copy(src(head), dst(head), self.sems.at[number, head])
            for number, (src, dst) in enumerate(self.pairs)
        ]

    def start(self, head):
        for copy in self.each(head):
            copy.start()

    def begin(self):
        for head in range(HL):
            self.start(head)

    def wait(self, head):
        for copy in self.each(head):
            copy.wait()


def over_heads(fetch, body, leave=None, started=False, group=GROUP):
    if fetch is not None and not started:
        fetch.begin()

    def step(number, carry):
        heads = [number * group + place for place in range(group)]
        for head in heads:
            if fetch is not None:
                fetch.wait(head)
        for head in heads:
            body(head)
        for head in heads:
            if leave is not None:
                leave.start(head)
        return carry

    lax.fori_loop(0, HL // group, step, 0)
    if leave is not None:
        for head in range(HL):
            leave.wait(head)


def split(value):
    coarse = value.astype(BF16)
    rest = value - coarse.astype(F32)
    middle = rest.astype(BF16)
    return coarse, middle, (rest - middle.astype(F32)).astype(BF16)


def summary_kernel(
    decay_ref, keys_ref, values_ref,
    send_ref, term_ref, cum_rows_ref, ends_ref,
    keys_buf, values_buf, decay_buf, send_buf, in_sems, out_sems, decay_sem,
):
    fetch = Copies(
        [
            (of_rows(keys_ref, P_DEV), of_lead(keys_buf)),
            (of_rows(values_ref, P_DEV), of_lead(values_buf)),
        ],
        in_sems,
    )
    leave = Copies([(of_lead(send_buf, PARTS), of_lead(send_ref, PARTS))], out_sems)
    decay_copy = pltpu.make_async_copy(decay_ref, decay_buf, decay_sem.at[0, 0])
    decay_copy.start()
    fetch.begin()
    before = lax.broadcasted_iota(jnp.int32, (BLK, BLK), 0)
    after = lax.broadcasted_iota(jnp.int32, (BLK, BLK), 1)
    upper = jnp.where(before <= after, 1.0, 0.0).astype(BF16)
    decay_copy.wait()
    stacked = jnp.concatenate(
        [decay_buf[0, :, rows(number)] for number in range(BLOCKS)], axis=0
    )
    coarse, middle, fine = (mm(part, upper) for part in split(stacked))
    cumulative = (fine + middle) + coarse
    for number in range(BLOCKS):
        total = cumulative[number * HL : (number + 1) * HL]
        cum_rows_ref[:, rows(number)] = total
        ends_ref[:, number, :] = jnp.broadcast_to(jnp.exp(total[:, BLK - 1 : BLK]), (HL, HD))
    row_ids = lax.broadcasted_iota(jnp.int32, (PACK, HD), 0)

    def body(head):
        terms = []
        for number in range(2):
            row = cum_rows_ref[pl.ds(head, 1), rows(number)]
            factor = jnp.exp(row[:, BLK - 1 : BLK] - row)
            turned = keys_buf[head, rows(number), :].T
            key_scaled = rounded_product(turned, factor)
            terms.append(mm(key_scaled, values_buf[head, rows(number), :]))
        term_ref[head] = terms[0]
        end_decays = ends_ref[head]
        summary = end_decays[1:2, :] * terms[0] + terms[1]
        decay = jnp.broadcast_to(end_decays[0:1, :] * end_decays[1:2, :], (PACK, HD))
        coarse, middle, _ = split(decay)
        packed = jnp.where(
            row_ids == 0, coarse.astype(F32), jnp.where(row_ids == 1, middle.astype(F32), 0.0)
        ).astype(BF16)
        for piece in range(PARTS):
            at = head * PARTS + piece
            send_buf[at, 0:PIECE, :] = summary[piece * PIECE : (piece + 1) * PIECE].astype(BF16)
            send_buf[at, PIECE : PIECE + PACK, :] = packed

    over_heads(fetch, body, leave, started=True, group=4)


def within_kernel(
    cum_rows_ref, queries_ref, keys_ref, values_ref,
    within_ref, scaled_keys_ref, weights_ref, done_ref,
    queries_buf, keys_buf, values_buf, within_buf, scaled_queries_buf, scaled_keys_buf,
    weights_buf, in_sems, out_sems,
):
    fetch = Copies(
        [
            (of_rows(queries_ref), of_lead(queries_buf)),
            (of_rows(keys_ref), of_lead(keys_buf)),
            (of_rows(values_ref), of_lead(values_buf)),
        ],
        in_sems,
    )
    leave = Copies(
        [
            (of_lead(within_buf), of_lead(within_ref)),
            (of_lead(scaled_queries_buf), of_lead(within_ref, first=HL)),
            (of_lead(scaled_keys_buf), of_lead(scaled_keys_ref)),
            (of_lead(weights_buf), of_lead(weights_ref)),
        ],
        out_sems,
    )
    done_ref[...] = jnp.zeros_like(done_ref)
    row_ids = lax.broadcasted_iota(jnp.int32, (BLK, BLK), 0)
    col_ids = lax.broadcasted_iota(jnp.int32, (BLK, BLK), 1)

    def body(head):
        for number in range(BLOCKS):
            part = rows(number)
            queries = queries_buf[head, part, :]
            keys = keys_buf[head, part, :]
            row = cum_rows_ref[pl.ds(head, 1), part]
            values = values_buf[head, part, :]
            if number < 2:
                gaps = twice(down(row)) - row
                mask = jnp.where(row_ids >= col_ids, jnp.exp(gaps), 0.0)
                weights = (mm_nt(queries, keys) * mask).astype(BF16)
                within = mm(weights, values)
            else:
                gaps = row - twice(down(row))
                mask = jnp.where(col_ids >= row_ids, jnp.exp(gaps), 0.0)
                weights = (mm_nt(keys, queries) * mask).astype(BF16)
                weights_buf[head] = weights
                within = mm_tn(weights, values)
            within_buf[head, part, :] = within.astype(BF16)
            scaled_queries_buf[head, part, :] = rounded_product(queries, down(jnp.exp(row)))
            if number < 2:
                factor = down(jnp.exp(row[:, BLK - 1 : BLK] - row))
                scaled_keys_buf[head, part, :] = rounded_product(keys, factor)

    over_heads(fetch, body, leave, group=4)


def forward_scan_kernel(parents_ref, got_ref, _after, send_ref, decay_ref):
    totals = []
    for prompt in range(PROMPTS):
        carry = jnp.zeros((PIECE, HD), F32)
        for index in range(prompt * SPAN, (prompt + 1) * SPAN):
            packed = got_ref[index, PIECE : PIECE + PACK, :].astype(F32)
            decay = packed[0:1, :] + packed[1:2, :]
            decay_ref[index : index + 1, :] = decay
            send_ref[index, 0:PIECE, :] = carry.astype(BF16)
            carry = decay * carry + got_ref[index, 0:PIECE, :].astype(F32)
        totals.append(carry)
    for index in range(N_SEQ):
        prompt = parents_ref[index] // SPAN
        chosen = jnp.where(prompt == 0, totals[0], totals[1])
        decay_ref[N_SEQ + index : N_SEQ + index + 1, :] = jnp.full((1, HD), prompt, F32)
        send_ref[index, PIECE : 2 * PIECE, :] = chosen.astype(BF16)


def attend_kernel(
    ends_ref, gain_ref, d_out_ref, starts_ref, term_ref, within_ref,
    queries_ref, attended_ref, stats_ref, kept_ref, states_ref,
    within_buf, states_buf, squares_ref, products_ref, in_sems, out_sems,
):
    fetch = Copies(
        [
            (of_lead(within_ref, first=HL), of_lead(queries_ref)),
            (of_lead(within_ref), of_lead(within_buf)),
        ],
        in_sems,
    )
    leave = Copies(
        [
            (of_lead(attended_ref), of_lead(kept_ref)),
            (of_lead(states_buf, BLOCKS), of_lead(states_ref, BLOCKS)),
        ],
        out_sems,
    )
    fetch.begin()
    squares_ref[...] = jnp.zeros_like(squares_ref)
    products_ref[...] = jnp.zeros_like(products_ref)

    def body(head):
        got = starts_ref[pl.ds(head * PARTS, PARTS)]
        first = got[:, 0:PIECE, :].reshape(HD, HD)
        reply = got[:, PIECE : 2 * PIECE, :].reshape(HD, HD)
        end_decay = ends_ref[head][0:1, :]
        second = (end_decay * first.astype(F32) + term_ref[head]).astype(BF16)
        gain = gain_ref[pl.ds(head, 1), :]
        for number, start in enumerate((first, second, reply)):
            part = rows(number)
            states_buf[head * BLOCKS + number] = start
            attended = within_buf[head, part, :].astype(F32) + mm(
                queries_ref[head, part, :], start
            )
            attended_ref[head, part, :] = attended.astype(BF16)
            weighted = gain * d_out_ref[0, part, lanes(head)].astype(F32)
            squares_ref[part, :] += attended * attended
            products_ref[part, :] += weighted * attended

    over_heads(fetch, body, leave, started=True)
    stats_ref[...] = jnp.zeros_like(stats_ref)
    for tile in range(TILES):
        for base, sums_ref in ((0, squares_ref), (8, products_ref)):
            row = jnp.sum(sums_ref[tile_rows(tile), :].T, axis=0, keepdims=True)
            stats_ref[:, base + tile : base + tile + 1, :] = jnp.broadcast_to(
                row[None], (HL, 1, HD)
            )


def row_factors(stats_ref, inverse_ref, slope_ref):
    total = stats_ref[0]
    for source in range(1, HL):
        total = total + stats_ref[source]
    turned = jnp.concatenate([total, jnp.zeros((HD - 16, HD), F32)], axis=0).T
    for tile in range(TILES):
        squares = turned[:, tile : tile + 1]
        products = turned[:, 8 + tile : 9 + tile]
        inverse = lax.rsqrt(squares / (H * HD) + EPS)
        slope = inverse * inverse * inverse * products / (H * HD)
        inverse_ref[tile_rows(tile), :] = jnp.broadcast_to(inverse, (HD, HD))
        slope_ref[tile_rows(tile), :] = jnp.broadcast_to(slope, (HD, HD))


def grad_kernel(
    ends_ref, gain_ref, stats_ref, queries_ref, d_out_ref, attended_ref,
    send_ref, inverse_ref, slope_ref,
):
    row_factors(stats_ref, inverse_ref, slope_ref)

    def body(head):
        gain = gain_ref[pl.ds(head, 1), :]
        terms = []
        for number in range(BLOCKS):
            part = rows(number)
            weighted = gain * d_out_ref[0, part, lanes(head)].astype(F32)
            grad = (
                inverse_ref[part, :] * weighted
                - attended_ref[head, part, :].astype(F32) * slope_ref[part, :]
            ).astype(BF16)
            terms.append(mm_tn(queries_ref[head, part, :], grad))
        local_sum = ends_ref[head][0:1, :] * terms[1] + terms[0]
        for piece in range(PARTS):
            at = head * PARTS + piece
            part = slice(piece * PIECE, (piece + 1) * PIECE)
            send_ref[at, 0:PIECE, :] = local_sum[part].astype(BF16)
            send_ref[at, PIECE : 2 * PIECE, :] = terms[2][part].astype(BF16)

    over_heads(None, body, group=HL)


def backward_scan_kernel(got_ref, decay_ref, _after, send_ref):
    branches = [jnp.zeros((PIECE, HD), F32) for _ in range(PROMPTS)]
    for index in range(N_SEQ):
        prompt = decay_ref[N_SEQ + index : N_SEQ + index + 1, :]
        start_grad = got_ref[index, PIECE : 2 * PIECE, :].astype(F32)
        for each in range(PROMPTS):
            branches[each] = branches[each] + jnp.where(prompt == each, start_grad, 0.0)
    for prompt in range(PROMPTS):
        carry = branches[prompt]
        for index in reversed(range(prompt * SPAN, (prompt + 1) * SPAN)):
            send_ref[index] = carry.astype(BF16)
            carry = decay_ref[index : index + 1, :] * carry + got_ref[index, 0:PIECE, :].astype(F32)


def local_grads_kernel(
    cum_rows_ref, stats_ref, gain_ref,
    queries_ref, keys_ref, values_ref, d_out_ref, attended_ref, states_ref, weights_ref,
    out_ref, d_queries_ref, d_keys_ref, d_values_ref, term_ref, done_ref,
    queries_buf, keys_buf, values_buf, d_out_buf, attended_buf, states_buf, weights_buf,
    out_buf, d_queries_buf, d_keys_buf, d_values_buf, term_buf,
    inverse_ref, slope_ref, in_sems, out_sems,
):
    fetch = Copies(
        [
            (of_rows(d_out_ref), of_lead(d_out_buf)),
            (of_lead(attended_ref), of_lead(attended_buf)),
            (of_rows(queries_ref), of_lead(queries_buf)),
            (of_rows(keys_ref), of_lead(keys_buf)),
            (of_rows(values_ref), of_lead(values_buf)),
            (of_lead(states_ref, BLOCKS), of_lead(states_buf, BLOCKS)),
            (of_lead(weights_ref), of_lead(weights_buf)),
        ],
        in_sems,
    )
    leave = Copies(
        [
            (of_lead(out_buf), of_rows(out_ref)),
            (of_lead(d_queries_buf), of_rows(d_queries_ref)),
            (of_lead(d_keys_buf), of_rows(d_keys_ref)),
            (of_lead(d_values_buf), of_rows(d_values_ref)),
            (of_lead(term_buf), of_lead(term_ref)),
        ],
        out_sems,
    )
    fetch.begin()
    done_ref[...] = jnp.zeros_like(done_ref)
    row_factors(stats_ref, inverse_ref, slope_ref)
    row_ids = lax.broadcasted_iota(jnp.int32, (BLK, BLK), 0)
    col_ids = lax.broadcasted_iota(jnp.int32, (BLK, BLK), 1)

    def body(head):
        gain = gain_ref[pl.ds(head, 1), :]
        for number in range(BLOCKS):
            part = rows(number)
            queries = queries_buf[head, part, :]
            keys = keys_buf[head, part, :]
            values = values_buf[head, part, :]
            attended = attended_buf[head, part, :].astype(F32)
            inverse = inverse_ref[part, :]
            weighted = gain * d_out_buf[head, part, :].astype(F32)
            grad = (inverse * weighted - attended * slope_ref[part, :]).astype(BF16)
            out_buf[head, part, :] = (attended * inverse * gain).astype(BF16)
            row = cum_rows_ref[pl.ds(head, 1), part]
            gaps = row - twice(down(row))
            mask = jnp.where(col_ids >= row_ids, jnp.exp(gaps), 0.0)
            if number < 2:
                weights = (mm_nt(keys, queries) * mask).astype(BF16)
            else:
                weights = weights_buf[head]
            score_grad = (mm_nt(values, grad) * mask).astype(BF16)
            growth = down(jnp.exp(row))
            start = states_buf[head * BLOCKS + number]
            grad_queries = mm_tn(score_grad, keys) + growth * mm_nt(grad, start)
            d_queries_buf[head, part, :] = grad_queries.astype(BF16)
            if number == 1:
                term_buf[head] = mm_tn(rounded_product(queries, growth), grad).astype(BF16)
            d_keys_buf[head, part, :] = mm(score_grad, queries).astype(BF16)
            d_values_buf[head, part, :] = mm(weights, grad).astype(BF16)

    over_heads(fetch, body, leave, started=True)


def far_grads_kernel(
    cum_rows_ref, ends_ref, far_ref, scaled_keys_ref, values_ref, term_ref,
    near_keys_ref, near_values_ref, d_keys_ref, d_values_ref,
    term_buf, near_keys_buf, near_values_buf, d_keys_buf, d_values_buf, in_sems, out_sems,
):
    fetch = Copies(
        [
            (of_lead(term_ref), of_lead(term_buf)),
            (of_rows(near_keys_ref, P_DEV), of_lead(near_keys_buf)),
            (of_rows(near_values_ref, P_DEV), of_lead(near_values_buf)),
        ],
        in_sems,
    )
    leave = Copies(
        [
            (of_lead(d_keys_buf), of_rows(d_keys_ref, P_DEV)),
            (of_lead(d_values_buf), of_rows(d_values_ref, P_DEV)),
        ],
        out_sems,
    )

    def body(head):
        second = far_ref[pl.ds(head * PARTS, PARTS)].reshape(HD, HD)
        first = (ends_ref[head][1:2, :] * second.astype(F32) + term_buf[head].astype(F32)).astype(BF16)
        for number, end_grad in enumerate((first, second)):
            part = rows(number)
            row = cum_rows_ref[pl.ds(head, 1), part]
            factor = down(jnp.exp(row[:, BLK - 1 : BLK] - row))
            grad_values = near_values_buf[head, part, :].astype(F32) + mm(
                scaled_keys_ref[head, part, :], end_grad
            )
            grad_keys = near_keys_buf[head, part, :].astype(F32) + factor * mm_nt(
                values_ref[0, part, lanes(head)], end_grad
            )
            d_values_buf[head, part, :] = grad_values.astype(BF16)
            d_keys_buf[head, part, :] = grad_keys.astype(BF16)

    over_heads(fetch, body, leave)


def shape(dims, kind):
    return jax.ShapeDtypeStruct(dims, kind)


HBM = pl.BlockSpec(memory_space=pltpu.HBM)
SMEM = pl.BlockSpec(memory_space=pltpu.SMEM)
VMEM = pl.BlockSpec(memory_space=pltpu.VMEM)
WIDE = shape((1, ROWS, COLS), BF16)
HEAD_ROWS = (HL, ROWS, HD)
HEAD_PROMPT = (HL, P_DEV, HD)
HEAD_REPLY = (HL, BLK, HD)
STATE = (HL, HD, HD)
PIECES = (N_SEQ, PIECE, HD)
TWO_PIECES = (N_SEQ, 2 * PIECE, HD)
SENT_PIECES = (N_SEQ, PIECE + PACK, HD)
CUM = (ROWS, HD)
FAR = 100


def call(kernel, name, in_specs, outs, scratch, semaphores, mib, flops, moved, aliases=None):
    return pl.pallas_call(
        kernel,
        in_specs=in_specs,
        out_specs=[spec for spec, _ in outs],
        out_shape=[made for _, made in outs],
        scratch_shapes=[pltpu.VMEM(dims, kind) for dims, kind in scratch]
        + [pltpu.SemaphoreType.DMA((count, HL)) for count in semaphores],
        input_output_aliases=aliases or {},
        compiler_params=pltpu.CompilerParams(vmem_limit_bytes=mib << 20),
        cost_estimate=pl.CostEstimate(
            flops=int(flops), bytes_accessed=int(moved) << 20, transcendentals=0
        ),
        name=name,
    )


def summarize(decay_rows, keys, values):
    return call(
        summary_kernel, "summary", [HBM, HBM, HBM],
        [
            (HBM, shape(SENT_PIECES, BF16)), (VMEM, shape(STATE, F32)),
            (VMEM, shape((HL, ROWS), F32)), (VMEM, shape((HL, 8, HD), F32)),
        ],
        [(HEAD_PROMPT, BF16), (HEAD_PROMPT, BF16), ((1, HL, ROWS), F32), (SENT_PIECES, BF16)],
        [2, 1, 1], 52, 3e8, 4,
    )(decay_rows, keys, values)


def inside(cum_rows, queries, keys, values):
    return call(
        within_kernel, "within", [VMEM] + [HBM] * 3,
        [
            (HBM, shape((FAR, ROWS, HD), BF16)), (HBM, shape(HEAD_PROMPT, BF16)),
            (HBM, shape((FAR * 3 // 2, BLK, BLK), BF16)), (VMEM, shape((8, HD), F32)),
        ],
        [(HEAD_ROWS, BF16)] * 5 + [(HEAD_PROMPT, BF16), ((HL, BLK, BLK), BF16)],
        [3, 4], 53, 4e9, 16,
    )(cum_rows, queries, keys, values)


def forward_scan(parents, got, after):
    return call(
        forward_scan_kernel, "forward_scan", [SMEM, VMEM, HBM],
        [(VMEM, shape(TWO_PIECES, BF16)), (VMEM, shape((2 * N_SEQ, HD), F32))],
        [], [], 12, 1e6, 1,
    )(parents, got, after)


def attend(ends, gains, d_out, starts, term, within):
    return call(
        attend_kernel, "attend", [VMEM] * 5 + [HBM],
        [
            (VMEM, shape(HEAD_ROWS, BF16)), (VMEM, shape(HEAD_ROWS, BF16)),
            (VMEM, shape((HL, 16, HD), F32)), (HBM, shape((FAR, ROWS, HD), BF16)),
            (HBM, shape((6 * FAR, HD, HD), BF16)),
        ],
        [(HEAD_ROWS, BF16), ((HL * BLOCKS, HD, HD), BF16), (CUM, F32), (CUM, F32)],
        [2, 2], 46, 3e8, 10,
    )(ends, gains, d_out, starts, term, within)


def grads(ends, gains, stats, scaled_queries, d_out, attended):
    return call(
        grad_kernel, "grad", [VMEM] * 6, [(VMEM, shape(TWO_PIECES, BF16))],
        [(CUM, F32), (CUM, F32)], [], 20, 3e8, 10,
    )(ends, gains, stats, scaled_queries, d_out, attended)[0]


def local_grads(
    cum_rows, stats, gains, queries, keys, values, d_out, attended, states, weights
):
    return call(
        local_grads_kernel, "local_grads", [VMEM] * 3 + [HBM] * 7,
        [
            (HBM, WIDE), (HBM, WIDE), (HBM, WIDE), (HBM, WIDE),
            (HBM, shape((8 * FAR, HD, HD), BF16)), (VMEM, shape((8, HD), F32)),
        ],
        [(HEAD_ROWS, BF16)] * 5 + [((HL * BLOCKS, HD, HD), BF16), ((HL, BLK, BLK), BF16)]
        + [(HEAD_ROWS, BF16)] * 4
        + [(STATE, BF16), (CUM, F32), (CUM, F32)],
        [7, 5], 53, 6e9, 24,
    )(cum_rows, stats, gains, queries, keys, values, d_out, attended, states, weights)


def far_grads(cum_rows, ends, far, scaled_keys, values, term, near_keys, near_values):
    return call(
        far_grads_kernel, "far_grads", [VMEM] * 5 + [HBM] * 3,
        [(HBM, WIDE), (HBM, WIDE)],
        [(STATE, BF16)] + [(HEAD_PROMPT, BF16)] * 4, [3, 2], 44, 3e8, 10, {6: 0, 7: 1},
    )(cum_rows, ends, far, scaled_keys, values, term, near_keys, near_values)


def backward_scan(got, decays, after):
    return call(
        backward_scan_kernel, "backward_scan", [VMEM, VMEM, HBM],
        [(VMEM, shape(PIECES, BF16))], [], [], 12, 1e6, 1,
    )(got, decays, after)[0]


def everyone(array, axis):
    return lax.all_to_all(array, axis, 0, 0, tiled=True)


def local(queries, keys, values, log_decay, gain, parents, d_out):
    gains = gain.reshape(HL, HD)
    decay_rows = jnp.swapaxes(log_decay, 1, 2)
    send, first_term, cum_rows, block_ends = summarize(decay_rows, keys, values)
    got = everyone(send, "seq")
    within, scaled_keys, weights, done = inside(cum_rows, queries, keys, values)
    send, decays = forward_scan(parents, got, done)
    starts = everyone(send, "seq")
    near_queries, attended, stats, kept, states = attend(
        block_ends, gains, d_out, starts, first_term, within
    )
    stats = everyone(stats, "head")
    send = grads(block_ends, gains, stats, near_queries, d_out, attended)
    got = everyone(send, "seq")
    out, d_queries, d_keys, d_values, last_term, done = local_grads(
        cum_rows, stats, gains, queries, keys, values, d_out, kept, states, weights
    )
    far = everyone(backward_scan(got, decays, done), "seq")
    d_keys, d_values = far_grads(
        cum_rows, block_ends, far, scaled_keys, values, last_term, d_keys, d_values
    )
    return (out, d_queries, d_keys, d_values)


def solution(mesh):
    cut = P("seq", None, "head")
    return jax.shard_map(
        local,
        mesh=mesh,
        in_specs=(cut, cut, cut, cut, P("head"), P(), cut),
        out_specs=(cut, cut, cut, cut),
        check_vma=False,
    )
```
